32 devices in a mesh: groups: 2 (over x), blk: 16 (over z, y, core).
Axes of the slice: x: 2, y: 2, z: 4, core: 2. Of those that a mesh axis runs over, the one named last changes fastest.
Arguments:
- embeddings: bfloat16 [32768, 1024], P(('groups', 'blk')), parts along dimension 0
- order: int32 [32768], P(('groups', 'blk')), parts along dimension 0, may hold values from 0 to 1023, as said below
- pad_counts: int32 [32], P('groups'), parts along dimension 0, may hold values from 0 to 256
Outputs:
- max_sim: float32 [32768], P(('groups', 'blk')), parts along dimension 0
The draws below stay inside these ranges and needn't reach their ends.
There are 2 independent parts, one for each index of `groups`. The reference program is written for one: setup_inputs(seed, part) draws one part's arguments, and reference() takes and returns one part's arrays. A program takes and returns all parts, laid end to end along the dimension named above; each array names one. Nothing has to cross between parts.
Inputs may be any that keep to these rules, and one draw needn't show every extreme that they name: `order`: each aligned block of 1024 entries is a permutation of 0 .. 1023.
All inputs are finite; a program needn't handle non-finite values.
Results may differ from the reference program's by a relative error of at most 0.00066.
Values may be sent and summed in bfloat16 or wider, within the bound.
No kernel may reach another device: no remote copies, remote signals or barrier semaphores. Data moves between devices by JAX's collectives and lax.ppermute only.
A program may use at most 64 MiB of HBM per device.

```python
import jax
import jax.numpy as jnp
from jax import lax

D = 1024
BR = 1024
STEPS = 6
BLOCKS = 16
ROWS = 16384


def draw_embeddings(key, part):
    key = jax.random.fold_in(key, 11)
    key_base, key_shift, key_weight = jax.random.split(key, 3)
    base = jax.random.normal(key_base, (ROWS, D), jnp.float32)
    shift = jax.random.randint(key_shift, (ROWS,), 1, STEPS * BR + 1)
    partner = (jnp.arange(ROWS, dtype=jnp.int32) + shift) % ROWS
    weight = jax.random.uniform(key_weight, (ROWS, 1), jnp.float32, 0.0, 2.0)
    return (base + weight * base[partner]).astype(jnp.bfloat16)


def draw_order(key, part):
    key = jax.random.fold_in(key, 23)
    keys = jax.random.split(key, ROWS // BR)
    perms = jax.vmap(lambda single: jax.random.permutation(single, BR))(keys)
    return perms.reshape(-1).astype(jnp.int32)


def with_ends(drawn, rng, least, high):
    shape = drawn.shape
    place = [jax.random.randint(jax.random.fold_in(rng, axis), (), 0, shape[axis]) for axis in range(len(shape))]
    drawn = drawn.at[tuple(place)].set(least)
    longest = shape.index(max(shape))
    place[longest] = (place[longest] + 1) % shape[longest]
    return drawn.at[tuple(place)].set(high)


def setup_inputs(seed: int = 0, part: int = 0) -> dict:
    key_of = jax.random.split(jax.random.key(seed), 4)
    part_splits = jax.random.split(jax.random.fold_in(key_of[3], part), 4)
    return {
        "embeddings": draw_embeddings(jax.random.fold_in(jax.random.fold_in(key_of[3], part), 71), part),
        "order": draw_order(jax.random.fold_in(jax.random.fold_in(key_of[3], part), 71), part),
        "pad_counts": with_ends(jax.random.randint(part_splits[2], (BLOCKS,), 0, BR // 4 + 1), jax.random.fold_in(part_splits[2], 1), 0, (BR // 4 + 1) - 1).astype(jnp.int32),
    }


def reference(embeddings, order, pad_counts):
    blocks = ROWS // BR
    starts = jnp.arange(blocks, dtype=jnp.int32) * BR
    rows_at = (order.reshape(blocks, BR) + starts[:, None]).reshape(-1)
    ordered = embeddings[rows_at].astype(jnp.float32)
    unit = (ordered * lax.rsqrt(lax.optimization_barrier(jnp.sum(ordered * ordered, axis=1, keepdims=True)) + 1e-06)).astype(jnp.bfloat16)
    unit = unit.reshape(blocks, BR, D).astype(jnp.float32)
    valid = jnp.arange(BR, dtype=jnp.int32)[None, :] < (BR - pad_counts)[:, None]
    rowbest = jnp.full((blocks, BR), -2.0, jnp.float32)
    colbest = jnp.full((blocks, BR), -2.0, jnp.float32)
    distinct = jnp.arange(BR)[:, None] != jnp.arange(BR)[None, :]
    for offset in range(STEPS + 1):
        other = jnp.roll(unit, -offset, axis=0)
        other_valid = jnp.roll(valid, -offset, axis=0)
        scores = jnp.einsum('bid,bjd->bij', unit, other)
        keep = valid[:, :, None] & other_valid[:, None, :]
        if offset == 0:
            keep = keep & distinct[None, :, :]
        scores = jnp.where(keep, scores, jnp.float32(-2.0))
        rowbest = jnp.maximum(rowbest, lax.optimization_barrier(jnp.max(scores, axis=2)))
        colbest = jnp.maximum(colbest, jnp.roll(lax.optimization_barrier(jnp.max(scores, axis=1)), offset, axis=0))
    best = jnp.where(valid, jnp.maximum(rowbest, colbest), jnp.float32(0.0))
    return best.reshape(-1)
```

```python
import functools

import jax
import jax.numpy as jnp
from jax import lax
from jax.experimental import pallas as pl
from jax.experimental.pallas import tpu as pltpu
from jax.sharding import PartitionSpec as P

STEPS = 6
CHUNKS = 4
VMEM = 48 * 2**20


def unit_kernel(first_row, pads, order_smem, order, embeddings, everything, unit, tile, sem):
    rows = order.shape[1]
    count = unit.shape[0]
    valid_count = rows - pads[lax.axis_index("blk")]
    first = order_smem[0]
    base = pl.multiple_of((first // 16) * 16, 16)
    copy = pltpu.make_async_copy(everything.at[pl.ds(base, 16)], tile, sem)
    copy.start()
    position = lax.broadcasted_iota(jnp.int32, (1, rows), 1)
    kept = jnp.where(position < valid_count, order[...], -1)
    row = first_row + lax.broadcasted_iota(jnp.int32, (count, 1), 0)
    valid = jnp.max(jnp.where(kept == row, 1.0, 0.0), axis=1, keepdims=True) > 0.0
    copy.wait()
    among = lax.broadcasted_iota(jnp.int32, (16, 1), 0) == first - base
    filler = jnp.sum(jnp.where(among, tile[...].astype(jnp.float32), 0.0), axis=0, keepdims=True)
    value = jnp.where(valid, embeddings[...].astype(jnp.float32), filler)
    scale = lax.rsqrt(jnp.sum(value * value, axis=1, keepdims=True) + 1e-06)
    unit[...] = (value * scale).astype(jnp.bfloat16)


def unit_chunk(embeddings, order, pad_counts, chunk):
    rows, depth = embeddings.shape
    count = rows // CHUNKS
    return pl.pallas_call(
        functools.partial(unit_kernel, chunk * count),
        out_shape=jax.ShapeDtypeStruct((count, depth), jnp.bfloat16),
        grid=(1,),
        in_specs=[
            pl.BlockSpec(memory_space=pltpu.SMEM),
            pl.BlockSpec(memory_space=pltpu.SMEM),
            pl.BlockSpec((1, rows), lambda i: (0, 0)),
            pl.BlockSpec((count, depth), lambda i: (chunk, 0)),
            pl.BlockSpec(memory_space=pl.ANY),
        ],
        out_specs=pl.BlockSpec((count, depth), lambda i: (0, 0)),
        scratch_shapes=[pltpu.VMEM((16, depth), jnp.bfloat16), pltpu.SemaphoreType.DMA],
        compiler_params=pltpu.CompilerParams(vmem_limit_bytes=VMEM),
        cost_estimate=pl.CostEstimate(
            flops=4 * count * depth, bytes_accessed=4 * count * depth, transcendentals=count
        ),
        name="unit_chunk",
    )(pad_counts, order, order.reshape(1, rows), embeddings, embeddings)


def folded(scores):
    return jnp.max(scores.reshape(-1, 8, scores.shape[1]), axis=0)


def own_kernel(pads, order, *refs):
    units, own, best = refs[:-2], refs[-2], refs[-1]
    rows = order.shape[1]
    count = units[0].shape[0]
    valid_count = rows - pads[lax.axis_index("blk")]
    position = lax.broadcasted_iota(jnp.int32, (1, rows), 1)
    kept = jnp.where(position < valid_count, order[...], -1)
    total = None
    for index, unit in enumerate(units):
        row = index * count + lax.broadcasted_iota(jnp.int32, (count, 1), 0)
        placed = (order[...] == row).astype(jnp.bfloat16)
        part = lax.dot_general(
            unit[...], placed, (((0,), (0,)), ((), ())), preferred_element_type=jnp.float32
        )
        if index == 0:
            total = part
        else:
            total = total + part
    own[...] = total.astype(jnp.bfloat16)
    running = jnp.full((8, rows), -2.0, jnp.float32)
    for index, unit in enumerate(units):
        row = index * count + lax.broadcasted_iota(jnp.int32, (count, 1), 0)
        valid = jnp.max(jnp.where(kept == row, 1.0, 0.0), axis=1, keepdims=True) > 0.0
        scores = jnp.dot(unit[...], own[...], preferred_element_type=jnp.float32)
        scores = jnp.where(valid & (order[...] != row), scores, -2.0)
        running = jnp.maximum(running, folded(scores))
    best[...] = running


def own_block(units, order, pad_counts):
    count, depth = units[0].shape
    rows = order.shape[0]
    whole = pl.BlockSpec(memory_space=pltpu.VMEM)
    return pl.pallas_call(
        own_kernel,
        out_shape=(
            jax.ShapeDtypeStruct((depth, rows), jnp.bfloat16),
            jax.ShapeDtypeStruct((8, rows), jnp.float32),
        ),
        in_specs=[pl.BlockSpec(memory_space=pltpu.SMEM), whole] + [whole] * len(units),
        out_specs=(whole, whole),
        compiler_params=pltpu.CompilerParams(vmem_limit_bytes=VMEM),
        cost_estimate=pl.CostEstimate(
            flops=4 * rows * rows * depth, bytes_accessed=4 * rows * depth, transcendentals=0
        ),
        name="own_block",
    )(pad_counts, order.reshape(1, rows), *units)


def tile_kernel(last, table, pads, own, best, blocks, out, running):
    step = pl.program_id(0)
    rows = own.shape[1]

    @pl.when(step == 0)
    def _():
        running[...] = best[...]

    for column in range(0, rows, 256):
        part = pl.ds(column, 256)
        scores = jnp.dot(blocks[0], own[:, part], preferred_element_type=jnp.float32)
        running[:, part] = jnp.maximum(running[:, part], folded(scores))

    @pl.when(step == pl.num_programs(0) - 1)
    def _():
        if last:
            valid_count = rows - pads[lax.axis_index("blk")]
            position = lax.broadcasted_iota(jnp.int32, (1, rows), 1)
            found = jnp.max(running[...], axis=0, keepdims=True)
            out[...] = jnp.where(position < valid_count, found, 0.0)
        else:
            out[...] = running[...]


def scored(table, pad_counts, own, best, blocks, last):
    depth, rows = own.shape
    count = blocks.shape[1]
    steps = table.shape[0]
    out_rows = 1 if last else 8
    return pl.pallas_call(
        functools.partial(tile_kernel, last),
        out_shape=jax.ShapeDtypeStruct((out_rows, rows), jnp.float32),
        grid_spec=pltpu.PrefetchScalarGridSpec(
            num_scalar_prefetch=2,
            grid=(steps,),
            in_specs=[
                pl.BlockSpec((depth, rows), lambda i, table, pads: (0, 0)),
                pl.BlockSpec((8, rows), lambda i, table, pads: (0, 0)),
                pl.BlockSpec((1, count, depth), lambda i, table, pads: (table[i], 0, 0)),
            ],
            out_specs=pl.BlockSpec((out_rows, rows), lambda i, table, pads: (0, 0)),
            scratch_shapes=[pltpu.VMEM((8, rows), jnp.float32)],
        ),
        compiler_params=pltpu.CompilerParams(vmem_limit_bytes=VMEM),
        cost_estimate=pl.CostEstimate(
            flops=2 * steps * count * rows * depth,
            bytes_accessed=2 * (steps * count + rows) * depth,
            transcendentals=0,
        ),
        name="scored",
    )(table, pad_counts, own, best, blocks)


def local(embeddings, order, pad_counts):
    rows, depth = embeddings.shape
    count = rows // CHUNKS
    nblocks = lax.axis_size("blk")
    here = lax.axis_index("blk")
    offsets = [k for step in range(1, STEPS + 1) for k in (step, -step)]
    units = [unit_chunk(embeddings, order, pad_counts, chunk) for chunk in range(CHUNKS)]
    if nblocks <= 16:
        arrived = [lax.all_gather(unit, "blk") for unit in units]
        table = (here + jnp.array(offsets, jnp.int32)) % nblocks
        rounds = [(table, blocks) for blocks in arrived]
    else:
        own_unit = jnp.concatenate(units)[None]
        rounds = []
        for offset in offsets:
            pairs = [(i, (i + offset) % nblocks) for i in range(nblocks)]
            rounds.append((jnp.zeros((1,), jnp.int32), lax.ppermute(own_unit, "blk", pairs)))
    own, best = own_block(units, order, pad_counts)
    for index, (table, blocks) in enumerate(rounds):
        best = scored(table, pad_counts, own, best, blocks, index == len(rounds) - 1)
    return best.reshape(rows)


def solution(mesh):
    in_specs = (P(("groups", "blk"), None), P(("groups", "blk")), P("groups"))
    out_specs = P(("groups", "blk"))
    return jax.shard_map(local, mesh=mesh, in_specs=in_specs, out_specs=out_specs, check_vma=False)
```

```python
import functools

import jax
import jax.numpy as jnp
import numpy as np
from jax import lax
from jax.experimental import pallas as pl
from jax.experimental.pallas import tpu as pltpu
from jax.sharding import PartitionSpec as P

STEPS = 6
VMEM = 56 * 2**20
FLOOR = -2.0


class Move:
    def __init__(self, name, source, pairs, stage, after=()):
        self.name, self.source, self.pairs = name, source, pairs
        self.stage, self.after = stage, after


def near(first, second, count):
    gap = (first - second) % count
    return min(gap, count - gap) <= STEPS


def grid_moves():
    def at(z, y, lane):
        return 4 * z + 2 * y + (y if lane == 0 else 1 - y)

    def rows(links):
        return [
            (at(z, y, lane), at(to, y, land)) for y in (0, 1) for (z, lane), (to, land) in links
        ]

    def across(planes, lane):
        return [(at(z, y, lane), at(z, 1 - y, lane)) for z in planes for y in (0, 1)]

    every = range(4)
    return [
        Move("R1", "own", rows([((0, 0), (2, 0)), ((2, 0), (3, 0)), ((3, 0), (1, 0)), ((1, 0), (0, 0))])
             + across(every, 1), 1),
        Move("R2a", "own", rows([((3, 1), (1, 1)), ((1, 1), (0, 1)), ((1, 0), (2, 0))]), 1),
        Move("R2b", "own", rows([((0, 1), (1, 1))]) + across(every, 0), 1),
        Move("A", "own", rows([((z, lane), (z, 1 - lane)) for z in every for lane in (0, 1)]), 0),
        Move("H", "R2b", across([1], 1), 3),
        Move("G", "R1", rows([((2, 0), (3, 0))]), 3),
        Move("R3", "own", rows([((1, 1), (2, 1)), ((2, 1), (3, 1)), ((2, 0), (1, 1))]), 3, ("R1",)),
        Move("FI", "R2b", rows([((z, 0), (z, 1)) for z in every] + [((1, 1), (1, 0))]), 2),
        Move("FK", "R1", rows([((z, 1), (z, 0)) for z in every] + [((1, 0), (1, 1))]), 2),
    ]


def ring_moves(count):
    return [
        Move("N%d" % k, "own", [((i + k) % count, i) for i in range(count)], k)
        for k in range(1, STEPS + 1)
    ]


def planned(count):
    moves = grid_moves() if count == 16 else ring_moves(count)
    holds = {"own": {d: d for d in range(count)}}
    stage_of = {"own": 0}
    for move in moves:
        holds[move.name] = {to: holds[move.source][of] for of, to in move.pairs if of in holds[move.source]}
        stage_of[move.name] = move.stage
    slots = ["own"] + [move.name for move in moves]
    stages = 1 + max(stage_of.values())
    where = {}
    for device in range(count):
        held = [(slot, holds[slot][device]) for slot in slots if device in holds[slot]]
        for i, (slot, block) in enumerate(held):
            for other, visitor in held[:i]:
                if block != visitor and near(block, visitor, count):
                    pair = (min(block, visitor), max(block, visitor))
                    stage = max(stage_of[slot], stage_of[other])
                    where.setdefault(pair, []).append((stage, device, slot, other, block, visitor))
    need = [(b, (b + k) % count) for b in range(count) for k in range(1, STEPS + 1)]
    need = sorted({(min(pair), max(pair)) for pair in need})
    load = np.zeros((stages, count), np.int64)
    work = [[[] for _ in range(count)] for _ in range(stages)]
    for pair in sorted(need, key=lambda p: (len({w[1] for w in where[p]}), p)):
        choice = min(
            where[pair],
            key=lambda w: (w[0], load[w[0], w[1]], load[:, w[1]].sum(), w[1]),
        )
        stage, device = choice[:2]
        load[stage, device] += 1
        work[stage][device].append(choice[2:])
    return moves, slots, work


def unit_kernel(pads, order_smem, order, embeddings, everything, unit, mask, tile, sem):
    rows = order.shape[1]
    count = unit.shape[0]
    valid_count = rows - pads[lax.axis_index("blk")]
    first = order_smem[0]
    base = pl.multiple_of((first // 16) * 16, 16)

    @pl.when(pl.program_id(0) == 0)
    def _():
        copy = pltpu.make_async_copy(everything.at[pl.ds(base, 16)], tile, sem)
        copy.start()
        copy.wait()

    position = lax.broadcasted_iota(jnp.int32, (1, rows), 1)
    kept = jnp.where(position < valid_count, order[...], -1)
    row = pl.program_id(0) * count + lax.broadcasted_iota(jnp.int32, (count, 1), 0)
    found = jnp.max(jnp.where(kept == row, 1.0, 0.0), axis=1, keepdims=True)
    among = lax.broadcasted_iota(jnp.int32, (16, 1), 0) == first - base
    filler = jnp.sum(jnp.where(among, tile[...].astype(jnp.float32), 0.0), axis=0, keepdims=True)
    value = jnp.where(found > 0.0, embeddings[...].astype(jnp.float32), filler)
    scale = lax.rsqrt(jnp.sum(value * value, axis=1, keepdims=True) + 1e-06)
    unit[...] = (value * scale).astype(jnp.bfloat16)
    mask[...] = jnp.broadcast_to(found, mask.shape)


def normalized(embeddings, order, pad_counts):
    rows, depth = embeddings.shape
    count = 256
    return pl.pallas_call(
        unit_kernel,
        out_shape=(
            jax.ShapeDtypeStruct((rows, depth), jnp.bfloat16),
            jax.ShapeDtypeStruct((rows, 128), jnp.float32),
        ),
        grid=(rows // count,),
        in_specs=[
            pl.BlockSpec(memory_space=pltpu.SMEM),
            pl.BlockSpec(memory_space=pltpu.SMEM),
            pl.BlockSpec((1, rows), lambda i: (0, 0)),
            pl.BlockSpec((count, depth), lambda i: (i, 0)),
            pl.BlockSpec(memory_space=pl.ANY),
        ],
        out_specs=(
            pl.BlockSpec((count, depth), lambda i: (i, 0)),
            pl.BlockSpec((count, 128), lambda i: (i, 0)),
        ),
        scratch_shapes=[pltpu.VMEM((16, depth), jnp.bfloat16), pltpu.SemaphoreType.DMA],
        compiler_params=pltpu.CompilerParams(vmem_limit_bytes=VMEM),
        cost_estimate=pl.CostEstimate(
            flops=4 * rows * depth, bytes_accessed=4 * rows * depth, transcendentals=rows
        ),
        name="normalized",
    )(pad_counts, order, order.reshape(1, rows), embeddings, embeddings)


def product(left, right):
    return lax.dot_general(left, right, (((1,), (1,)), ((), ())), preferred_element_type=jnp.float32)


def own_kernel(unit, mask, best):
    rows = unit.shape[0]
    best[...] = jnp.full(best.shape, FLOOR, jnp.float32)
    total = None
    for start in range(0, rows, 256):
        scores = product(unit[pl.ds(start, 256), :], unit[...])
        row = start + lax.broadcasted_iota(jnp.int32, (256, 1), 0)
        column = lax.broadcasted_iota(jnp.int32, (1, rows), 1)
        keep = (mask[pl.ds(start, 256), :1] > 0.0) & (row != column)
        found = jnp.max(jnp.where(keep, scores, FLOOR), axis=0, keepdims=True)
        total = found if total is None else jnp.maximum(total, found)
    best[pl.ds(lax.axis_index("blk"), 1), :] = total


def own_block(unit, mask, nblocks):
    rows, depth = unit.shape
    return pl.pallas_call(
        own_kernel,
        out_shape=jax.ShapeDtypeStruct((nblocks, rows), jnp.float32),
        in_specs=[pl.BlockSpec(memory_space=pltpu.VMEM)] * 2,
        out_specs=pl.BlockSpec(memory_space=pltpu.VMEM),
        compiler_params=pltpu.CompilerParams(vmem_limit_bytes=VMEM),
        cost_estimate=pl.CostEstimate(
            flops=2 * rows * rows * depth, bytes_accessed=2 * rows * depth, transcendentals=0
        ),
        name="own_block",
    )(unit, mask)


def pairs_kernel(nslots, table, best, *refs):
    slots, out, held, sems = refs[:nslots], refs[nslots], refs[nslots + 1], refs[nslots + 2]
    rows = out.shape[1]
    here = lax.axis_index("blk")
    steps = table[here, 0, 0]
    out[...] = best[...]

    def fetch(step):
        for side in range(2):
            wanted = table[here, step + 1, side]
            for index, slot in enumerate(slots):
                @pl.when(wanted == index)
                def _(slot=slot, side=side):
                    pltpu.make_async_copy(slot, held.at[step % 2, side], sems.at[step % 2, side]).start()

    def arrived(step):
        for side in range(2):
            pltpu.make_async_copy(slots[0], held.at[step % 2, side], sems.at[step % 2, side]).wait()

    @pl.when(steps > 0)
    def _():
        fetch(0)

    @pl.loop(0, steps)
    def _(step):
        arrived(step)

        @pl.when(step + 1 < steps)
        def _():
            fetch(step + 1)

        now = step % 2
        total = None
        first = pl.ds(table[here, step + 1, 2], 1)
        second = pl.ds(table[here, step + 1, 3], 1)
        for start in range(0, rows, 256):
            scores = product(held[now, 0, pl.ds(start, 256), :], held[now, 1])
            down = jnp.max(scores.reshape(32, 8, rows), axis=0)
            total = down if total is None else jnp.maximum(total, down)
            along = scores[:, :128]
            for lane in range(128, rows, 128):
                along = jnp.maximum(along, scores[:, lane : lane + 128])
            found = jnp.max(along.T, axis=0, keepdims=True)
            part = pl.ds(start, 256)
            out[first, part] = jnp.maximum(out[first, part], found)
        out[second, :] = jnp.maximum(out[second, :], jnp.max(total, axis=0, keepdims=True))


def scored(best, slots, work):
    names = sorted({slot for pairs in work for pair in pairs for slot in pair[:2]})
    most = max(len(pairs) for pairs in work)
    table = np.zeros((len(work), most + 1, 4), np.int32)
    for device, pairs in enumerate(work):
        table[device, 0, 0] = len(pairs)
        for step, (slot, other, block, visitor) in enumerate(pairs):
            table[device, step + 1] = (names.index(slot), names.index(other), block, visitor)
    given = [slots[name] for name in names]
    rows, depth = given[0].shape
    return pl.pallas_call(
        functools.partial(pairs_kernel, len(given)),
        out_shape=jax.ShapeDtypeStruct(best.shape, jnp.float32),
        in_specs=[pl.BlockSpec(memory_space=pltpu.SMEM), pl.BlockSpec(memory_space=pltpu.VMEM)]
        + [pl.BlockSpec(memory_space=pl.ANY)] * len(given),
        out_specs=pl.BlockSpec(memory_space=pltpu.VMEM),
        scratch_shapes=[
            pltpu.VMEM((2, 2, rows, depth), jnp.bfloat16),
            pltpu.SemaphoreType.DMA((2, 2)),
        ],
        compiler_params=pltpu.CompilerParams(vmem_limit_bytes=VMEM),
        cost_estimate=pl.CostEstimate(
            flops=2 * most * rows * rows * depth,
            bytes_accessed=4 * most * rows * depth,
            transcendentals=0,
        ),
        name="scored",
    )(jnp.asarray(table), best, *given)


def placed_kernel(pads, order, found, out):
    rows = order.shape[1]
    valid_count = rows - pads[lax.axis_index("blk")]
    best = jnp.max(found[...], axis=0, keepdims=True)
    column = jnp.broadcast_to(best, (128, rows)).T[:, :1]
    row = lax.broadcasted_iota(jnp.int32, (rows, 1), 0)
    sorted_best = jnp.max(jnp.where(order[...] == row, column, FLOOR), axis=0, keepdims=True)
    position = lax.broadcasted_iota(jnp.int32, (1, rows), 1)
    out[...] = jnp.where(position < valid_count, sorted_best, 0.0)


def placed(found, order, pad_counts):
    rows = order.shape[0]
    whole = pl.BlockSpec(memory_space=pltpu.VMEM)
    return pl.pallas_call(
        placed_kernel,
        out_shape=jax.ShapeDtypeStruct((1, rows), jnp.float32),
        in_specs=[pl.BlockSpec(memory_space=pltpu.SMEM), whole, whole],
        out_specs=whole,
        compiler_params=pltpu.CompilerParams(vmem_limit_bytes=VMEM),
        name="placed",
    )(pad_counts, order.reshape(1, rows), found).reshape(rows)


def local(embeddings, order, pad_counts):
    nblocks = lax.axis_size("blk")
    moves, names, work = planned(nblocks)
    unit, mask = normalized(embeddings, order, pad_counts)
    slots = {"own": unit}
    for move in moves:
        value = slots[move.source]
        if move.after:
            value = lax.optimization_barrier((value, *[slots[name] for name in move.after]))[0]
        slots[move.name] = lax.ppermute(value, "blk", move.pairs)
    best = own_block(unit, mask, nblocks)
    for pairs in work:
        if any(pairs):
            best = scored(best, slots, pairs)
    return placed(lax.all_to_all(best, "blk", 0, 0, tiled=True), order, pad_counts)


def solution(mesh):
    in_specs = (P(("groups", "blk"), None), P(("groups", "blk")), P("groups"))
    out_specs = P(("groups", "blk"))
    return jax.shard_map(local, mesh=mesh, in_specs=in_specs, out_specs=out_specs, check_vma=False)
```

```python
import functools

import jax
import jax.numpy as jnp
import numpy as np
from jax import lax
from jax.experimental import pallas as pl
from jax.experimental.pallas import tpu as pltpu
from jax.sharding import PartitionSpec as P

STEPS = 6
VMEM = 56 * 2**20
FLOOR = -2.0


class Move:
    def __init__(self, name, source, pairs, stage):
        self.name, self.source, self.pairs, self.stage = name, source, pairs, stage


def grid_moves():
    def at(z, y, lane):
        return 4 * z + 2 * y + (y if lane == 0 else 1 - y)

    def rows(links):
        return [
            (at(z, y, lane), at(to, y, land)) for y in (0, 1) for (z, lane), (to, land) in links
        ]

    def across(planes):
        return [(at(z, y, lane), at(z, 1 - y, lane)) for z, lane in planes for y in (0, 1)]

    every = [(z, lane) for z in range(4) for lane in range(2)]
    cores = rows([((z, lane), (z, 1 - lane)) for z, lane in every])
    first = [((0, 0), (2, 0)), ((2, 0), (3, 0)), ((3, 0), (1, 0)), ((1, 0), (0, 0)), ((0, 1), (1, 1))]
    second = [((3, 1), (1, 1)), ((1, 1), (0, 1)), ((2, 1), (3, 1)), ((1, 0), (2, 0))]
    return [
        Move("R1", "own", rows(first), 1),
        Move("R2", "own", rows(second), 1),
        Move("Y", "own", across(every), 1),
        Move("A", "own", cores, 0),
        Move("V", "R1", rows([((2, 0), (3, 0))]) + across([(1, 1)]), 3),
        Move("R3", "late", rows([((1, 1), (2, 1)), ((2, 0), (1, 1))]), 3),
        Move("F", "Y", cores, 2),
        Move("W", "R1", rows([((1, 0), (1, 1)), ((1, 1), (1, 0))]), 2),
    ]


GRID_PAIRS = (
    ((0, 2), (0, 4), (1, 4), (2, 4), (3, 4)),
    ((0, 1), (0, 3), (0, 5), (3, 5)),
    ((0, 6), (1, 2), (1, 6), (3, 6)),
    ((1, 3), (1, 7), (2, 3), (3, 7)),
    ((1, 12), (4, 5), (4, 7), (5, 7), (6, 12), (7, 12)),
    ((1, 5), (1, 13), (2, 5), (2, 8), (2, 12), (2, 13), (5, 6), (6, 7), (7, 13)),
    ((1, 11), (1, 14), (1, 15), (2, 6), (2, 14), (4, 14), (5, 15), (11, 14)),
    ((2, 7), (2, 15), (4, 6), (4, 15)),
    ((0, 10), (0, 11), (4, 8), (4, 9), (4, 10)),
    ((5, 8), (5, 9), (5, 10), (5, 11), (8, 10), (8, 11), (9, 10)),
    ((6, 8), (6, 9), (6, 10), (6, 11), (8, 9), (9, 11)),
    ((3, 8), (3, 9), (7, 8), (7, 9), (7, 10), (7, 11), (10, 11)),
    ((0, 12), (0, 13), (0, 14), (0, 15), (8, 12), (8, 13), (8, 14), (12, 13), (13, 14)),
    ((9, 12), (9, 13), (9, 14), (9, 15), (12, 14)),
    ((10, 12), (10, 13), (10, 14), (10, 15), (12, 15), (14, 15)),
    ((3, 13), (3, 14), (3, 15), (11, 12), (11, 13), (11, 15), (13, 15)),
)


def ring_moves(count):
    return [
        Move("N%d" % k, "own", [((i + k) % count, i) for i in range(count)], k)
        for k in range(1, STEPS + 1)
    ]


def planned(count):
    if count == 16:
        moves, placed_pairs, sending = grid_moves(), GRID_PAIRS, (2, 3)
    else:
        moves, sending = ring_moves(count), (STEPS,)
        placed_pairs = [[(b, (b + k) % count) for k in range(1, STEPS + 1)] for b in range(count)]
    holds = {"own": {d: d for d in range(count)}}
    holds["late"] = holds["own"]
    stage_of = {"own": 0}
    for move in moves:
        holds[move.name] = {to: holds[move.source][of] for of, to in move.pairs}
        stage_of[move.name] = move.stage
    stages = 1 + max(stage_of.values())
    work = [[[] for _ in range(count)] for _ in range(stages)]
    for device, pairs in enumerate(placed_pairs):
        slot_of = {}
        for slot in sorted(stage_of, key=stage_of.get):
            if device in holds[slot]:
                slot_of.setdefault(holds[slot][device], slot)
        for block, visitor in pairs:
            slot, other = slot_of[block], slot_of[visitor]
            stage = max(stage_of[slot], stage_of[other])
            work[stage][device].append((slot, other, block, visitor))
    scored_pairs = sorted(tuple(sorted(pair)) for pairs in placed_pairs for pair in pairs)
    needed = {tuple(sorted((b, (b + k) % count))) for b in range(count) for k in range(1, STEPS + 1)}
    assert scored_pairs == sorted(needed)
    return moves, work, sending


def colored(edges, count):
    sends, takes = [{} for _ in range(count)], [{} for _ in range(count)]
    for of, to in edges:
        a = next(c for c in range(len(edges)) if c not in sends[of])
        b = next(c for c in range(len(edges)) if c not in takes[to])
        path, node, tables, colour = [], to, (takes, sends), a
        while a != b and colour in tables[0][node]:
            end = tables[0][node][colour]
            path.append(((end, node) if tables[0] is takes else (node, end), colour))
            node, tables, colour = end, tables[::-1], a + b - colour
        for (first, second), colour in path:
            del sends[first][colour], takes[second][colour]
        for (first, second), colour in path:
            sends[first][a + b - colour], takes[second][a + b - colour] = second, first
        sends[of][a], takes[to][a] = to, of
    return [
        [(of, to[c]) for of, to in enumerate(sends) if c in to]
        for c in range(max((c + 1 for to in sends for c in to), default=0))
    ]


def unit_kernel(order_smem, pads, order, embeddings, tile, unit):
    count = unit.shape[0]
    found = valid_rows(pads, order, pl.program_id(0) * count, count)
    among = lax.broadcasted_iota(jnp.int32, (16, 1), 0) == lax.rem(order_smem[0], 16)
    filler = jnp.sum(jnp.where(among, tile[...].astype(jnp.float32), 0.0), axis=0, keepdims=True)
    value = jnp.where(found, embeddings[...].astype(jnp.float32), filler)
    scale = lax.rsqrt(jnp.sum(value * value, axis=1, keepdims=True) + 1e-06)
    unit[...] = (value * scale).astype(jnp.bfloat16)


def valid_rows(pads, order, start, count):
    rows = order.shape[1]
    valid_count = rows - pads[lax.axis_index("blk")]
    position = lax.broadcasted_iota(jnp.int32, (1, rows), 1)
    kept = jnp.where(position < valid_count, order[...], -1)
    row = start + lax.broadcasted_iota(jnp.int32, (count, 1), 0)
    return jnp.max(jnp.where(kept == row, 1.0, 0.0), axis=1, keepdims=True) > 0.0


def normalized(embeddings, order, pad_counts):
    rows, depth = embeddings.shape
    count = 256
    return pl.pallas_call(
        unit_kernel,
        out_shape=jax.ShapeDtypeStruct((rows, depth), jnp.bfloat16),
        grid_spec=pltpu.PrefetchScalarGridSpec(
            num_scalar_prefetch=2,
            grid=(rows // count,),
            in_specs=[
                pl.BlockSpec((1, rows), lambda i, order, pads: (0, 0)),
                pl.BlockSpec((count, depth), lambda i, order, pads: (i, 0)),
                pl.BlockSpec((16, depth), lambda i, order, pads: (order[0] // 16, 0)),
            ],
            out_specs=pl.BlockSpec((count, depth), lambda i, order, pads: (i, 0)),
        ),
        compiler_params=pltpu.CompilerParams(vmem_limit_bytes=VMEM),
        cost_estimate=pl.CostEstimate(
            flops=4 * rows * depth, bytes_accessed=4 * rows * depth, transcendentals=rows
        ),
        name="normalized",
    )(order, pad_counts, order.reshape(1, rows), embeddings, embeddings)


def product(left, right):
    return lax.dot_general(left, right, (((1,), (1,)), ((), ())), preferred_element_type=jnp.float32)


def own_kernel(pads, order, unit, best):
    rows = unit.shape[0]
    best[...] = jnp.full(best.shape, FLOOR, jnp.float32)
    valid = valid_rows(pads, order, 0, rows)
    row = lax.broadcasted_iota(jnp.int32, (rows, 1), 0)
    here = pl.ds(lax.axis_index("blk"), 1)
    for start in range(0, rows, 256):
        part = pl.ds(start, 256)
        scores = product(unit[...], unit[part, :])
        column = start + lax.broadcasted_iota(jnp.int32, (1, 256), 1)
        scores = jnp.where(valid & (row != column), scores, FLOOR)
        best[here, part] = jnp.max(scores, axis=0, keepdims=True)


def own_block(unit, order, pad_counts, nblocks):
    rows, depth = unit.shape
    whole = pl.BlockSpec(memory_space=pltpu.VMEM)
    return pl.pallas_call(
        own_kernel,
        out_shape=jax.ShapeDtypeStruct((nblocks, rows), jnp.float32),
        in_specs=[pl.BlockSpec(memory_space=pltpu.SMEM), whole, whole],
        out_specs=whole,
        compiler_params=pltpu.CompilerParams(vmem_limit_bytes=VMEM),
        cost_estimate=pl.CostEstimate(
            flops=2 * rows * rows * depth, bytes_accessed=2 * rows * depth, transcendentals=0
        ),
        name="own_block",
    )(pad_counts, order.reshape(1, rows), unit)


def pairs_kernel(nslots, nsends, most, table, best, *refs):
    slots, out, sent = refs[:nslots], refs[nslots], refs[nslots + 1 : nslots + 1 + nsends]
    held, across, sems = refs[nslots + 1 + nsends :]
    rows = out.shape[1]
    at = lax.axis_index("blk") * (1 + nsends + 4 * most)
    steps = table[at]
    out[...] = best[...]

    def entry(step, which):
        return table[at + 1 + nsends + 4 * step + which]

    def fetch(step):
        for side in range(2):
            wanted = entry(step, side)
            for index, slot in enumerate(slots):
                @pl.when(wanted == index)
                def _(slot=slot, side=side):
                    pltpu.make_async_copy(slot, held.at[step % 2, side], sems.at[step % 2, side]).start()

    def arrived(step):
        for side in range(2):
            pltpu.make_async_copy(slots[0], held.at[step % 2, side], sems.at[step % 2, side]).wait()

    @pl.when(steps > 0)
    def _():
        fetch(0)

    @pl.loop(0, steps)
    def _(step):
        arrived(step)

        @pl.when(step + 1 < steps)
        def _():
            fetch(step + 1)

        now = step % 2
        first, second = pl.ds(entry(step, 2), 1), pl.ds(entry(step, 3), 1)
        for start in range(0, rows, 256):
            part = pl.ds(start, 256)
            scores = product(held[now, 0], held[now, 1, part, :])
            down = jnp.max(scores, axis=0, keepdims=True)
            out[second, part] = jnp.maximum(out[second, part], down)
            along = jnp.maximum(scores[:, :128], scores[:, 128:])
            across[...] = along if start == 0 else jnp.maximum(across[...], along)
        found = jnp.max(across[...].T, axis=0, keepdims=True)
        out[first, :] = jnp.maximum(out[first, :], found)

    for index, row in enumerate(sent):
        row[...] = out[pl.ds(table[at + 1 + index], 1), :]


def scored(best, slots, work, sends):
    names = sorted({slot for pairs in work for pair in pairs for slot in pair[:2]})
    most = max(len(pairs) for pairs in work)
    table = []
    for device, pairs in enumerate(work):
        table.append(len(pairs))
        table += [dict(permute).get(device, device) for permute in sends]
        for slot, other, block, visitor in pairs + [(names[0], names[0], 0, 0)] * (most - len(pairs)):
            table += [names.index(slot), names.index(other), block, visitor]
    given = [slots[name] for name in names]
    rows, depth = given[0].shape
    whole = pl.BlockSpec(memory_space=pltpu.VMEM)
    return pl.pallas_call(
        functools.partial(pairs_kernel, len(given), len(sends), most),
        out_shape=[jax.ShapeDtypeStruct(best.shape, jnp.float32)]
        + [jax.ShapeDtypeStruct((1, rows), jnp.float32)] * len(sends),
        in_specs=[pl.BlockSpec(memory_space=pltpu.SMEM), whole]
        + [pl.BlockSpec(memory_space=pl.ANY)] * len(given),
        out_specs=[whole] * (1 + len(sends)),
        scratch_shapes=[
            pltpu.VMEM((2, 2, rows, depth), jnp.bfloat16),
            pltpu.VMEM((rows, 128), jnp.float32),
            pltpu.SemaphoreType.DMA((2, 2)),
        ],
        compiler_params=pltpu.CompilerParams(vmem_limit_bytes=VMEM),
        cost_estimate=pl.CostEstimate(
            flops=2 * most * rows * rows * depth,
            bytes_accessed=4 * most * rows * depth,
            transcendentals=0,
        ),
        name="scored",
    )(jnp.asarray(np.array(table, np.int32)), best, *given)


def placed_kernel(taken, pads, order, best, *refs):
    found, out = refs[:-1], refs[-1]
    rows = order.shape[1]
    here = lax.axis_index("blk")
    total = best[pl.ds(here, 1), :]
    for index, row in enumerate(found):
        total = jnp.where(taken[here * len(found) + index] > 0, jnp.maximum(total, row[...]), total)
    column = jnp.broadcast_to(total, (128, rows)).T[:, :1]
    row = lax.broadcasted_iota(jnp.int32, (rows, 1), 0)
    in_order = jnp.max(jnp.where(order[...] == row, column, FLOOR), axis=0, keepdims=True)
    position = lax.broadcasted_iota(jnp.int32, (1, rows), 1)
    out[...] = jnp.where(position < rows - pads[here], in_order, 0.0)


def placed(best, found, permutes, order, pad_counts):
    rows = order.shape[0]
    taken = np.zeros((best.shape[0], len(permutes)), np.int32)
    for index, permute in enumerate(permutes):
        taken[[to for _, to in permute], index] = 1
    whole, scalars = pl.BlockSpec(memory_space=pltpu.VMEM), pl.BlockSpec(memory_space=pltpu.SMEM)
    return pl.pallas_call(
        placed_kernel,
        out_shape=jax.ShapeDtypeStruct((1, rows), jnp.float32),
        in_specs=[scalars, scalars] + [whole] * (2 + len(found)),
        out_specs=whole,
        compiler_params=pltpu.CompilerParams(vmem_limit_bytes=VMEM),
        name="placed",
    )(jnp.asarray(taken.reshape(-1)), pad_counts, order.reshape(1, rows), best, *found).reshape(rows)


def local(embeddings, order, pad_counts):
    nblocks = lax.axis_size("blk")
    moves, work, sending = planned(nblocks)
    unit = normalized(embeddings, order, pad_counts)
    slots = {"own": unit}
    best = own_block(unit, order, pad_counts, nblocks)
    touched, permutes, found = [set() for _ in range(nblocks)], [], []
    waiting = list(moves)
    for stage, pairs in enumerate(work):
        if stage == 1 and nblocks == 16:
            slots["late"], slots["R1"], best = lax.optimization_barrier((unit, slots["R1"], best))
        while waiting and waiting[0].source in slots:
            move = waiting.pop(0)
            slots[move.name] = lax.ppermute(slots[move.source], "blk", move.pairs)
            if move.name == "A":
                break
        for device, mine in enumerate(pairs):
            touched[device] |= {block for pair in mine for block in pair[2:] if block != device}
        sends = []
        if stage in sending:
            sends = colored([(of, to) for of in range(nblocks) for to in sorted(touched[of])], nblocks)
            touched = [set() for _ in range(nblocks)]
        if any(pairs):
            best, *rows = scored(best, slots, pairs, sends)
            found += [lax.ppermute(row, "blk", permute) for row, permute in zip(rows, sends)]
            permutes += sends
    return placed(best, found, permutes, order, pad_counts)


def solution(mesh):
    in_specs = (P(("groups", "blk"), None), P(("groups", "blk")), P("groups"))
    out_specs = P(("groups", "blk"))
    return jax.shard_map(local, mesh=mesh, in_specs=in_specs, out_specs=out_specs, check_vma=False)
```

```python
import functools

import jax
import jax.numpy as jnp
import numpy as np
from jax import lax
from jax.experimental import pallas as pl
from jax.experimental.pallas import tpu as pltpu
from jax.sharding import PartitionSpec as P

STEPS = 6
VMEM = 62 * 2**20
FLOOR = -2.0


class Move:
    def __init__(self, name, source, pairs, begins, stage, *after):
        self.name, self.source, self.pairs = name, source, pairs
        self.begins, self.stage, self.needs = begins, stage, (source, *after)


def grid_moves():
    def at(z, y, lane):
        return 4 * z + 2 * y + (y if lane == 0 else 1 - y)

    def rows(links):
        return [
            (at(z, y, lane), at(to, y, land)) for y in (0, 1) for (z, lane), (to, land) in links
        ]

    def across(planes, lane):
        return [(at(z, y, lane), at(z, 1 - y, lane)) for z in planes for y in (0, 1)]

    planes = range(4)
    first = [((0, 0), (2, 0)), ((2, 0), (3, 0)), ((3, 0), (1, 0)), ((1, 0), (0, 0)), ((0, 1), (1, 1))]
    second = [((3, 1), (1, 1)), ((1, 1), (0, 1)), ((2, 1), (3, 1)), ((1, 0), (2, 0))]
    swap = [((z, lane), (z, 1 - lane)) for z in planes for lane in (0, 1)]
    return [
        Move("A", "own", rows(swap), 0, 0),
        Move("R1", "own", rows(first), 0, 1),
        Move("YX", "own", across(planes, 0), 0, 1),
        Move("R2", "own", rows(second), 1, 2, "R1"),
        Move("YN", "own", across(planes, 1), 1, 2, "R1"),
        Move("V", "R1", rows([((2, 0), (3, 0))]) + across([1], 1), 1, 2),
        Move("W", "R1", rows([((1, 0), (1, 1)), ((1, 1), (1, 0))]), 1, 1),
        Move("FX", "YX", rows([((z, 0), (z, 1)) for z in planes]), 1, 1),
        Move("R3", "own", rows([((1, 1), (2, 1)), ((2, 0), (1, 1))]), 2, 3, "R2"),
        Move("FN", "YN", rows([((z, 1), (z, 0)) for z in planes]), 2, 2),
    ]


GRID_PAIRS = (
    ((0, 1), (0, 4), (1, 4), (3, 4)),
    ((0, 5), (1, 3), (3, 5)),
    ((0, 2), (0, 3), (0, 6), (2, 3), (3, 6)),
    ((1, 2), (2, 7), (3, 7)),
    ((1, 5), (1, 6), (1, 12), (4, 5), (6, 12)),
    ((1, 7), (1, 13), (2, 8), (2, 12), (2, 13), (5, 7), (5, 8), (7, 12), (7, 13)),
    ((1, 11), (1, 14), (1, 15), (2, 6), (2, 14), (2, 15), (4, 14), (4, 15), (6, 11)),
    ((2, 4), (2, 5), (4, 6), (4, 7), (5, 6), (5, 15), (6, 7)),
    ((0, 10), (0, 11), (4, 8), (4, 9), (4, 10), (8, 9), (8, 11), (9, 11)),
    ((5, 9), (5, 10), (5, 11), (9, 10)),
    ((6, 8), (6, 9), (6, 10)),
    ((3, 8), (3, 9), (7, 8), (7, 9), (7, 10), (7, 11), (8, 10), (10, 11)),
    ((0, 12), (0, 13), (0, 14), (0, 15), (8, 12), (8, 13), (8, 14)),
    ((9, 12), (9, 13), (9, 14), (9, 15), (12, 13), (13, 15)),
    ((10, 12), (10, 13), (10, 14), (10, 15), (12, 14), (12, 15)),
    ((3, 13), (3, 14), (3, 15), (11, 12), (11, 13), (11, 14), (11, 15), (13, 14), (14, 15)),
)


def ring_moves(count):
    return [
        Move("N%d" % k, "own", [((i + k) % count, i) for i in range(count)], 0, k)
        for k in range(1, STEPS + 1)
    ]


def planned(count):
    if count == 16:
        moves, placed_pairs, sending = grid_moves(), GRID_PAIRS, (2, 3)
    else:
        moves, sending = ring_moves(count), (STEPS,)
        placed_pairs = [[(b, (b + k) % count) for k in range(1, STEPS + 1)] for b in range(count)]
    holds = {"own": {d: d for d in range(count)}}
    stage_of = {"own": 0}
    for move in moves:
        holds[move.name] = {to: holds[move.source][of] for of, to in move.pairs}
        stage_of[move.name] = move.stage
    stages = 1 + max(stage_of.values())
    work = [[[] for _ in range(count)] for _ in range(stages)]
    for device, pairs in enumerate(placed_pairs):
        slot_of = {}
        for slot in sorted(stage_of, key=stage_of.get):
            if device in holds[slot]:
                slot_of.setdefault(holds[slot][device], slot)
        for block, visitor in pairs:
            slot, other = slot_of[block], slot_of[visitor]
            stage = max(stage_of[slot], stage_of[other])
            work[stage][device].append((slot, other, block, visitor))
    scored_pairs = sorted(tuple(sorted(pair)) for pairs in placed_pairs for pair in pairs)
    needed = {tuple(sorted((b, (b + k) % count))) for b in range(count) for k in range(1, STEPS + 1)}
    assert scored_pairs == sorted(needed)
    return moves, work, sending


def colored(edges, count):
    sends, takes = [{} for _ in range(count)], [{} for _ in range(count)]
    for of, to in edges:
        a = next(c for c in range(len(edges)) if c not in sends[of])
        b = next(c for c in range(len(edges)) if c not in takes[to])
        path, node, tables, colour = [], to, (takes, sends), a
        while a != b and colour in tables[0][node]:
            end = tables[0][node][colour]
            path.append(((end, node) if tables[0] is takes else (node, end), colour))
            node, tables, colour = end, tables[::-1], a + b - colour
        for (first, second), colour in path:
            del sends[first][colour], takes[second][colour]
        for (first, second), colour in path:
            sends[first][a + b - colour], takes[second][a + b - colour] = second, first
        sends[of][a], takes[to][a] = to, of
    return [
        [(of, to[c]) for of, to in enumerate(sends) if c in to]
        for c in range(max((c + 1 for to in sends for c in to), default=0))
    ]


def unit_kernel(pads, order_smem, order, embeddings, unit, value, result, tile, into, out, sem):
    rows = unit.shape[0]
    count = rows // into.shape[0]
    parts = [pl.ds(start, count) for start in range(0, rows, count)]
    loads = [
        pltpu.make_async_copy(embeddings.at[part], value.at[part], into.at[index])
        for index, part in enumerate(parts)
    ]
    stores = [
        pltpu.make_async_copy(result.at[part], unit.at[part], out.at[index])
        for index, part in enumerate(parts)
    ]
    first = order_smem[0]
    base = pl.multiple_of((first // 16) * 16, 16)
    filling = pltpu.make_async_copy(embeddings.at[pl.ds(base, 16)], tile, sem)
    filling.start()
    for load in loads:
        load.start()
    filling.wait()
    among = lax.broadcasted_iota(jnp.int32, (16, 1), 0) == first - base
    filler = jnp.sum(jnp.where(among, tile[...].astype(jnp.float32), 0.0), axis=0, keepdims=True)
    for index, part in enumerate(parts):
        found = valid_rows(pads, order, index * count, count)
        loads[index].wait()
        chunk = jnp.where(found, value[part, :].astype(jnp.float32), filler)
        scale = lax.rsqrt(jnp.sum(chunk * chunk, axis=1, keepdims=True) + 1e-06)
        result[part, :] = (chunk * scale).astype(jnp.bfloat16)
        stores[index].start()
    for store in stores:
        store.wait()


def valid_rows(pads, order, start, count):
    rows = order.shape[1]
    valid_count = rows - pads[lax.axis_index("blk")]
    position = lax.broadcasted_iota(jnp.int32, (1, rows), 1)
    kept = jnp.where(position < valid_count, order[...], -1)
    row = start + lax.broadcasted_iota(jnp.int32, (count, 1), 0)
    return jnp.max(jnp.where(kept == row, 1.0, 0.0), axis=1, keepdims=True) > 0.0


def normalized(embeddings, order, pad_counts):
    rows, depth = embeddings.shape
    chunks = 4
    scalars = pl.BlockSpec(memory_space=pltpu.SMEM)
    return pl.pallas_call(
        unit_kernel,
        out_shape=jax.ShapeDtypeStruct((rows, depth), jnp.bfloat16),
        in_specs=[
            scalars,
            scalars,
            pl.BlockSpec(memory_space=pltpu.VMEM),
            pl.BlockSpec(memory_space=pl.ANY),
        ],
        out_specs=pl.BlockSpec(memory_space=pl.ANY),
        scratch_shapes=[
            pltpu.VMEM((rows, depth), jnp.bfloat16),
            pltpu.VMEM((rows, depth), jnp.bfloat16),
            pltpu.VMEM((16, depth), jnp.bfloat16),
            pltpu.SemaphoreType.DMA((chunks,)),
            pltpu.SemaphoreType.DMA((chunks,)),
            pltpu.SemaphoreType.DMA,
        ],
        compiler_params=pltpu.CompilerParams(vmem_limit_bytes=VMEM),
        cost_estimate=pl.CostEstimate(
            flops=4 * rows * depth, bytes_accessed=4 * rows * depth, transcendentals=rows
        ),
        name="normalized",
    )(pad_counts, order, order.reshape(1, rows), embeddings)


def product(left, right):
    return lax.dot_general(left, right, (((1,), (1,)), ((), ())), preferred_element_type=jnp.float32)


def own_kernel(pads, order, unit, best):
    rows = unit.shape[0]
    best[...] = jnp.full(best.shape, FLOOR, jnp.float32)
    valid = valid_rows(pads, order, 0, rows)
    row = lax.broadcasted_iota(jnp.int32, (rows, 1), 0)
    here = pl.ds(lax.axis_index("blk"), 1)
    for start in range(0, rows, 256):
        part = pl.ds(start, 256)
        scores = product(unit[...], unit[part, :])
        column = start + lax.broadcasted_iota(jnp.int32, (1, 256), 1)
        scores = jnp.where(valid & (row != column), scores, FLOOR)
        best[here, part] = jnp.max(scores, axis=0, keepdims=True)


def own_block(unit, order, pad_counts, nblocks):
    rows, depth = unit.shape
    whole = pl.BlockSpec(memory_space=pltpu.VMEM)
    return pl.pallas_call(
        own_kernel,
        out_shape=jax.ShapeDtypeStruct((nblocks, rows), jnp.float32),
        in_specs=[pl.BlockSpec(memory_space=pltpu.SMEM), whole, whole],
        out_specs=whole,
        compiler_params=pltpu.CompilerParams(vmem_limit_bytes=VMEM),
        cost_estimate=pl.CostEstimate(
            flops=2 * rows * rows * depth, bytes_accessed=2 * rows * depth, transcendentals=0
        ),
        name="own_block",
    )(pad_counts, order.reshape(1, rows), unit)


def pairs_kernel(ntaken, nslots, nsends, most, table, best, *refs):
    refs = list(refs)
    arrivals, slots, (out, *sent) = (
        [refs.pop(0) for _ in range(count)] for count in (ntaken, nslots, 1 + nsends)
    )
    held, across, sems = refs
    rows = out.shape[1]
    here = lax.axis_index("blk")
    fixed = 1 + nsends + ntaken
    at = here * (fixed + 4 * most)
    steps = table[at]

    def entry(step, which):
        return table[at + fixed + 4 * step + which]

    def fetch(step):
        for side in range(2):
            wanted = entry(step, side)
            for index, slot in enumerate(slots):
                @pl.when(wanted == index)
                def _(slot=slot, side=side):
                    pltpu.make_async_copy(slot, held.at[step % 2, side], sems.at[step % 2, side]).start()

    def arrived(step):
        for side in range(2):
            pltpu.make_async_copy(slots[0], held.at[step % 2, side], sems.at[step % 2, side]).wait()

    @pl.when(steps > 0)
    def _():
        fetch(0)

    out[...] = best[...]
    own = pl.ds(here, 1)
    for index, row in enumerate(arrivals):
        taken = table[at + 1 + nsends + index] > 0
        out[own, :] = jnp.where(taken, jnp.maximum(out[own, :], row[...]), out[own, :])

    @pl.loop(0, steps)
    def _(step):
        arrived(step)

        @pl.when(step + 1 < steps)
        def _():
            fetch(step + 1)

        now = step % 2
        first, second = pl.ds(entry(step, 2), 1), pl.ds(entry(step, 3), 1)
        for start in range(0, rows, 256):
            part = pl.ds(start, 256)
            scores = product(held[now, 0], held[now, 1, part, :])
            down = jnp.max(scores, axis=0, keepdims=True)
            out[second, part] = jnp.maximum(out[second, part], down)
            along = jnp.maximum(scores[:, :128], scores[:, 128:])
            across[...] = along if start == 0 else jnp.maximum(across[...], along)
        found = jnp.max(across[...].T, axis=0, keepdims=True)
        out[first, :] = jnp.maximum(out[first, :], found)

    for index, row in enumerate(sent):
        row[...] = out[pl.ds(table[at + 1 + index], 1), :]


def scored(best, found, permutes, slots, work, sends):
    names = sorted({slot for pairs in work for pair in pairs for slot in pair[:2]})
    most = max(len(pairs) for pairs in work)
    table = []
    for device, pairs in enumerate(work):
        table.append(len(pairs))
        table += [dict(permute).get(device, device) for permute in sends]
        table += [int(device in dict(permute).values()) for permute in permutes]
        for slot, other, block, visitor in pairs + [(names[0], names[0], 0, 0)] * (most - len(pairs)):
            table += [names.index(slot), names.index(other), block, visitor]
    given = [slots[name] for name in names]
    rows, depth = given[0].shape
    whole = pl.BlockSpec(memory_space=pltpu.VMEM)
    return pl.pallas_call(
        functools.partial(pairs_kernel, len(found), len(given), len(sends), most),
        out_shape=[jax.ShapeDtypeStruct(best.shape, jnp.float32)]
        + [jax.ShapeDtypeStruct((1, rows), jnp.float32)] * len(sends),
        in_specs=[pl.BlockSpec(memory_space=pltpu.SMEM)]
        + [whole] * (1 + len(found))
        + [pl.BlockSpec(memory_space=pl.ANY)] * len(given),
        out_specs=[whole] * (1 + len(sends)),
        scratch_shapes=[
            pltpu.VMEM((2, 2, rows, depth), jnp.bfloat16),
            pltpu.VMEM((rows, 128), jnp.float32),
            pltpu.SemaphoreType.DMA((2, 2)),
        ],
        compiler_params=pltpu.CompilerParams(vmem_limit_bytes=VMEM),
        cost_estimate=pl.CostEstimate(
            flops=2 * most * rows * rows * depth,
            bytes_accessed=4 * most * rows * depth,
            transcendentals=0,
        ),
        name="scored",
    )(jnp.asarray(np.array(table, np.int32)), best, *found, *given)


def placed_kernel(taken, pads, order, best, *refs):
    found, out = refs[:-1], refs[-1]
    rows = order.shape[1]
    here = lax.axis_index("blk")
    total = best[pl.ds(here, 1), :]
    for index, row in enumerate(found):
        total = jnp.where(taken[here * len(found) + index] > 0, jnp.maximum(total, row[...]), total)
    column = jnp.broadcast_to(total, (128, rows)).T[:, :1]
    row = lax.broadcasted_iota(jnp.int32, (rows, 1), 0)
    in_order = jnp.max(jnp.where(order[...] == row, column, FLOOR), axis=0, keepdims=True)
    position = lax.broadcasted_iota(jnp.int32, (1, rows), 1)
    out[...] = jnp.where(position < rows - pads[here], in_order, 0.0)


def placed(best, found, permutes, order, pad_counts):
    rows = order.shape[0]
    taken = np.zeros((best.shape[0], len(permutes)), np.int32)
    for index, permute in enumerate(permutes):
        taken[[to for _, to in permute], index] = 1
    whole, scalars = pl.BlockSpec(memory_space=pltpu.VMEM), pl.BlockSpec(memory_space=pltpu.SMEM)
    return pl.pallas_call(
        placed_kernel,
        out_shape=jax.ShapeDtypeStruct((1, rows), jnp.float32),
        in_specs=[scalars, scalars] + [whole] * (2 + len(found)),
        out_specs=whole,
        compiler_params=pltpu.CompilerParams(vmem_limit_bytes=VMEM),
        name="placed",
    )(jnp.asarray(taken.reshape(-1)), pad_counts, order.reshape(1, rows), best, *found).reshape(rows)


def local(embeddings, order, pad_counts):
    nblocks = lax.axis_size("blk")
    moves, work, sending = planned(nblocks)
    unit = normalized(embeddings, order, pad_counts)
    slots, best = {"own": unit}, None
    touched, permutes, found = [set() for _ in range(nblocks)], [], []
    for stage, pairs in enumerate(work):
        starting = [move for move in moves if move.begins == stage]
        for needs in sorted({move.needs for move in starting}):
            values = [slots[name] for name in needs]
            if best is not None:
                *values, best = lax.optimization_barrier((*values, best))
            for move in starting:
                if move.needs == needs:
                    value = values[needs.index(move.source)]
                    slots[move.name] = lax.ppermute(value, "blk", move.pairs)
        if stage == 0:
            best = own_block(unit, order, pad_counts, nblocks)
        for device, mine in enumerate(pairs):
            touched[device] |= {block for pair in mine for block in pair[2:] if block != device}
        sends = []
        if stage in sending:
            sends = colored([(of, to) for of in range(nblocks) for to in sorted(touched[of])], nblocks)
            touched = [set() for _ in range(nblocks)]
        if any(pairs):
            best, *rows = scored(best, found, permutes, slots, pairs, sends)
            found = [lax.ppermute(row, "blk", permute) for row, permute in zip(rows, sends)]
            permutes = sends
    return placed(best, found, permutes, order, pad_counts)


def solution(mesh):
    in_specs = (P(("groups", "blk"), None), P(("groups", "blk")), P("groups"))
    out_specs = P(("groups", "blk"))
    return jax.shard_map(local, mesh=mesh, in_specs=in_specs, out_specs=out_specs, check_vma=False)
```

```python
import functools

import jax
import jax.numpy as jnp
import numpy as np
from jax import lax
from jax.experimental import pallas as pl
from jax.experimental.pallas import tpu as pltpu
from jax.sharding import PartitionSpec as P

STEPS = 6
VMEM = 62 * 2**20
FLOOR = -2.0
MOST_PADS = 256


class Move:
    def __init__(self, name, source, pairs, begins, stage, *after):
        self.name, self.source, self.pairs = name, source, pairs
        self.begins, self.stage, self.needs = begins, stage, (source, *after)


def grid_moves():
    def at(z, y, lane):
        return 4 * z + 2 * y + (y if lane == 0 else 1 - y)

    def rows(links):
        return [
            (at(z, y, lane), at(to, y, land)) for y in (0, 1) for (z, lane), (to, land) in links
        ]

    def across(planes):
        return [(at(z, y, lane), at(z, 1 - y, lane)) for z, lane in planes for y in (0, 1)]

    every = [(z, lane) for z in range(4) for lane in (0, 1)]
    swap = rows([((z, lane), (z, 1 - lane)) for z, lane in every])
    first = [((0, 0), (2, 0)), ((2, 0), (3, 0)), ((3, 0), (1, 0)), ((1, 0), (0, 0)), ((0, 1), (1, 1))]
    second = [((3, 1), (1, 1)), ((1, 1), (0, 1)), ((2, 1), (3, 1)), ((1, 0), (2, 0))]
    return [
        Move("R1", "own", rows(first), 0, 1),
        Move("R2", "own", rows(second), 0, 1),
        Move("Y", "own", across(every), 0, 1),
        Move("A", "own", swap, 0, 0),
        Move("R3", "own", rows([((1, 1), (2, 1)), ((2, 0), (1, 1))]), 1, 2, "R1"),
        Move("V", "R1", rows([((2, 0), (3, 0))]) + across([(1, 1)]), 1, 2),
        Move("F", "Y", swap, 1, 1),
        Move("W", "R1", rows([((1, 0), (1, 1)), ((1, 1), (1, 0))]), 1, 1),
    ]


GRID_PAIRS = (
    ((0, 1), (0, 4), (1, 2), (1, 4), (3, 4)),
    ((0, 5), (1, 5), (2, 5), (3, 5)),
    ((0, 2), (0, 6), (1, 6), (2, 6), (3, 6)),
    ((0, 3), (1, 3), (2, 3), (2, 7), (3, 7)),
    ((1, 7), (4, 5), (4, 7), (5, 6), (7, 12)),
    ((1, 12), (1, 13), (2, 8), (2, 12), (2, 13), (6, 12), (7, 13), (8, 13)),
    ((1, 11), (1, 14), (1, 15), (2, 4), (2, 14), (4, 14), (4, 15), (6, 7), (11, 15)),
    ((2, 15), (4, 6), (5, 7), (5, 15)),
    ((0, 10), (0, 11), (4, 8), (4, 9), (4, 10)),
    ((5, 8), (5, 9), (5, 10), (5, 11), (8, 9), (8, 11), (9, 11)),
    ((6, 8), (6, 9), (6, 10), (6, 11), (8, 10), (9, 10)),
    ((3, 8), (3, 9), (7, 8), (7, 9), (7, 10), (7, 11), (10, 11)),
    ((0, 12), (0, 13), (0, 14), (0, 15), (8, 12), (8, 14), (12, 13), (13, 14), (13, 15)),
    ((9, 12), (9, 13), (9, 14), (9, 15), (12, 14)),
    ((10, 12), (10, 13), (10, 14), (10, 15)),
    ((3, 13), (3, 14), (3, 15), (11, 12), (11, 13), (11, 14), (12, 15), (14, 15)),
)


def ring_moves(count):
    return [
        Move("N%d" % k, "own", [((i + k) % count, i) for i in range(count)], 0, k)
        for k in range(1, STEPS + 1)
    ]


def planned(count):
    if count == 16:
        moves, placed_pairs = grid_moves(), GRID_PAIRS
    else:
        moves = ring_moves(count)
        placed_pairs = [[(b, (b + k) % count) for k in range(1, STEPS + 1)] for b in range(count)]
    holds = {"own": {d: d for d in range(count)}}
    stage_of = {"own": 0}
    for move in moves:
        holds[move.name] = {to: holds[move.source][of] for of, to in move.pairs}
        stage_of[move.name] = move.stage
    stages = 1 + max(stage_of.values())
    work = [[[] for _ in range(count)] for _ in range(stages)]
    for device, pairs in enumerate(placed_pairs):
        slot_of = {}
        for slot in sorted(stage_of, key=stage_of.get):
            if device in holds[slot]:
                slot_of.setdefault(holds[slot][device], slot)
        for block, visitor in pairs:
            slot, other = slot_of[block], slot_of[visitor]
            stage = max(stage_of[slot], stage_of[other])
            work[stage][device].append((slot, other, block, visitor))
    scored_pairs = sorted(tuple(sorted(pair)) for pairs in placed_pairs for pair in pairs)
    needed = {tuple(sorted((b, (b + k) % count))) for b in range(count) for k in range(1, STEPS + 1)}
    assert scored_pairs == sorted(needed)
    return moves, work


def colored(edges, count):
    sends, takes = [{} for _ in range(count)], [{} for _ in range(count)]
    for of, to in edges:
        a = next(c for c in range(len(edges)) if c not in sends[of])
        b = next(c for c in range(len(edges)) if c not in takes[to])
        path, node, tables, colour = [], to, (takes, sends), a
        while a != b and colour in tables[0][node]:
            end = tables[0][node][colour]
            path.append(((end, node) if tables[0] is takes else (node, end), colour))
            node, tables, colour = end, tables[::-1], a + b - colour
        for (first, second), colour in path:
            del sends[first][colour], takes[second][colour]
        for (first, second), colour in path:
            sends[first][a + b - colour], takes[second][a + b - colour] = second, first
        sends[of][a], takes[to][a] = to, of
    return [
        [(of, to[c]) for of, to in enumerate(sends) if c in to]
        for c in range(max((c + 1 for to in sends for c in to), default=0))
    ]


def unit_kernel(pads, order_smem, order, embeddings, unit, value, result, tile, into, out, sem):
    rows = unit.shape[0]
    count = rows // into.shape[0]
    parts = [pl.ds(start, count) for start in range(0, rows, count)]
    loads = [
        pltpu.make_async_copy(embeddings.at[part], value.at[part], into.at[index])
        for index, part in enumerate(parts)
    ]
    stores = [
        pltpu.make_async_copy(result.at[part], unit.at[part], out.at[index])
        for index, part in enumerate(parts)
    ]
    first = order_smem[0]
    base = pl.multiple_of((first // 16) * 16, 16)
    filling = pltpu.make_async_copy(embeddings.at[pl.ds(base, 16)], tile, sem)
    filling.start()
    for load in loads:
        load.start()
    filling.wait()
    among = lax.broadcasted_iota(jnp.int32, (16, 1), 0) == first - base
    filler = jnp.sum(jnp.where(among, tile[...].astype(jnp.float32), 0.0), axis=0, keepdims=True)
    for index, part in enumerate(parts):
        found = valid_rows(pads, order, index * count, count)
        loads[index].wait()
        chunk = jnp.where(found, value[part, :].astype(jnp.float32), filler)
        scale = lax.rsqrt(jnp.sum(chunk * chunk, axis=1, keepdims=True) + 1e-06)
        result[part, :] = (chunk * scale).astype(jnp.bfloat16)
        stores[index].start()
    for store in stores:
        store.wait()


def valid_rows(pads, order, start, count):
    rows = order.shape[1]
    most = min(rows, MOST_PADS)
    valid_count = rows - pads[lax.axis_index("blk")]
    position = rows - most + lax.broadcasted_iota(jnp.int32, (1, most), 1)
    padding = jnp.where(position < valid_count, -1, order[:, rows - most :])
    row = start + lax.broadcasted_iota(jnp.int32, (count, 1), 0)
    return jnp.max(jnp.where(padding == row, 1.0, 0.0), axis=1, keepdims=True) < 1.0


def normalized(embeddings, order, pad_counts):
    rows, depth = embeddings.shape
    chunks = 4
    scalars = pl.BlockSpec(memory_space=pltpu.SMEM)
    return pl.pallas_call(
        unit_kernel,
        out_shape=jax.ShapeDtypeStruct((rows, depth), jnp.bfloat16),
        in_specs=[
            scalars,
            scalars,
            pl.BlockSpec(memory_space=pltpu.VMEM),
            pl.BlockSpec(memory_space=pl.ANY),
        ],
        out_specs=pl.BlockSpec(memory_space=pl.ANY),
        scratch_shapes=[
            pltpu.VMEM((rows, depth), jnp.bfloat16),
            pltpu.VMEM((rows, depth), jnp.bfloat16),
            pltpu.VMEM((16, depth), jnp.bfloat16),
            pltpu.SemaphoreType.DMA((chunks,)),
            pltpu.SemaphoreType.DMA((chunks,)),
            pltpu.SemaphoreType.DMA,
        ],
        compiler_params=pltpu.CompilerParams(vmem_limit_bytes=VMEM),
        cost_estimate=pl.CostEstimate(
            flops=4 * rows * depth, bytes_accessed=4 * rows * depth, transcendentals=rows
        ),
        name="normalized",
    )(pad_counts, order, order.reshape(1, rows), embeddings)


def product(left, right):
    return lax.dot_general(left, right, (((1,), (1,)), ((), ())), preferred_element_type=jnp.float32)


def own_kernel(pads, order, unit, best):
    rows = unit.shape[0]
    best[...] = jnp.full(best.shape, FLOOR, jnp.float32)
    valid = valid_rows(pads, order, 0, rows)
    row = lax.broadcasted_iota(jnp.int32, (rows, 1), 0)
    here = pl.ds(lax.axis_index("blk"), 1)
    for start in range(0, rows, 256):
        part = pl.ds(start, 256)
        scores = product(unit[...], unit[part, :])
        column = start + lax.broadcasted_iota(jnp.int32, (1, 256), 1)
        scores = jnp.where(valid & (row != column), scores, FLOOR)
        best[here, part] = jnp.max(scores, axis=0, keepdims=True)


def own_block(unit, order, pad_counts, nblocks):
    rows, depth = unit.shape
    whole = pl.BlockSpec(memory_space=pltpu.VMEM)
    return pl.pallas_call(
        own_kernel,
        out_shape=jax.ShapeDtypeStruct((nblocks, rows), jnp.float32),
        in_specs=[pl.BlockSpec(memory_space=pltpu.SMEM), whole, whole],
        out_specs=whole,
        compiler_params=pltpu.CompilerParams(vmem_limit_bytes=VMEM),
        cost_estimate=pl.CostEstimate(
            flops=2 * rows * rows * depth, bytes_accessed=2 * rows * depth, transcendentals=0
        ),
        name="own_block",
    )(pad_counts, order.reshape(1, rows), unit)


def pairs_kernel(nslots, nrows, most, fresh, table, *refs):
    refs = list(refs)
    best = None if fresh else refs.pop(0)
    slots, out, sent, (held, across, sems) = refs[:nslots], refs[nslots], refs[nslots + 1 : -3], refs[-3:]
    rows = out.shape[1]
    fixed = 1 + nrows
    at = lax.axis_index("blk") * (fixed + 4 * most)
    steps = table[at]

    def entry(step, which):
        return table[at + fixed + 4 * step + which]

    def fetch(step):
        for side in range(2):
            wanted = entry(step, side)
            for index, slot in enumerate(slots):
                @pl.when(wanted == index)
                def _(slot=slot, side=side):
                    pltpu.make_async_copy(slot, held.at[step % 2, side], sems.at[step % 2, side]).start()

    def arrived(step):
        for side in range(2):
            pltpu.make_async_copy(slots[0], held.at[step % 2, side], sems.at[step % 2, side]).wait()

    @pl.when(steps > 0)
    def _():
        fetch(0)

    out[...] = jnp.full(out.shape, FLOOR, jnp.float32) if fresh else best[...]

    @pl.loop(0, steps)
    def _(step):
        arrived(step)

        @pl.when(step + 1 < steps)
        def _():
            fetch(step + 1)

        now = step % 2
        first, second = pl.ds(entry(step, 2), 1), pl.ds(entry(step, 3), 1)

        def maxima(start, scores):
            part = pl.ds(start, 256)
            down = jnp.max(scores, axis=0, keepdims=True)
            out[second, part] = jnp.maximum(out[second, part], down)
            along = jnp.maximum(scores[:, :128], scores[:, 128:])
            across[...] = along if start == 0 else jnp.maximum(across[...], along)

        last = None
        for start in range(0, rows, 256):
            scores = product(held[now, 0], held[now, 1, pl.ds(start, 256), :])
            if last is not None:
                maxima(*last)
            last = (start, scores)
        maxima(*last)
        found = jnp.max(across[...].T, axis=0, keepdims=True)
        out[first, :] = jnp.maximum(out[first, :], found)

    for index in range(nrows):
        row = out[pl.ds(table[at + 1 + index], 1), :]
        if len(sent) == nrows:
            sent[index][...] = row
        else:
            sent[0][pl.ds(index, 1), :] = row


def scored(best, slots, work, taken, split):
    names = sorted({slot for pairs in work for pair in pairs for slot in pair[:2]})
    most = max(len(pairs) for pairs in work)
    nrows = max(len(blocks) for blocks in taken)
    table = []
    for device, pairs in enumerate(work):
        table += [len(pairs)] + list(taken[device]) + [device] * (nrows - len(taken[device]))
        for slot, other, block, visitor in pairs + [(names[0], names[0], 0, 0)] * (most - len(pairs)):
            table += [names.index(slot), names.index(other), block, visitor]
    given = [slots[name] for name in names]
    rows, depth = given[0].shape
    whole = pl.BlockSpec(memory_space=pltpu.VMEM)
    before = [] if best is None else [best]
    out, *sent = pl.pallas_call(
        functools.partial(pairs_kernel, len(given), nrows, most, best is None),
        out_shape=[jax.ShapeDtypeStruct((len(work), rows), jnp.float32)]
        + [jax.ShapeDtypeStruct((1 if split else nrows, rows), jnp.float32)] * (nrows if split else 1),
        in_specs=[pl.BlockSpec(memory_space=pltpu.SMEM)]
        + [whole] * len(before)
        + [pl.BlockSpec(memory_space=pl.ANY)] * len(given),
        out_specs=[whole] * (1 + (nrows if split else 1)),
        scratch_shapes=[
            pltpu.VMEM((2, 2, rows, depth), jnp.bfloat16),
            pltpu.VMEM((rows, 128), jnp.float32),
            pltpu.SemaphoreType.DMA((2, 2)),
        ],
        compiler_params=pltpu.CompilerParams(vmem_limit_bytes=VMEM),
        cost_estimate=pl.CostEstimate(
            flops=2 * most * rows * rows * depth,
            bytes_accessed=4 * most * rows * depth,
            transcendentals=0,
        ),
        name="scored",
    )(jnp.asarray(np.array(table, np.int32)), *before, *given)
    return out, sent


def placed_kernel(ngathered, taken, pads, order, *refs):
    refs = list(refs)
    out, gathered = refs.pop(), refs.pop(0) if ngathered else None
    here = lax.axis_index("blk")
    rows = order.shape[1]
    own = [ref for ref in refs if ref.shape[0] > 1]
    found = [ref for ref in refs if ref.shape[0] == 1]
    at = here * (1 + 2 * ngathered + len(found))
    total = jnp.full((1, rows), FLOOR, jnp.float32)
    for ref in own:
        total = jnp.maximum(total, ref[pl.ds(here, 1), :])
    for index in range(ngathered):
        entry = at + 1 + 2 * index
        row = gathered[taken[entry], pl.ds(taken[entry + 1], 1), :]
        total = jnp.where(index < taken[at], jnp.maximum(total, row), total)
    for index, ref in enumerate(found):
        handed = taken[at + 1 + 2 * ngathered + index] > 0
        total = jnp.where(handed, jnp.maximum(total, ref[...]), total)
    column = jnp.broadcast_to(total, (128, rows)).T[:, :1]
    row = lax.broadcasted_iota(jnp.int32, (rows, 1), 0)
    in_order = jnp.max(jnp.where(order[...] == row, column, FLOOR), axis=0, keepdims=True)
    position = lax.broadcasted_iota(jnp.int32, (1, rows), 1)
    out[...] = jnp.where(position < rows - pads[here], in_order, 0.0)


def placed(bests, gathered, handed, found, permutes, order, pad_counts):
    rows = order.shape[0]
    count = bests[0].shape[0]
    entries = [
        [(device, index) for device in range(count) for index, b in enumerate(handed[device]) if b == mine]
        for mine in range(count)
    ]
    most = max(len(mine) for mine in entries)
    taken = []
    for mine in range(count):
        taken.append(len(entries[mine]))
        for entry in entries[mine] + [(0, 0)] * (most - len(entries[mine])):
            taken += entry
        taken += [int(mine in dict(permute).values()) for permute in permutes]
    whole, scalars = pl.BlockSpec(memory_space=pltpu.VMEM), pl.BlockSpec(memory_space=pltpu.SMEM)
    given = [order.reshape(1, rows)] + [gathered] * (most > 0) + bests + found
    return pl.pallas_call(
        functools.partial(placed_kernel, most),
        out_shape=jax.ShapeDtypeStruct((1, rows), jnp.float32),
        in_specs=[scalars, scalars] + [whole] * len(given),
        out_specs=whole,
        compiler_params=pltpu.CompilerParams(vmem_limit_bytes=VMEM),
        name="placed",
    )(jnp.asarray(np.array(taken, np.int32)), pad_counts, *given).reshape(rows)


def local(embeddings, order, pad_counts):
    nblocks = lax.axis_size("blk")
    moves, work = planned(nblocks)
    unit = normalized(embeddings, order, pad_counts)
    slots, best = {"own": unit}, None
    nothing = [[] for _ in range(nblocks)]
    touched, gathered, handed, bests = [set() for _ in range(nblocks)], None, nothing, []
    for stage, pairs in enumerate(work):
        starting = [move for move in moves if move.begins == stage]
        for needs in sorted({move.needs for move in starting}):
            values = [slots[name] for name in needs]
            if best is not None:
                *values, best = lax.optimization_barrier((*values, best))
            for move in starting:
                if move.needs == needs:
                    value = values[needs.index(move.source)]
                    slots[move.name] = lax.ppermute(value, "blk", move.pairs)
        if stage == 0:
            best = own_block(unit, order, pad_counts, nblocks)
        for device, mine in enumerate(pairs):
            touched[device] |= {block for pair in mine for block in pair[2:] if block != device}
        if stage == len(work) - 1:
            edges = [(of, to) for of in range(nblocks) for to in sorted(touched[of])]
            permutes = colored(edges, nblocks)
            rows = [[dict(permute).get(device, device) for permute in permutes] for device in range(nblocks)]
            bests = [best] * (gathered is not None)
            best, sent = scored(None if bests else best, slots, pairs, rows, True)
            found = [lax.ppermute(row, "blk", permute) for row, permute in zip(sent, permutes)]
        elif any(pairs):
            last = nblocks == 16 and stage == len(work) - 2
            handed = [sorted(mine) for mine in touched] if last else nothing
            best, sent = scored(best, slots, pairs, handed if last else [[d] for d in range(nblocks)], False)
            if last:
                gathered = lax.all_gather(sent[0], "blk")
                touched = [set() for _ in range(nblocks)]
    return placed(bests + [best], gathered, handed, found, permutes, order, pad_counts)


def solution(mesh):
    in_specs = (P(("groups", "blk"), None), P(("groups", "blk")), P("groups"))
    out_specs = P(("groups", "blk"))
    return jax.shard_map(local, mesh=mesh, in_specs=in_specs, out_specs=out_specs, check_vma=False)
```

```python
import functools

import jax
import jax.numpy as jnp
import numpy as np
from jax import lax
from jax.experimental import pallas as pl
from jax.experimental.pallas import tpu as pltpu
from jax.sharding import PartitionSpec as P

STEPS = 6
VMEM = 62 * 2**20
FLOOR = -2.0
MOST_PADS = 256
AHEAD = 3


class Move:
    def __init__(self, name, source, pairs, begins, stage, *after):
        self.name, self.source, self.pairs = name, source, pairs
        self.begins, self.stage, self.needs = begins, stage, (source, *after)


def grid_moves():
    def at(z, y, lane):
        return 4 * z + 2 * y + (y if lane == 0 else 1 - y)

    def rows(links):
        return [
            (at(z, y, lane), at(to, y, land)) for y in (0, 1) for (z, lane), (to, land) in links
        ]

    def across(planes):
        return [(at(z, y, lane), at(z, 1 - y, lane)) for z, lane in planes for y in (0, 1)]

    every = [(z, lane) for z in range(4) for lane in (0, 1)]
    swap = rows([((z, lane), (z, 1 - lane)) for z, lane in every])
    first = [((0, 0), (2, 0)), ((2, 0), (3, 0)), ((3, 0), (1, 0)), ((1, 0), (0, 0)), ((0, 1), (1, 1))]
    second = [((3, 1), (1, 1)), ((1, 1), (0, 1)), ((2, 1), (3, 1)), ((1, 0), (2, 0))]
    return [
        Move("R1", "own", rows(first), 0, 1),
        Move("R2", "own", rows(second), 0, 1),
        Move("Y", "own", across(every), 0, 1),
        Move("A", "own", swap, 0, 0),
        Move("R3", "own", rows([((1, 1), (2, 1)), ((2, 0), (1, 1))]), 1, 2, "R1"),
        Move("V", "R1", rows([((2, 0), (3, 0))]) + across([(1, 1)]), 1, 2),
        Move("F", "Y", swap, 1, 1),
        Move("W", "R1", rows([((1, 0), (1, 1)), ((1, 1), (1, 0))]), 1, 1),
    ]


GRID_PAIRS = (
    ((0, 1), (0, 4), (1, 2), (1, 4), (3, 4)),
    ((0, 5), (1, 5), (2, 5), (3, 5)),
    ((0, 2), (0, 6), (1, 6), (2, 6), (3, 6)),
    ((0, 3), (1, 3), (2, 3), (2, 7), (3, 7)),
    ((1, 7), (4, 5), (4, 7), (5, 6), (7, 12)),
    ((1, 12), (1, 13), (2, 8), (2, 12), (2, 13), (6, 12), (7, 13), (8, 13)),
    ((1, 11), (1, 14), (1, 15), (2, 4), (2, 14), (4, 14), (4, 15), (6, 7), (11, 15)),
    ((2, 15), (4, 6), (5, 7), (5, 15)),
    ((0, 10), (0, 11), (4, 8), (4, 9), (4, 10)),
    ((5, 8), (5, 9), (5, 10), (5, 11), (8, 9), (8, 11), (9, 11)),
    ((6, 8), (6, 9), (6, 10), (6, 11), (8, 10), (9, 10)),
    ((3, 8), (3, 9), (7, 8), (7, 9), (7, 10), (7, 11), (10, 11)),
    ((0, 12), (0, 13), (0, 14), (0, 15), (8, 12), (8, 14), (12, 13), (13, 14), (13, 15)),
    ((9, 12), (9, 13), (9, 14), (9, 15), (12, 14)),
    ((10, 12), (10, 13), (10, 14), (10, 15)),
    ((3, 13), (3, 14), (3, 15), (11, 12), (11, 13), (11, 14), (12, 15), (14, 15)),
)


def ring_moves(count):
    return [
        Move("N%d" % k, "own", [((i + k) % count, i) for i in range(count)], 0, k)
        for k in range(1, STEPS + 1)
    ]


def planned(count):
    if count == 16:
        moves, placed_pairs, sending = grid_moves(), GRID_PAIRS, (1, 2)
    else:
        moves, sending = ring_moves(count), (STEPS,)
        placed_pairs = [[(b, (b + k) % count) for k in range(1, STEPS + 1)] for b in range(count)]
    holds = {"own": {d: d for d in range(count)}}
    stage_of = {"own": 0}
    for move in moves:
        holds[move.name] = {to: holds[move.source][of] for of, to in move.pairs}
        stage_of[move.name] = move.stage
    stages = 1 + max(stage_of.values())
    work = [[[] for _ in range(count)] for _ in range(stages)]
    for device, pairs in enumerate(placed_pairs):
        slot_of = {}
        for slot in sorted(stage_of, key=stage_of.get):
            if device in holds[slot]:
                slot_of.setdefault(holds[slot][device], slot)
        for block, visitor in pairs:
            slot, other = slot_of[block], slot_of[visitor]
            stage = max(stage_of[slot], stage_of[other])
            work[stage][device].append((slot, other, block, visitor))
    scored_pairs = sorted(tuple(sorted(pair)) for pairs in placed_pairs for pair in pairs)
    needed = {tuple(sorted((b, (b + k) % count))) for b in range(count) for k in range(1, STEPS + 1)}
    assert scored_pairs == sorted(needed)
    return moves, work, sending


def colored(edges, count):
    sends, takes = [{} for _ in range(count)], [{} for _ in range(count)]
    for of, to in edges:
        a = next(c for c in range(len(edges)) if c not in sends[of])
        b = next(c for c in range(len(edges)) if c not in takes[to])
        path, node, tables, colour = [], to, (takes, sends), a
        while a != b and colour in tables[0][node]:
            end = tables[0][node][colour]
            path.append(((end, node) if tables[0] is takes else (node, end), colour))
            node, tables, colour = end, tables[::-1], a + b - colour
        for (first, second), colour in path:
            del sends[first][colour], takes[second][colour]
        for (first, second), colour in path:
            sends[first][a + b - colour], takes[second][a + b - colour] = second, first
        sends[of][a], takes[to][a] = to, of
    return [
        [(of, to[c]) for of, to in enumerate(sends) if c in to]
        for c in range(max((c + 1 for to in sends for c in to), default=0))
    ]


def unit_kernel(pads, order_smem, order, embeddings, unit, value, result, tile, into, out, sem):
    rows = unit.shape[0]
    count = rows // into.shape[0]
    parts = [pl.ds(start, count) for start in range(0, rows, count)]
    loads = [
        pltpu.make_async_copy(embeddings.at[part], value.at[part], into.at[index])
        for index, part in enumerate(parts)
    ]
    stores = [
        pltpu.make_async_copy(result.at[part], unit.at[part], out.at[index])
        for index, part in enumerate(parts)
    ]
    first = order_smem[0]
    base = pl.multiple_of((first // 16) * 16, 16)
    filling = pltpu.make_async_copy(embeddings.at[pl.ds(base, 16)], tile, sem)
    filling.start()
    for load in loads:
        load.start()
    filling.wait()
    among = lax.broadcasted_iota(jnp.int32, (16, 1), 0) == first - base
    filler = jnp.sum(jnp.where(among, tile[...].astype(jnp.float32), 0.0), axis=0, keepdims=True)
    for index, part in enumerate(parts):
        found = valid_rows(pads, order, index * count, count)
        loads[index].wait()
        chunk = jnp.where(found, value[part, :].astype(jnp.float32), filler)
        scale = lax.rsqrt(jnp.sum(chunk * chunk, axis=1, keepdims=True) + 1e-06)
        result[part, :] = (chunk * scale).astype(jnp.bfloat16)
        stores[index].start()
    for store in stores:
        store.wait()


def valid_rows(pads, order, start, count):
    rows = order.shape[1]
    most = min(rows, MOST_PADS)
    valid_count = rows - pads[lax.axis_index("blk")]
    position = rows - most + lax.broadcasted_iota(jnp.int32, (1, most), 1)
    padding = jnp.where(position < valid_count, -1, order[:, rows - most :])
    row = start + lax.broadcasted_iota(jnp.int32, (count, 1), 0)
    return jnp.max(jnp.where(padding == row, 1.0, 0.0), axis=1, keepdims=True) < 1.0


def normalized(embeddings, order, pad_counts):
    rows, depth = embeddings.shape
    chunks = 4
    scalars = pl.BlockSpec(memory_space=pltpu.SMEM)
    return pl.pallas_call(
        unit_kernel,
        out_shape=jax.ShapeDtypeStruct((rows, depth), jnp.bfloat16),
        in_specs=[
            scalars,
            scalars,
            pl.BlockSpec(memory_space=pltpu.VMEM),
            pl.BlockSpec(memory_space=pl.ANY),
        ],
        out_specs=pl.BlockSpec(memory_space=pl.ANY),
        scratch_shapes=[
            pltpu.VMEM((rows, depth), jnp.bfloat16),
            pltpu.VMEM((rows, depth), jnp.bfloat16),
            pltpu.VMEM((16, depth), jnp.bfloat16),
            pltpu.SemaphoreType.DMA((chunks,)),
            pltpu.SemaphoreType.DMA((chunks,)),
            pltpu.SemaphoreType.DMA,
        ],
        compiler_params=pltpu.CompilerParams(vmem_limit_bytes=VMEM),
        cost_estimate=pl.CostEstimate(
            flops=4 * rows * depth, bytes_accessed=4 * rows * depth, transcendentals=rows
        ),
        name="normalized",
    )(pad_counts, order, order.reshape(1, rows), embeddings)


def product(left, right):
    return lax.dot_general(left, right, (((1,), (1,)), ((), ())), preferred_element_type=jnp.float32)


def own_kernel(pads, order, unit, best):
    rows = unit.shape[0]
    best[...] = jnp.full(best.shape, FLOOR, jnp.float32)
    valid = valid_rows(pads, order, 0, rows)
    row = lax.broadcasted_iota(jnp.int32, (rows, 1), 0)
    here = pl.ds(lax.axis_index("blk"), 1)
    for start in range(0, rows, 256):
        part = pl.ds(start, 256)
        scores = product(unit[...], unit[part, :])
        column = start + lax.broadcasted_iota(jnp.int32, (1, 256), 1)
        scores = jnp.where(valid & (row != column), scores, FLOOR)
        best[here, part] = jnp.max(scores, axis=0, keepdims=True)


def own_block(unit, order, pad_counts, nblocks):
    rows, depth = unit.shape
    whole = pl.BlockSpec(memory_space=pltpu.VMEM)
    return pl.pallas_call(
        own_kernel,
        out_shape=jax.ShapeDtypeStruct((nblocks, rows), jnp.float32),
        in_specs=[pl.BlockSpec(memory_space=pltpu.SMEM), whole, whole],
        out_specs=whole,
        compiler_params=pltpu.CompilerParams(vmem_limit_bytes=VMEM),
        cost_estimate=pl.CostEstimate(
            flops=2 * rows * rows * depth, bytes_accessed=2 * rows * depth, transcendentals=0
        ),
        name="own_block",
    )(pad_counts, order.reshape(1, rows), unit)


def pairs_kernel(nslots, nrows, ntaken, nloads, npairs, table, best, *refs):
    arrivals, slots, out = refs[:ntaken], refs[ntaken : ntaken + nslots], refs[ntaken + nslots]
    sent, (held, across, sems) = refs[ntaken + nslots + 1 : -3], refs[-3:]
    rows = out.shape[1]
    here = lax.axis_index("blk")
    loads_at = here * (2 + nrows + ntaken + nloads + 5 * npairs) + 2 + nrows + ntaken
    pairs_at = loads_at + nloads
    rows_at = loads_at - nrows - ntaken
    loads, pairs = table[rows_at - 2], table[rows_at - 1]

    def fetch(load):
        @pl.when(load < loads)
        def _():
            wanted = table[loads_at + jnp.minimum(load, nloads - 1)]
            for index, slot in enumerate(slots):
                @pl.when(wanted == index)
                def _(slot=slot):
                    for start in range(0, rows, 256):
                        part = pl.ds(start, 256)
                        pltpu.make_async_copy(slot.at[part], held.at[load, part], sems.at[load]).start()

    for load in range(min(AHEAD, nloads)):
        fetch(load)
    out[...] = best[...]
    own = pl.ds(here, 1)
    for index, row in enumerate(arrivals):
        handed = table[rows_at + nrows + index] > 0
        out[own, :] = jnp.where(handed, jnp.maximum(out[own, :], row[...]), out[own, :])

    @pl.loop(0, pairs)
    def _(step):
        at = pairs_at + 5 * step
        before = jnp.where(step == 0, 0, table[jnp.maximum(at - 1, 0)])

        @pl.loop(before, table[at + 4])
        def _(load):
            pltpu.make_async_copy(slots[0], held.at[load], sems.at[load]).wait()
            fetch(load + AHEAD)

        left, right = table[at], table[at + 1]
        first, second = pl.ds(table[at + 2], 1), pl.ds(table[at + 3], 1)
        for start in range(0, rows, 256):
            part = pl.ds(start, 256)
            scores = product(held[left], held[right, part, :])
            down = jnp.max(scores, axis=0, keepdims=True)
            out[second, part] = jnp.maximum(out[second, part], down)
            along = jnp.maximum(scores[:, :128], scores[:, 128:])
            across[...] = along if start == 0 else jnp.maximum(across[...], along)
        found = jnp.max(across[...].T, axis=0, keepdims=True)
        out[first, :] = jnp.maximum(out[first, :], found)

    for index, row in enumerate(sent):
        row[...] = out[pl.ds(table[rows_at + index], 1), :]


def in_order_of_loads(pairs, rank):
    left, loaded, ordered = list(pairs), [], []
    while left:
        pair = min(
            left,
            key=lambda p: (sum(s not in loaded for s in p[:2]), max(rank[s] for s in p[:2]), p[2:]),
        )
        left.remove(pair)
        loaded += [slot for slot in pair[:2] if slot not in loaded]
        ordered.append((pair, len(loaded)))
    return loaded, ordered


def scored(best, found, permutes, slots, rank, work, sends):
    names = sorted({slot for pairs in work for pair in pairs for slot in pair[:2]})
    plans = [in_order_of_loads(pairs, rank) for pairs in work]
    nloads = max(len(loaded) for loaded, _ in plans)
    npairs = max(len(pairs) for pairs in work)
    table = []
    for device, (loaded, ordered) in enumerate(plans):
        table += [len(loaded), len(ordered)]
        table += [dict(permute).get(device, device) for permute in sends]
        table += [int(device in dict(permute).values()) for permute in permutes]
        table += [names.index(slot) for slot in loaded] + [0] * (nloads - len(loaded))
        for (slot, other, block, visitor), need in ordered:
            table += [loaded.index(slot), loaded.index(other), block, visitor, need]
        table += [0] * (5 * (npairs - len(ordered)))
    given = [slots[name] for name in names]
    rows, depth = given[0].shape
    whole = pl.BlockSpec(memory_space=pltpu.VMEM)
    return pl.pallas_call(
        functools.partial(pairs_kernel, len(given), len(sends), len(found), nloads, npairs),
        out_shape=[jax.ShapeDtypeStruct(best.shape, jnp.float32)]
        + [jax.ShapeDtypeStruct((1, rows), jnp.float32)] * len(sends),
        in_specs=[pl.BlockSpec(memory_space=pltpu.SMEM)]
        + [whole] * (1 + len(found))
        + [pl.BlockSpec(memory_space=pl.ANY)] * len(given),
        out_specs=[whole] * (1 + len(sends)),
        scratch_shapes=[
            pltpu.VMEM((nloads, rows, depth), jnp.bfloat16),
            pltpu.VMEM((rows, 128), jnp.float32),
            pltpu.SemaphoreType.DMA((nloads,)),
        ],
        compiler_params=pltpu.CompilerParams(vmem_limit_bytes=VMEM),
        cost_estimate=pl.CostEstimate(
            flops=2 * npairs * rows * rows * depth,
            bytes_accessed=2 * nloads * rows * depth,
            transcendentals=0,
        ),
        name="scored",
    )(jnp.asarray(np.array(table, np.int32)), best, *found, *given)


def placed_kernel(taken, pads, order, best, *refs):
    found, out = refs[:-1], refs[-1]
    rows = order.shape[1]
    here = lax.axis_index("blk")
    total = best[pl.ds(here, 1), :]
    for index, row in enumerate(found):
        total = jnp.where(taken[here * len(found) + index] > 0, jnp.maximum(total, row[...]), total)
    column = jnp.broadcast_to(total, (128, rows)).T[:, :1]
    row = lax.broadcasted_iota(jnp.int32, (rows, 1), 0)
    in_order = jnp.max(jnp.where(order[...] == row, column, FLOOR), axis=0, keepdims=True)
    position = lax.broadcasted_iota(jnp.int32, (1, rows), 1)
    out[...] = jnp.where(position < rows - pads[here], in_order, 0.0)


def placed(best, found, permutes, order, pad_counts):
    rows = order.shape[0]
    taken = np.zeros((best.shape[0], len(permutes)), np.int32)
    for index, permute in enumerate(permutes):
        taken[[to for _, to in permute], index] = 1
    whole, scalars = pl.BlockSpec(memory_space=pltpu.VMEM), pl.BlockSpec(memory_space=pltpu.SMEM)
    return pl.pallas_call(
        placed_kernel,
        out_shape=jax.ShapeDtypeStruct((1, rows), jnp.float32),
        in_specs=[scalars, scalars] + [whole] * (2 + len(found)),
        out_specs=whole,
        compiler_params=pltpu.CompilerParams(vmem_limit_bytes=VMEM),
        name="placed",
    )(jnp.asarray(taken.reshape(-1)), pad_counts, order.reshape(1, rows), best, *found).reshape(rows)


def local(embeddings, order, pad_counts):
    nblocks = lax.axis_size("blk")
    moves, work, sending = planned(nblocks)
    unit = normalized(embeddings, order, pad_counts)
    slots, best = {"own": unit}, None
    rank = dict({"own": -1}, **{move.name: move.stage for move in moves})
    touched, permutes, found = [set() for _ in range(nblocks)], [], []
    for stage, pairs in enumerate(work):
        starting = [move for move in moves if move.begins == stage]
        for needs in sorted({move.needs for move in starting}):
            values = [slots[name] for name in needs]
            if best is not None:
                *values, best = lax.optimization_barrier((*values, best))
            for move in starting:
                if move.needs == needs:
                    value = values[needs.index(move.source)]
                    slots[move.name] = lax.ppermute(value, "blk", move.pairs)
        if stage == 0:
            best = own_block(unit, order, pad_counts, nblocks)
        for device, mine in enumerate(pairs):
            touched[device] |= {block for pair in mine for block in pair[2:] if block != device}
        sends = []
        if stage in sending:
            sends = colored([(of, to) for of in range(nblocks) for to in sorted(touched[of])], nblocks)
            touched = [set() for _ in range(nblocks)]
        if any(pairs):
            best, *rows = scored(best, found, permutes, slots, rank, pairs, sends)
            found = [lax.ppermute(row, "blk", permute) for row, permute in zip(rows, sends)]
            permutes = sends
    return placed(best, found, permutes, order, pad_counts)


def solution(mesh):
    in_specs = (P(("groups", "blk"), None), P(("groups", "blk")), P("groups"))
    out_specs = P(("groups", "blk"))
    return jax.shard_map(local, mesh=mesh, in_specs=in_specs, out_specs=out_specs, check_vma=False)
```

```python
import functools

import jax
import jax.numpy as jnp
import numpy as np
from jax import lax
from jax.experimental import pallas as pl
from jax.experimental.pallas import tpu as pltpu
from jax.sharding import PartitionSpec as P

STEPS = 6
VMEM = 62 * 2**20
FLOOR = -2.0
MOST_PADS = 256
AHEAD = 3


class Move:
    def __init__(self, name, source, pairs, begins, stage, *after):
        self.name, self.source, self.pairs = name, source, pairs
        self.begins, self.stage, self.needs = begins, stage, (source, *after)


def grid_moves():
    def at(z, y, lane):
        return 4 * z + 2 * y + (y if lane == 0 else 1 - y)

    def rows(links):
        return [
            (at(z, y, lane), at(to, y, land)) for y in (0, 1) for (z, lane), (to, land) in links
        ]

    def across(planes):
        return [(at(z, y, lane), at(z, 1 - y, lane)) for z, lane in planes for y in (0, 1)]

    every = [(z, lane) for z in range(4) for lane in (0, 1)]
    swap = rows([((z, lane), (z, 1 - lane)) for z, lane in every])
    first = [((0, 0), (2, 0)), ((2, 0), (3, 0)), ((3, 0), (1, 0)), ((1, 0), (0, 0)), ((0, 1), (1, 1))]
    second = [((3, 1), (1, 1)), ((1, 1), (0, 1)), ((2, 1), (3, 1)), ((1, 0), (2, 1))]
    return [
        Move("R1", "own", rows(first), 0, 1),
        Move("R2", "own", rows(second), 0, 1),
        Move("Y", "own", across(every), 0, 1),
        Move("A", "own", swap, 0, 0),
        Move("R3", "own", rows([((1, 1), (2, 0)), ((2, 0), (1, 1))]), 1, 2, "R1"),
        Move("V", "R1", rows([((2, 0), (3, 0))]) + across([(1, 1)]), 1, 2),
        Move("F", "Y", swap, 1, 1),
        Move("W", "R1", rows([((1, 0), (1, 1)), ((1, 1), (1, 0))]), 1, 1),
    ]


GRID_PAIRS = (
    ((0, 1), (0, 4), (1, 3), (1, 4), (3, 4)),
    ((0, 5), (1, 2), (2, 5), (3, 5)),
    ((0, 6), (1, 6), (2, 6), (3, 6)),
    ((0, 2), (0, 3), (1, 7), (2, 3), (2, 7), (3, 7)),
    ((4, 5), (4, 7), (5, 6), (6, 12), (7, 12)),
    ((1, 5), (1, 12), (1, 13), (2, 8), (2, 12), (2, 13), (7, 13), (8, 12)),
    ((1, 11), (1, 14), (1, 15), (2, 4), (2, 14), (4, 6), (4, 14), (11, 14)),
    ((2, 15), (4, 15), (5, 7), (5, 15), (6, 7)),
    ((0, 10), (0, 11), (5, 8), (5, 9), (5, 10), (5, 11), (8, 11)),
    ((4, 8), (4, 9), (4, 10), (8, 9), (9, 11)),
    ((7, 8), (7, 9), (7, 10), (7, 11)),
    ((3, 8), (3, 9), (6, 8), (6, 9), (6, 10), (6, 11), (8, 10), (9, 10), (10, 11)),
    ((0, 12), (0, 13), (0, 14), (0, 15), (8, 13), (8, 14), (12, 15), (13, 14)),
    ((9, 12), (9, 13), (9, 14), (9, 15), (12, 13)),
    ((10, 12), (10, 13), (10, 14), (10, 15), (12, 14), (14, 15)),
    ((3, 13), (3, 14), (3, 15), (11, 12), (11, 13), (11, 15), (13, 15)),
)


def ring_moves(count):
    return [
        Move("N%d" % k, "own", [((i + k) % count, i) for i in range(count)], 0, k)
        for k in range(1, STEPS + 1)
    ]


def planned(count):
    if count == 16:
        moves, placed_pairs, sending = grid_moves(), GRID_PAIRS, (2,)
    else:
        moves, sending = ring_moves(count), (STEPS,)
        placed_pairs = [[(b, (b + k) % count) for k in range(1, STEPS + 1)] for b in range(count)]
    holds = {"own": {d: d for d in range(count)}}
    stage_of = {"own": 0}
    for move in moves:
        holds[move.name] = {to: holds[move.source][of] for of, to in move.pairs}
        stage_of[move.name] = move.stage
    stages = 1 + max(stage_of.values())
    work = [[[] for _ in range(count)] for _ in range(stages)]
    for device, pairs in enumerate(placed_pairs):
        slot_of = {}
        for slot in sorted(stage_of, key=stage_of.get):
            if device in holds[slot]:
                slot_of.setdefault(holds[slot][device], slot)
        for block, visitor in pairs:
            slot, other = slot_of[block], slot_of[visitor]
            stage = max(stage_of[slot], stage_of[other])
            work[stage][device].append((slot, other, block, visitor))
    scored_pairs = sorted(tuple(sorted(pair)) for pairs in placed_pairs for pair in pairs)
    needed = {tuple(sorted((b, (b + k) % count))) for b in range(count) for k in range(1, STEPS + 1)}
    assert scored_pairs == sorted(needed)
    return moves, work, sending


def colored(edges, count):
    sends, takes = [{} for _ in range(count)], [{} for _ in range(count)]
    for of, to in edges:
        a = next(c for c in range(len(edges)) if c not in sends[of])
        b = next(c for c in range(len(edges)) if c not in takes[to])
        path, node, tables, colour = [], to, (takes, sends), a
        while a != b and colour in tables[0][node]:
            end = tables[0][node][colour]
            path.append(((end, node) if tables[0] is takes else (node, end), colour))
            node, tables, colour = end, tables[::-1], a + b - colour
        for (first, second), colour in path:
            del sends[first][colour], takes[second][colour]
        for (first, second), colour in path:
            sends[first][a + b - colour], takes[second][a + b - colour] = second, first
        sends[of][a], takes[to][a] = to, of
    return [
        [(of, to[c]) for of, to in enumerate(sends) if c in to]
        for c in range(max((c + 1 for to in sends for c in to), default=0))
    ]


def unit_kernel(pads, order_smem, order, embeddings, unit, value, result, tile, into, out, sem):
    rows = unit.shape[0]
    count = rows // into.shape[0]
    parts = [pl.ds(start, count) for start in range(0, rows, count)]
    loads = [
        pltpu.make_async_copy(embeddings.at[part], value.at[part], into.at[index])
        for index, part in enumerate(parts)
    ]
    stores = [
        pltpu.make_async_copy(result.at[part], unit.at[part], out.at[index])
        for index, part in enumerate(parts)
    ]
    first = order_smem[0]
    base = pl.multiple_of((first // 16) * 16, 16)
    filling = pltpu.make_async_copy(embeddings.at[pl.ds(base, 16)], tile, sem)
    filling.start()
    for load in loads:
        load.start()
    filling.wait()
    among = lax.broadcasted_iota(jnp.int32, (16, 1), 0) == first - base
    filler = jnp.sum(jnp.where(among, tile[...].astype(jnp.float32), 0.0), axis=0, keepdims=True)
    for index, part in enumerate(parts):
        found = valid_rows(pads, order, index * count, count)
        loads[index].wait()
        chunk = jnp.where(found, value[part, :].astype(jnp.float32), filler)
        scale = lax.rsqrt(jnp.sum(chunk * chunk, axis=1, keepdims=True) + 1e-06)
        result[part, :] = (chunk * scale).astype(jnp.bfloat16)
        stores[index].start()
    for store in stores:
        store.wait()


def valid_rows(pads, order, start, count):
    rows = order.shape[1]
    most = min(rows, MOST_PADS)
    valid_count = rows - pads[lax.axis_index("blk")]
    position = rows - most + lax.broadcasted_iota(jnp.int32, (1, most), 1)
    padding = jnp.where(position < valid_count, -1, order[:, rows - most :])
    row = start + lax.broadcasted_iota(jnp.int32, (count, 1), 0)
    return jnp.max(jnp.where(padding == row, 1.0, 0.0), axis=1, keepdims=True) < 1.0


def normalized(embeddings, order, pad_counts):
    rows, depth = embeddings.shape
    chunks = 4
    scalars = pl.BlockSpec(memory_space=pltpu.SMEM)
    return pl.pallas_call(
        unit_kernel,
        out_shape=jax.ShapeDtypeStruct((rows, depth), jnp.bfloat16),
        in_specs=[
            scalars,
            scalars,
            pl.BlockSpec(memory_space=pltpu.VMEM),
            pl.BlockSpec(memory_space=pl.ANY),
        ],
        out_specs=pl.BlockSpec(memory_space=pl.ANY),
        scratch_shapes=[
            pltpu.VMEM((rows, depth), jnp.bfloat16),
            pltpu.VMEM((rows, depth), jnp.bfloat16),
            pltpu.VMEM((16, depth), jnp.bfloat16),
            pltpu.SemaphoreType.DMA((chunks,)),
            pltpu.SemaphoreType.DMA((chunks,)),
            pltpu.SemaphoreType.DMA,
        ],
        compiler_params=pltpu.CompilerParams(vmem_limit_bytes=VMEM),
        cost_estimate=pl.CostEstimate(
            flops=4 * rows * depth, bytes_accessed=4 * rows * depth, transcendentals=rows
        ),
        name="normalized",
    )(pad_counts, order, order.reshape(1, rows), embeddings)


def product(left, right):
    return lax.dot_general(left, right, (((1,), (1,)), ((), ())), preferred_element_type=jnp.float32)


def own_kernel(pads, order, unit, best):
    rows = unit.shape[0]
    best[...] = jnp.full(best.shape, FLOOR, jnp.float32)
    valid = valid_rows(pads, order, 0, rows)
    row = lax.broadcasted_iota(jnp.int32, (rows, 1), 0)
    here = pl.ds(lax.axis_index("blk"), 1)
    for start in range(0, rows, 256):
        part = pl.ds(start, 256)
        scores = product(unit[...], unit[part, :])
        column = start + lax.broadcasted_iota(jnp.int32, (1, 256), 1)
        scores = jnp.where(valid & (row != column), scores, FLOOR)
        best[here, part] = jnp.max(scores, axis=0, keepdims=True)


def own_block(unit, order, pad_counts, nblocks):
    rows, depth = unit.shape
    whole = pl.BlockSpec(memory_space=pltpu.VMEM)
    return pl.pallas_call(
        own_kernel,
        out_shape=jax.ShapeDtypeStruct((nblocks, rows), jnp.float32),
        in_specs=[pl.BlockSpec(memory_space=pltpu.SMEM), whole, whole],
        out_specs=whole,
        compiler_params=pltpu.CompilerParams(vmem_limit_bytes=VMEM),
        cost_estimate=pl.CostEstimate(
            flops=2 * rows * rows * depth, bytes_accessed=2 * rows * depth, transcendentals=0
        ),
        name="own_block",
    )(pad_counts, order.reshape(1, rows), unit)


def pairs_kernel(nslots, nrows, ntaken, nloads, npairs, table, best, *refs):
    arrivals, slots, out = refs[:ntaken], refs[ntaken : ntaken + nslots], refs[ntaken + nslots]
    sent, (held, across, sems) = refs[ntaken + nslots + 1 : -3], refs[-3:]
    rows = out.shape[1]
    here = lax.axis_index("blk")
    loads_at = here * (2 + nrows + ntaken + nloads + 5 * npairs) + 2 + nrows + ntaken
    pairs_at = loads_at + nloads
    rows_at = loads_at - nrows - ntaken
    loads, pairs = table[rows_at - 2], table[rows_at - 1]

    def fetch(load):
        @pl.when(load < loads)
        def _():
            wanted = table[loads_at + jnp.minimum(load, nloads - 1)]
            for index, slot in enumerate(slots):
                @pl.when(wanted == index)
                def _(slot=slot):
                    for start in range(0, rows, 256):
                        part = pl.ds(start, 256)
                        pltpu.make_async_copy(slot.at[part], held.at[load, part], sems.at[load]).start()

    for load in range(min(AHEAD, nloads)):
        fetch(load)
    out[...] = best[...]
    own = pl.ds(here, 1)
    for index, row in enumerate(arrivals):
        handed = table[rows_at + nrows + index] > 0
        out[own, :] = jnp.where(handed, jnp.maximum(out[own, :], row[...]), out[own, :])

    @pl.loop(0, pairs)
    def _(step):
        at = pairs_at + 5 * step
        before = jnp.where(step == 0, 0, table[jnp.maximum(at - 1, 0)])

        @pl.loop(before, table[at + 4])
        def _(load):
            pltpu.make_async_copy(slots[0], held.at[load], sems.at[load]).wait()
            fetch(load + AHEAD)

        left, right = table[at], table[at + 1]
        first, second = pl.ds(table[at + 2], 1), pl.ds(table[at + 3], 1)
        for start in range(0, rows, 256):
            part = pl.ds(start, 256)
            scores = product(held[left], held[right, part, :])
            down = jnp.max(scores, axis=0, keepdims=True)
            out[second, part] = jnp.maximum(out[second, part], down)
            along = jnp.maximum(scores[:, :128], scores[:, 128:])
            across[...] = along if start == 0 else jnp.maximum(across[...], along)
        found = jnp.max(across[...].T, axis=0, keepdims=True)
        out[first, :] = jnp.maximum(out[first, :], found)

    for index, row in enumerate(sent):
        row[...] = out[pl.ds(table[rows_at + index], 1), :]


def in_order_of_loads(pairs, rank):
    left, loaded, ordered = list(pairs), [], []
    while left:
        pair = min(
            left,
            key=lambda p: (sum(s not in loaded for s in p[:2]), max(rank[s] for s in p[:2]), p[2:]),
        )
        left.remove(pair)
        loaded += [slot for slot in pair[:2] if slot not in loaded]
        ordered.append((pair, len(loaded)))
    return loaded, ordered


def scored(best, found, permutes, slots, rank, work, sends):
    names = sorted({slot for pairs in work for pair in pairs for slot in pair[:2]})
    plans = [in_order_of_loads(pairs, rank) for pairs in work]
    nloads = max(len(loaded) for loaded, _ in plans)
    npairs = max(len(pairs) for pairs in work)
    table = []
    for device, (loaded, ordered) in enumerate(plans):
        table += [len(loaded), len(ordered)]
        table += [dict(permute).get(device, device) for permute in sends]
        table += [int(device in dict(permute).values()) for permute in permutes]
        table += [names.index(slot) for slot in loaded] + [0] * (nloads - len(loaded))
        for (slot, other, block, visitor), need in ordered:
            table += [loaded.index(slot), loaded.index(other), block, visitor, need]
        table += [0] * (5 * (npairs - len(ordered)))
    given = [slots[name] for name in names]
    rows, depth = given[0].shape
    whole = pl.BlockSpec(memory_space=pltpu.VMEM)
    return pl.pallas_call(
        functools.partial(pairs_kernel, len(given), len(sends), len(found), nloads, npairs),
        out_shape=[jax.ShapeDtypeStruct(best.shape, jnp.float32)]
        + [jax.ShapeDtypeStruct((1, rows), jnp.float32)] * len(sends),
        in_specs=[pl.BlockSpec(memory_space=pltpu.SMEM)]
        + [whole] * (1 + len(found))
        + [pl.BlockSpec(memory_space=pl.ANY)] * len(given),
        out_specs=[whole] * (1 + len(sends)),
        scratch_shapes=[
            pltpu.VMEM((nloads, rows, depth), jnp.bfloat16),
            pltpu.VMEM((rows, 128), jnp.float32),
            pltpu.SemaphoreType.DMA((nloads,)),
        ],
        compiler_params=pltpu.CompilerParams(vmem_limit_bytes=VMEM),
        cost_estimate=pl.CostEstimate(
            flops=2 * npairs * rows * rows * depth,
            bytes_accessed=2 * nloads * rows * depth,
            transcendentals=0,
        ),
        name="scored",
    )(jnp.asarray(np.array(table, np.int32)), best, *found, *given)


def placed_kernel(taken, pads, order, best, *refs):
    found, out = refs[:-1], refs[-1]
    rows = order.shape[1]
    here = lax.axis_index("blk")
    total = best[pl.ds(here, 1), :]
    for index, row in enumerate(found):
        total = jnp.where(taken[here * len(found) + index] > 0, jnp.maximum(total, row[...]), total)
    column = jnp.broadcast_to(total, (128, rows)).T[:, :1]
    row = lax.broadcasted_iota(jnp.int32, (rows, 1), 0)
    in_order = jnp.max(jnp.where(order[...] == row, column, FLOOR), axis=0, keepdims=True)
    position = lax.broadcasted_iota(jnp.int32, (1, rows), 1)
    out[...] = jnp.where(position < rows - pads[here], in_order, 0.0)


def placed(best, found, permutes, order, pad_counts):
    rows = order.shape[0]
    taken = np.zeros((best.shape[0], len(permutes)), np.int32)
    for index, permute in enumerate(permutes):
        taken[[to for _, to in permute], index] = 1
    whole, scalars = pl.BlockSpec(memory_space=pltpu.VMEM), pl.BlockSpec(memory_space=pltpu.SMEM)
    return pl.pallas_call(
        placed_kernel,
        out_shape=jax.ShapeDtypeStruct((1, rows), jnp.float32),
        in_specs=[scalars, scalars] + [whole] * (2 + len(found)),
        out_specs=whole,
        compiler_params=pltpu.CompilerParams(vmem_limit_bytes=VMEM),
        name="placed",
    )(jnp.asarray(taken.reshape(-1)), pad_counts, order.reshape(1, rows), best, *found).reshape(rows)


def local(embeddings, order, pad_counts):
    nblocks = lax.axis_size("blk")
    moves, work, sending = planned(nblocks)
    unit = normalized(embeddings, order, pad_counts)
    slots, best = {"own": unit}, None
    rank = dict({"own": -1}, **{move.name: move.stage for move in moves})
    touched, permutes, found = [set() for _ in range(nblocks)], [], []
    for stage, pairs in enumerate(work):
        starting = [move for move in moves if move.begins == stage]
        for needs in sorted({move.needs for move in starting}):
            values = [slots[name] for name in needs]
            if best is not None:
                *values, best = lax.optimization_barrier((*values, best))
            for move in starting:
                if move.needs == needs:
                    value = values[needs.index(move.source)]
                    slots[move.name] = lax.ppermute(value, "blk", move.pairs)
        if stage == 0:
            best = own_block(unit, order, pad_counts, nblocks)
        for device, mine in enumerate(pairs):
            touched[device] |= {block for pair in mine for block in pair[2:] if block != device}
        sends = []
        if stage in sending:
            sends = colored([(of, to) for of in range(nblocks) for to in sorted(touched[of])], nblocks)
            touched = [set() for _ in range(nblocks)]
        if any(pairs):
            best, *rows = scored(best, found, permutes, slots, rank, pairs, sends)
            found = [lax.ppermute(row, "blk", permute) for row, permute in zip(rows, sends)]
            permutes = sends
    return placed(best, found, permutes, order, pad_counts)


def solution(mesh):
    in_specs = (P(("groups", "blk"), None), P(("groups", "blk")), P("groups"))
    out_specs = P(("groups", "blk"))
    return jax.shard_map(local, mesh=mesh, in_specs=in_specs, out_specs=out_specs, check_vma=False)
```

```python
import functools

import jax
import jax.numpy as jnp
import numpy as np
from jax import lax
from jax.experimental import pallas as pl
from jax.experimental.pallas import tpu as pltpu
from jax.sharding import PartitionSpec as P

STEPS = 6
VMEM = 62 * 2**20
FLOOR = -2.0
MOST_PADS = 256
AHEAD = 3


class Move:
    def __init__(self, name, source, pairs, begins, stage, *after):
        self.name, self.source, self.pairs = name, source, pairs
        self.begins, self.stage, self.needs = begins, stage, (source, *after)


def grid_moves():
    def at(z, y, lane):
        return 4 * z + 2 * y + (y if lane == 0 else 1 - y)

    def rows(links):
        return [
            (at(z, y, lane), at(to, y, land)) for y in (0, 1) for (z, lane), (to, land) in links
        ]

    def across(planes):
        return [(at(z, y, lane), at(z, 1 - y, lane)) for z, lane in planes for y in (0, 1)]

    every = [(z, lane) for z in range(4) for lane in (0, 1)]
    swap = rows([((z, lane), (z, 1 - lane)) for z, lane in every])
    first = [((0, 0), (2, 0)), ((2, 0), (3, 0)), ((3, 0), (1, 0)), ((1, 0), (0, 0)), ((0, 1), (1, 1))]
    second = [((3, 1), (1, 1)), ((1, 1), (0, 1)), ((2, 1), (3, 1)), ((1, 0), (2, 1))]
    return [
        Move("R1", "own", rows(first), 0, 1),
        Move("R2", "own", rows(second), 0, 1),
        Move("Y", "own", across(every), 0, 1),
        Move("A", "own", swap, 0, 0),
        Move("R3", "own", rows([((1, 1), (2, 0)), ((2, 0), (1, 1))]), 1, 2, "R1"),
        Move("V", "R1", rows([((2, 0), (3, 0))]) + across([(1, 1)]), 1, 2),
        Move("F", "Y", swap, 1, 1),
        Move("W", "R1", rows([((1, 0), (1, 1)), ((1, 1), (1, 0))]), 1, 1),
    ]


GRID_PAIRS = (
    ((0, 1), (0, 4), (1, 3), (1, 4), (3, 4)),
    ((0, 5), (1, 2), (2, 5), (3, 5)),
    ((0, 6), (1, 6), (2, 6), (3, 6)),
    ((0, 2), (0, 3), (1, 7), (2, 3), (2, 7), (3, 7)),
    ((4, 5), (4, 7), (5, 6), (6, 12), (7, 12)),
    ((1, 5), (1, 12), (1, 13), (2, 8), (2, 12), (2, 13), (7, 13), (8, 12)),
    ((1, 11), (1, 14), (1, 15), (2, 4), (2, 14), (4, 6), (4, 14), (11, 14)),
    ((2, 15), (4, 15), (5, 7), (5, 15), (6, 7)),
    ((0, 10), (0, 11), (5, 8), (5, 9), (5, 10), (5, 11), (8, 11)),
    ((4, 8), (4, 9), (4, 10), (8, 9), (9, 11)),
    ((7, 8), (7, 9), (7, 10), (7, 11)),
    ((3, 8), (3, 9), (6, 8), (6, 9), (6, 10), (6, 11), (8, 10), (9, 10), (10, 11)),
    ((0, 12), (0, 13), (0, 14), (0, 15), (8, 13), (8, 14), (12, 15), (13, 14)),
    ((9, 12), (9, 13), (9, 14), (9, 15), (12, 13)),
    ((10, 12), (10, 13), (10, 14), (10, 15), (12, 14), (14, 15)),
    ((3, 13), (3, 14), (3, 15), (11, 12), (11, 13), (11, 15), (13, 15)),
)


def ring_moves(count):
    return [
        Move("N%d" % k, "own", [((i + k) % count, i) for i in range(count)], 0, k)
        for k in range(1, STEPS + 1)
    ]


def planned(count):
    if count == 16:
        moves, placed_pairs, sending = grid_moves(), GRID_PAIRS, (1, 2)
    else:
        moves, sending = ring_moves(count), (STEPS,)
        placed_pairs = [[(b, (b + k) % count) for k in range(1, STEPS + 1)] for b in range(count)]
    holds = {"own": {d: d for d in range(count)}}
    stage_of = {"own": 0}
    for move in moves:
        holds[move.name] = {to: holds[move.source][of] for of, to in move.pairs}
        stage_of[move.name] = move.stage
    stages = 1 + max(stage_of.values())
    work = [[[] for _ in range(count)] for _ in range(stages)]
    for device, pairs in enumerate(placed_pairs):
        slot_of = {}
        for slot in sorted(stage_of, key=stage_of.get):
            if device in holds[slot]:
                slot_of.setdefault(holds[slot][device], slot)
        for block, visitor in pairs:
            slot, other = slot_of[block], slot_of[visitor]
            stage = max(stage_of[slot], stage_of[other])
            work[stage][device].append((slot, other, block, visitor))
    scored_pairs = sorted(tuple(sorted(pair)) for pairs in placed_pairs for pair in pairs)
    needed = {tuple(sorted((b, (b + k) % count))) for b in range(count) for k in range(1, STEPS + 1)}
    assert scored_pairs == sorted(needed)
    return moves, work, sending


def colored(edges, count):
    sends, takes = [{} for _ in range(count)], [{} for _ in range(count)]
    for of, to in edges:
        a = next(c for c in range(len(edges)) if c not in sends[of])
        b = next(c for c in range(len(edges)) if c not in takes[to])
        path, node, tables, colour = [], to, (takes, sends), a
        while a != b and colour in tables[0][node]:
            end = tables[0][node][colour]
            path.append(((end, node) if tables[0] is takes else (node, end), colour))
            node, tables, colour = end, tables[::-1], a + b - colour
        for (first, second), colour in path:
            del sends[first][colour], takes[second][colour]
        for (first, second), colour in path:
            sends[first][a + b - colour], takes[second][a + b - colour] = second, first
        sends[of][a], takes[to][a] = to, of
    return [
        [(of, to[c]) for of, to in enumerate(sends) if c in to]
        for c in range(max((c + 1 for to in sends for c in to), default=0))
    ]


def in_two(early, late, count):
    early, late = set(early) - set(late), set(late)

    def degrees(edges):
        return [
            [sum(edge[side] == device for edge in edges) for device in range(count)] for side in (0, 1)
        ]

    most = max(degrees(late)[0] + degrees(late)[1])
    while early:
        busy, taken = degrees(early), degrees(late)
        top = max(busy[0] + busy[1])
        free = [
            (max(busy[0][of], busy[1][to]), busy[0][of] + busy[1][to], of, to)
            for of, to in sorted(early)
            if max(taken[0][of], taken[1][to]) < most and max(busy[0][of], busy[1][to]) == top
        ]
        if not free:
            break
        early.remove(max(free)[2:])
        late.add(max(free)[2:])
    return sorted(early), sorted(late)


def unit_kernel(pads, order_smem, order, embeddings, unit, value, result, tile, into, out, sem):
    rows = unit.shape[0]
    count = rows // into.shape[0]
    parts = [pl.ds(start, count) for start in range(0, rows, count)]
    loads = [
        pltpu.make_async_copy(embeddings.at[part], value.at[part], into.at[index])
        for index, part in enumerate(parts)
    ]
    stores = [
        pltpu.make_async_copy(result.at[part], unit.at[part], out.at[index])
        for index, part in enumerate(parts)
    ]
    first = order_smem[0]
    base = pl.multiple_of((first // 16) * 16, 16)
    filling = pltpu.make_async_copy(embeddings.at[pl.ds(base, 16)], tile, sem)
    filling.start()
    for load in loads:
        load.start()
    filling.wait()
    among = lax.broadcasted_iota(jnp.int32, (16, 1), 0) == first - base
    filler = jnp.sum(jnp.where(among, tile[...].astype(jnp.float32), 0.0), axis=0, keepdims=True)
    for index, part in enumerate(parts):
        found = valid_rows(pads, order, index * count, count)
        loads[index].wait()
        chunk = jnp.where(found, value[part, :].astype(jnp.float32), filler)
        scale = lax.rsqrt(jnp.sum(chunk * chunk, axis=1, keepdims=True) + 1e-06)
        result[part, :] = (chunk * scale).astype(jnp.bfloat16)
        stores[index].start()
    for store in stores:
        store.wait()


def valid_rows(pads, order, start, count):
    rows = order.shape[1]
    most = min(rows, MOST_PADS)
    valid_count = rows - pads[lax.axis_index("blk")]
    position = rows - most + lax.broadcasted_iota(jnp.int32, (1, most), 1)
    padding = jnp.where(position < valid_count, -1, order[:, rows - most :])
    row = start + lax.broadcasted_iota(jnp.int32, (count, 1), 0)
    return jnp.max(jnp.where(padding == row, 1.0, 0.0), axis=1, keepdims=True) < 1.0


def normalized(embeddings, order, pad_counts):
    rows, depth = embeddings.shape
    chunks = 4
    scalars = pl.BlockSpec(memory_space=pltpu.SMEM)
    return pl.pallas_call(
        unit_kernel,
        out_shape=jax.ShapeDtypeStruct((rows, depth), jnp.bfloat16),
        in_specs=[
            scalars,
            scalars,
            pl.BlockSpec(memory_space=pltpu.VMEM),
            pl.BlockSpec(memory_space=pl.ANY),
        ],
        out_specs=pl.BlockSpec(memory_space=pl.ANY),
        scratch_shapes=[
            pltpu.VMEM((rows, depth), jnp.bfloat16),
            pltpu.VMEM((rows, depth), jnp.bfloat16),
            pltpu.VMEM((16, depth), jnp.bfloat16),
            pltpu.SemaphoreType.DMA((chunks,)),
            pltpu.SemaphoreType.DMA((chunks,)),
            pltpu.SemaphoreType.DMA,
        ],
        compiler_params=pltpu.CompilerParams(vmem_limit_bytes=VMEM),
        cost_estimate=pl.CostEstimate(
            flops=4 * rows * depth, bytes_accessed=4 * rows * depth, transcendentals=rows
        ),
        name="normalized",
    )(pad_counts, order, order.reshape(1, rows), embeddings)


def product(left, right):
    return lax.dot_general(left, right, (((1,), (1,)), ((), ())), preferred_element_type=jnp.float32)


def own_kernel(pads, order, unit, best):
    rows = unit.shape[0]
    best[...] = jnp.full(best.shape, FLOOR, jnp.float32)
    valid = valid_rows(pads, order, 0, rows)
    row = lax.broadcasted_iota(jnp.int32, (rows, 1), 0)
    here = pl.ds(lax.axis_index("blk"), 1)
    for start in range(0, rows, 256):
        part = pl.ds(start, 256)
        scores = product(unit[...], unit[part, :])
        column = start + lax.broadcasted_iota(jnp.int32, (1, 256), 1)
        scores = jnp.where(valid & (row != column), scores, FLOOR)
        best[here, part] = jnp.max(scores, axis=0, keepdims=True)


def own_block(unit, order, pad_counts, nblocks):
    rows, depth = unit.shape
    whole = pl.BlockSpec(memory_space=pltpu.VMEM)
    return pl.pallas_call(
        own_kernel,
        out_shape=jax.ShapeDtypeStruct((nblocks, rows), jnp.float32),
        in_specs=[pl.BlockSpec(memory_space=pltpu.SMEM), whole, whole],
        out_specs=whole,
        compiler_params=pltpu.CompilerParams(vmem_limit_bytes=VMEM),
        cost_estimate=pl.CostEstimate(
            flops=2 * rows * rows * depth, bytes_accessed=2 * rows * depth, transcendentals=0
        ),
        name="own_block",
    )(pad_counts, order.reshape(1, rows), unit)


def pairs_kernel(nslots, nrows, ntaken, nloads, npairs, table, best, *refs):
    arrivals, slots, out = refs[:ntaken], refs[ntaken : ntaken + nslots], refs[ntaken + nslots]
    sent, (held, across, sems) = refs[ntaken + nslots + 1 : -3], refs[-3:]
    rows = out.shape[1]
    here = lax.axis_index("blk")
    loads_at = here * (2 + nrows + ntaken + nloads + 5 * npairs) + 2 + nrows + ntaken
    pairs_at = loads_at + nloads
    rows_at = loads_at - nrows - ntaken
    loads, pairs = table[rows_at - 2], table[rows_at - 1]

    def fetch(load):
        @pl.when(load < loads)
        def _():
            wanted = table[loads_at + jnp.minimum(load, nloads - 1)]
            for index, slot in enumerate(slots):
                @pl.when(wanted == index)
                def _(slot=slot):
                    for start in range(0, rows, 256):
                        part = pl.ds(start, 256)
                        pltpu.make_async_copy(slot.at[part], held.at[load, part], sems.at[load]).start()

    for load in range(min(AHEAD, nloads)):
        fetch(load)
    out[...] = best[...]
    own = pl.ds(here, 1)
    for index, row in enumerate(arrivals):
        handed = table[rows_at + nrows + index] > 0
        out[own, :] = jnp.where(handed, jnp.maximum(out[own, :], row[...]), out[own, :])

    @pl.loop(0, pairs)
    def _(step):
        at = pairs_at + 5 * step
        before = jnp.where(step == 0, 0, table[jnp.maximum(at - 1, 0)])

        @pl.loop(before, table[at + 4])
        def _(load):
            pltpu.make_async_copy(slots[0], held.at[load], sems.at[load]).wait()
            fetch(load + AHEAD)

        left, right = table[at], table[at + 1]
        first, second = pl.ds(table[at + 2], 1), pl.ds(table[at + 3], 1)
        for start in range(0, rows, 256):
            part = pl.ds(start, 256)
            scores = product(held[left], held[right, part, :])
            down = jnp.max(scores, axis=0, keepdims=True)
            out[second, part] = jnp.maximum(out[second, part], down)
            along = jnp.maximum(scores[:, :128], scores[:, 128:])
            across[...] = along if start == 0 else jnp.maximum(across[...], along)
        found = jnp.max(across[...].T, axis=0, keepdims=True)
        out[first, :] = jnp.maximum(out[first, :], found)

    for index, row in enumerate(sent):
        row[...] = out[pl.ds(table[rows_at + index], 1), :]


def in_order_of_loads(pairs, rank):
    left, loaded, ordered = list(pairs), [], []
    while left:
        pair = min(
            left,
            key=lambda p: (sum(s not in loaded for s in p[:2]), max(rank[s] for s in p[:2]), p[2:]),
        )
        left.remove(pair)
        loaded += [slot for slot in pair[:2] if slot not in loaded]
        ordered.append((pair, len(loaded)))
    return loaded, ordered


def scored(best, found, permutes, slots, rank, work, sends):
    names = sorted({slot for pairs in work for pair in pairs for slot in pair[:2]})
    plans = [in_order_of_loads(pairs, rank) for pairs in work]
    nloads = max(len(loaded) for loaded, _ in plans)
    npairs = max(len(pairs) for pairs in work)
    table = []
    for device, (loaded, ordered) in enumerate(plans):
        table += [len(loaded), len(ordered)]
        table += [dict(permute).get(device, device) for permute in sends]
        table += [int(device in dict(permute).values()) for permute in permutes]
        table += [names.index(slot) for slot in loaded] + [0] * (nloads - len(loaded))
        for (slot, other, block, visitor), need in ordered:
            table += [loaded.index(slot), loaded.index(other), block, visitor, need]
        table += [0] * (5 * (npairs - len(ordered)))
    given = [slots[name] for name in names]
    rows, depth = given[0].shape
    whole = pl.BlockSpec(memory_space=pltpu.VMEM)
    return pl.pallas_call(
        functools.partial(pairs_kernel, len(given), len(sends), len(found), nloads, npairs),
        out_shape=[jax.ShapeDtypeStruct(best.shape, jnp.float32)]
        + [jax.ShapeDtypeStruct((1, rows), jnp.float32)] * len(sends),
        in_specs=[pl.BlockSpec(memory_space=pltpu.SMEM)]
        + [whole] * (1 + len(found))
        + [pl.BlockSpec(memory_space=pl.ANY)] * len(given),
        out_specs=[whole] * (1 + len(sends)),
        scratch_shapes=[
            pltpu.VMEM((nloads, rows, depth), jnp.bfloat16),
            pltpu.VMEM((rows, 128), jnp.float32),
            pltpu.SemaphoreType.DMA((nloads,)),
        ],
        compiler_params=pltpu.CompilerParams(vmem_limit_bytes=VMEM),
        cost_estimate=pl.CostEstimate(
            flops=2 * npairs * rows * rows * depth,
            bytes_accessed=2 * nloads * rows * depth,
            transcendentals=0,
        ),
        name="scored",
    )(jnp.asarray(np.array(table, np.int32)), best, *found, *given)


def placed_kernel(taken, pads, order, best, *refs):
    found, out = refs[:-1], refs[-1]
    rows = order.shape[1]
    here = lax.axis_index("blk")
    total = best[pl.ds(here, 1), :]
    for index, row in enumerate(found):
        total = jnp.where(taken[here * len(found) + index] > 0, jnp.maximum(total, row[...]), total)
    column = jnp.broadcast_to(total, (128, rows)).T[:, :1]
    row = lax.broadcasted_iota(jnp.int32, (rows, 1), 0)
    in_order = jnp.max(jnp.where(order[...] == row, column, FLOOR), axis=0, keepdims=True)
    position = lax.broadcasted_iota(jnp.int32, (1, rows), 1)
    out[...] = jnp.where(position < rows - pads[here], in_order, 0.0)


def placed(best, found, permutes, order, pad_counts):
    rows = order.shape[0]
    taken = np.zeros((best.shape[0], len(permutes)), np.int32)
    for index, permute in enumerate(permutes):
        taken[[to for _, to in permute], index] = 1
    whole, scalars = pl.BlockSpec(memory_space=pltpu.VMEM), pl.BlockSpec(memory_space=pltpu.SMEM)
    return pl.pallas_call(
        placed_kernel,
        out_shape=jax.ShapeDtypeStruct((1, rows), jnp.float32),
        in_specs=[scalars, scalars] + [whole] * (2 + len(found)),
        out_specs=whole,
        compiler_params=pltpu.CompilerParams(vmem_limit_bytes=VMEM),
        name="placed",
    )(jnp.asarray(taken.reshape(-1)), pad_counts, order.reshape(1, rows), best, *found).reshape(rows)


def local(embeddings, order, pad_counts):
    nblocks = lax.axis_size("blk")
    moves, work, sending = planned(nblocks)
    unit = normalized(embeddings, order, pad_counts)
    slots, best = {"own": unit}, None
    rank = dict({"own": -1}, **{move.name: move.stage for move in moves})
    edges = [
        {(of, to) for of in range(nblocks) for pair in pairs[of] for to in pair[2:] if to != of}
        for pairs in work
    ]
    edges = {sending[-1]: set().union(*edges[sending[0] + 1 :] if len(sending) > 1 else edges),
             sending[0]: set().union(*edges[: sending[0] + 1])}
    if len(sending) > 1:
        edges = dict(zip(sending, in_two(edges[sending[0]], edges[sending[1]], nblocks)))
    permutes, found = [], []
    for stage, pairs in enumerate(work):
        starting = [move for move in moves if move.begins == stage]
        for needs in sorted({move.needs for move in starting}):
            values = [slots[name] for name in needs]
            if best is not None:
                *values, best = lax.optimization_barrier((*values, best))
            for move in starting:
                if move.needs == needs:
                    value = values[needs.index(move.source)]
                    slots[move.name] = lax.ppermute(value, "blk", move.pairs)
        if stage == 0:
            best = own_block(unit, order, pad_counts, nblocks)
        sends = colored(sorted(edges[stage]), nblocks) if stage in sending else []
        if any(pairs):
            best, *rows = scored(best, found, permutes, slots, rank, pairs, sends)
            found = [lax.ppermute(row, "blk", permute) for row, permute in zip(rows, sends)]
            permutes = sends
    return placed(best, found, permutes, order, pad_counts)


def solution(mesh):
    in_specs = (P(("groups", "blk"), None), P(("groups", "blk")), P("groups"))
    out_specs = P(("groups", "blk"))
    return jax.shard_map(local, mesh=mesh, in_specs=in_specs, out_specs=out_specs, check_vma=False)
```

```python
import functools

import jax
import jax.numpy as jnp
import numpy as np
from jax import lax
from jax.experimental import pallas as pl
from jax.experimental.pallas import tpu as pltpu
from jax.sharding import PartitionSpec as P

STEPS = 6
VMEM = 62 * 2**20
FLOOR = -2.0
MOST_PADS = 256
AHEAD = 3


class Move:
    def __init__(self, name, source, pairs, begins, stage, *after):
        self.name, self.source, self.pairs = name, source, pairs
        self.begins, self.stage, self.needs = begins, stage, (source, *after)


def grid_moves():
    def at(z, y, lane):
        return 4 * z + 2 * y + (y if lane == 0 else 1 - y)

    def rows(links):
        return [
            (at(z, y, lane), at(to, y, land)) for y in (0, 1) for (z, lane), (to, land) in links
        ]

    def across(planes):
        return [(at(z, y, lane), at(z, 1 - y, lane)) for z, lane in planes for y in (0, 1)]

    every = [(z, lane) for z in range(4) for lane in (0, 1)]
    swap = rows([((z, lane), (z, 1 - lane)) for z, lane in every])
    crossed = [(at(1, y, lane), at(1, 1 - y, 1 - lane)) for y in (0, 1) for lane in (0, 1)]
    first = [((0, 0), (2, 1)), ((2, 0), (3, 1)), ((3, 0), (1, 0)), ((1, 0), (0, 0)), ((0, 1), (1, 1))]
    second = [((3, 1), (1, 1)), ((1, 1), (0, 1)), ((2, 1), (3, 0)), ((1, 0), (2, 1))]
    return [
        Move("R1", "own", rows(first), 0, 1),
        Move("R2", "own", rows(second), 0, 1),
        Move("Y", "own", across([place for place in every if place[0] != 1]) + crossed, 0, 1),
        Move("A", "own", swap, 0, 0),
        Move("R3", "own", rows([((1, 1), (2, 0)), ((2, 0), (1, 1))]), 1, 2, "R1"),
        Move("V", "R1", [(at(2, y, 1), at(3, y, 1 - y)) for y in (0, 1)] + across([(1, 1)]), 1, 2),
        Move("F", "Y", swap, 2, 2),
        Move("W", "R1", rows([((1, 0), (1, 1)), ((1, 1), (1, 0))]), 2, 2),
    ]


GRID_PAIRS = (
    ((0, 2), (0, 4), (1, 4), (2, 4), (3, 4)),
    ((0, 1), (0, 5), (1, 3), (1, 5), (3, 5)),
    ((0, 3), (0, 6), (1, 6), (2, 3), (2, 6), (3, 6)),
    ((1, 2), (1, 7), (2, 7), (3, 7)),
    ((1, 12), (4, 5), (4, 6), (4, 7), (6, 12), (7, 12)),
    ((1, 13), (2, 8), (2, 12), (2, 13), (5, 8), (7, 13)),
    ((1, 11), (1, 14), (1, 15), (2, 14), (4, 14)),
    ((2, 5), (2, 15), (4, 15), (5, 6), (5, 7), (5, 15), (6, 7)),
    ((5, 9), (5, 10), (5, 11), (9, 10), (9, 11)),
    ((0, 10), (0, 11), (4, 8), (4, 9), (4, 10), (8, 9), (8, 11)),
    ((3, 8), (3, 9), (7, 8), (7, 9), (7, 10), (7, 11)),
    ((6, 8), (6, 9), (6, 10), (6, 11), (8, 10), (10, 11)),
    ((9, 12), (9, 13), (9, 14), (9, 15), (12, 13), (12, 14), (13, 14), (13, 15)),
    ((0, 12), (0, 13), (0, 14), (0, 15), (8, 12), (8, 13), (8, 14)),
    ((11, 12), (11, 13), (11, 14), (11, 15), (12, 15)),
    ((3, 13), (3, 14), (3, 15), (10, 12), (10, 13), (10, 14), (10, 15), (14, 15)),
)


def ring_moves(count):
    return [
        Move("N%d" % k, "own", [((i + k) % count, i) for i in range(count)], 0, k)
        for k in range(1, STEPS + 1)
    ]


def planned(count):
    if count == 16:
        moves, placed_pairs, sending = grid_moves(), GRID_PAIRS, (1, 2)
    else:
        moves, sending = ring_moves(count), (STEPS,)
        placed_pairs = [[(b, (b + k) % count) for k in range(1, STEPS + 1)] for b in range(count)]
    holds = {"own": {d: d for d in range(count)}}
    stage_of = {"own": 0}
    for move in moves:
        holds[move.name] = {to: holds[move.source][of] for of, to in move.pairs}
        stage_of[move.name] = move.stage
    stages = 1 + max(stage_of.values())
    work = [[[] for _ in range(count)] for _ in range(stages)]
    for device, pairs in enumerate(placed_pairs):
        slot_of = {}
        for slot in sorted(stage_of, key=stage_of.get):
            if device in holds[slot]:
                slot_of.setdefault(holds[slot][device], slot)
        for block, visitor in pairs:
            slot, other = slot_of[block], slot_of[visitor]
            stage = max(stage_of[slot], stage_of[other])
            work[stage][device].append((slot, other, block, visitor))
    scored_pairs = sorted(tuple(sorted(pair)) for pairs in placed_pairs for pair in pairs)
    needed = {tuple(sorted((b, (b + k) % count))) for b in range(count) for k in range(1, STEPS + 1)}
    assert scored_pairs == sorted(needed)
    return moves, work, sending


def colored(edges, count):
    sends, takes = [{} for _ in range(count)], [{} for _ in range(count)]
    for of, to in edges:
        a = next(c for c in range(len(edges)) if c not in sends[of])
        b = next(c for c in range(len(edges)) if c not in takes[to])
        path, node, tables, colour = [], to, (takes, sends), a
        while a != b and colour in tables[0][node]:
            end = tables[0][node][colour]
            path.append(((end, node) if tables[0] is takes else (node, end), colour))
            node, tables, colour = end, tables[::-1], a + b - colour
        for (first, second), colour in path:
            del sends[first][colour], takes[second][colour]
        for (first, second), colour in path:
            sends[first][a + b - colour], takes[second][a + b - colour] = second, first
        sends[of][a], takes[to][a] = to, of
    return [
        [(of, to[c]) for of, to in enumerate(sends) if c in to]
        for c in range(max((c + 1 for to in sends for c in to), default=0))
    ]


def in_two(early, late, count):
    early, late = set(early) - set(late), set(late)

    def degrees(edges):
        return [
            [sum(edge[side] == device for edge in edges) for device in range(count)] for side in (0, 1)
        ]

    most = max(degrees(late)[0] + degrees(late)[1])
    while early:
        busy, taken = degrees(early), degrees(late)
        top = max(busy[0] + busy[1])
        free = [
            (max(busy[0][of], busy[1][to]), busy[0][of] + busy[1][to], of, to)
            for of, to in sorted(early)
            if max(taken[0][of], taken[1][to]) < most and max(busy[0][of], busy[1][to]) == top
        ]
        if not free:
            break
        early.remove(max(free)[2:])
        late.add(max(free)[2:])
    return sorted(early), sorted(late)


def unit_kernel(pads, order_smem, order, embeddings, unit, value, result, tile, into, out, sem):
    rows = unit.shape[0]
    count = rows // into.shape[0]
    parts = [pl.ds(start, count) for start in range(0, rows, count)]
    loads = [
        pltpu.make_async_copy(embeddings.at[part], value.at[part], into.at[index])
        for index, part in enumerate(parts)
    ]
    stores = [
        pltpu.make_async_copy(result.at[part], unit.at[part], out.at[index])
        for index, part in enumerate(parts)
    ]
    first = order_smem[0]
    base = pl.multiple_of((first // 16) * 16, 16)
    filling = pltpu.make_async_copy(embeddings.at[pl.ds(base, 16)], tile, sem)
    filling.start()
    for load in loads:
        load.start()
    filling.wait()
    among = lax.broadcasted_iota(jnp.int32, (16, 1), 0) == first - base
    filler = jnp.sum(jnp.where(among, tile[...].astype(jnp.float32), 0.0), axis=0, keepdims=True)
    for index, part in enumerate(parts):
        found = valid_rows(pads, order, index * count, count)
        loads[index].wait()
        chunk = jnp.where(found, value[part, :].astype(jnp.float32), filler)
        scale = lax.rsqrt(jnp.sum(chunk * chunk, axis=1, keepdims=True) + 1e-06)
        result[part, :] = (chunk * scale).astype(jnp.bfloat16)
        stores[index].start()
    for store in stores:
        store.wait()


def valid_rows(pads, order, start, count):
    rows = order.shape[1]
    most = min(rows, MOST_PADS)
    valid_count = rows - pads[lax.axis_index("blk")]
    position = rows - most + lax.broadcasted_iota(jnp.int32, (1, most), 1)
    padding = jnp.where(position < valid_count, -1, order[:, rows - most :])
    row = start + lax.broadcasted_iota(jnp.int32, (count, 1), 0)
    return jnp.max(jnp.where(padding == row, 1.0, 0.0), axis=1, keepdims=True) < 1.0


def normalized(embeddings, order, pad_counts):
    rows, depth = embeddings.shape
    chunks = 4
    scalars = pl.BlockSpec(memory_space=pltpu.SMEM)
    return pl.pallas_call(
        unit_kernel,
        out_shape=jax.ShapeDtypeStruct((rows, depth), jnp.bfloat16),
        in_specs=[
            scalars,
            scalars,
            pl.BlockSpec(memory_space=pltpu.VMEM),
            pl.BlockSpec(memory_space=pl.ANY),
        ],
        out_specs=pl.BlockSpec(memory_space=pl.ANY),
        scratch_shapes=[
            pltpu.VMEM((rows, depth), jnp.bfloat16),
            pltpu.VMEM((rows, depth), jnp.bfloat16),
            pltpu.VMEM((16, depth), jnp.bfloat16),
            pltpu.SemaphoreType.DMA((chunks,)),
            pltpu.SemaphoreType.DMA((chunks,)),
            pltpu.SemaphoreType.DMA,
        ],
        compiler_params=pltpu.CompilerParams(vmem_limit_bytes=VMEM),
        cost_estimate=pl.CostEstimate(
            flops=4 * rows * depth, bytes_accessed=4 * rows * depth, transcendentals=rows
        ),
        name="normalized",
    )(pad_counts, order, order.reshape(1, rows), embeddings)


def product(left, right):
    return lax.dot_general(left, right, (((1,), (1,)), ((), ())), preferred_element_type=jnp.float32)


def own_kernel(pads, order, unit, best):
    rows = unit.shape[0]
    best[...] = jnp.full(best.shape, FLOOR, jnp.float32)
    valid = valid_rows(pads, order, 0, rows)
    row = lax.broadcasted_iota(jnp.int32, (rows, 1), 0)
    here = pl.ds(lax.axis_index("blk"), 1)
    for start in range(0, rows, 256):
        part = pl.ds(start, 256)
        scores = product(unit[...], unit[part, :])
        column = start + lax.broadcasted_iota(jnp.int32, (1, 256), 1)
        scores = jnp.where(valid & (row != column), scores, FLOOR)
        best[here, part] = jnp.max(scores, axis=0, keepdims=True)


def own_block(unit, order, pad_counts, nblocks):
    rows, depth = unit.shape
    whole = pl.BlockSpec(memory_space=pltpu.VMEM)
    return pl.pallas_call(
        own_kernel,
        out_shape=jax.ShapeDtypeStruct((nblocks, rows), jnp.float32),
        in_specs=[pl.BlockSpec(memory_space=pltpu.SMEM), whole, whole],
        out_specs=whole,
        compiler_params=pltpu.CompilerParams(vmem_limit_bytes=VMEM),
        cost_estimate=pl.CostEstimate(
            flops=2 * rows * rows * depth, bytes_accessed=2 * rows * depth, transcendentals=0
        ),
        name="own_block",
    )(pad_counts, order.reshape(1, rows), unit)


def pairs_kernel(nslots, nrows, ntaken, nloads, npairs, table, best, *refs):
    arrivals, slots, out = refs[:ntaken], refs[ntaken : ntaken + nslots], refs[ntaken + nslots]
    sent, (held, across, sems) = refs[ntaken + nslots + 1 : -3], refs[-3:]
    rows = out.shape[1]
    here = lax.axis_index("blk")
    loads_at = here * (2 + nrows + ntaken + nloads + 5 * npairs) + 2 + nrows + ntaken
    pairs_at = loads_at + nloads
    rows_at = loads_at - nrows - ntaken
    loads, pairs = table[rows_at - 2], table[rows_at - 1]

    def fetch(load):
        @pl.when(load < loads)
        def _():
            wanted = table[loads_at + jnp.minimum(load, nloads - 1)]
            for index, slot in enumerate(slots):
                @pl.when(wanted == index)
                def _(slot=slot):
                    for start in range(0, rows, 256):
                        part = pl.ds(start, 256)
                        pltpu.make_async_copy(slot.at[part], held.at[load, part], sems.at[load]).start()

    for load in range(min(AHEAD, nloads)):
        fetch(load)
    out[...] = best[...]
    own = pl.ds(here, 1)
    for index, row in enumerate(arrivals):
        handed = table[rows_at + nrows + index] > 0
        out[own, :] = jnp.where(handed, jnp.maximum(out[own, :], row[...]), out[own, :])

    @pl.loop(0, pairs)
    def _(step):
        at = pairs_at + 5 * step
        before = jnp.where(step == 0, 0, table[jnp.maximum(at - 1, 0)])

        @pl.loop(before, table[at + 4])
        def _(load):
            pltpu.make_async_copy(slots[0], held.at[load], sems.at[load]).wait()
            fetch(load + AHEAD)

        left, right = table[at], table[at + 1]
        first, second = pl.ds(table[at + 2], 1), pl.ds(table[at + 3], 1)
        for start in range(0, rows, 256):
            part = pl.ds(start, 256)
            scores = product(held[left], held[right, part, :])
            down = jnp.max(scores, axis=0, keepdims=True)
            out[second, part] = jnp.maximum(out[second, part], down)
            along = jnp.maximum(scores[:, :128], scores[:, 128:])
            across[...] = along if start == 0 else jnp.maximum(across[...], along)
        found = jnp.max(across[...].T, axis=0, keepdims=True)
        out[first, :] = jnp.maximum(out[first, :], found)

    for index, row in enumerate(sent):
        row[...] = out[pl.ds(table[rows_at + index], 1), :]


def in_order_of_loads(pairs, rank):
    left, loaded, ordered = list(pairs), [], []
    while left:
        pair = min(
            left,
            key=lambda p: (sum(s not in loaded for s in p[:2]), max(rank[s] for s in p[:2]), p[2:]),
        )
        left.remove(pair)
        loaded += [slot for slot in pair[:2] if slot not in loaded]
        ordered.append((pair, len(loaded)))
    return loaded, ordered


def scored(best, found, permutes, slots, rank, work, sends):
    names = sorted({slot for pairs in work for pair in pairs for slot in pair[:2]})
    plans = [in_order_of_loads(pairs, rank) for pairs in work]
    nloads = max(len(loaded) for loaded, _ in plans)
    npairs = max(len(pairs) for pairs in work)
    table = []
    for device, (loaded, ordered) in enumerate(plans):
        table += [len(loaded), len(ordered)]
        table += [dict(permute).get(device, device) for permute in sends]
        table += [int(device in dict(permute).values()) for permute in permutes]
        table += [names.index(slot) for slot in loaded] + [0] * (nloads - len(loaded))
        for (slot, other, block, visitor), need in ordered:
            table += [loaded.index(slot), loaded.index(other), block, visitor, need]
        table += [0] * (5 * (npairs - len(ordered)))
    given = [slots[name] for name in names]
    rows, depth = given[0].shape
    whole = pl.BlockSpec(memory_space=pltpu.VMEM)
    return pl.pallas_call(
        functools.partial(pairs_kernel, len(given), len(sends), len(found), nloads, npairs),
        out_shape=[jax.ShapeDtypeStruct(best.shape, jnp.float32)]
        + [jax.ShapeDtypeStruct((1, rows), jnp.float32)] * len(sends),
        in_specs=[pl.BlockSpec(memory_space=pltpu.SMEM)]
        + [whole] * (1 + len(found))
        + [pl.BlockSpec(memory_space=pl.ANY)] * len(given),
        out_specs=[whole] * (1 + len(sends)),
        scratch_shapes=[
            pltpu.VMEM((nloads, rows, depth), jnp.bfloat16),
            pltpu.VMEM((rows, 128), jnp.float32),
            pltpu.SemaphoreType.DMA((nloads,)),
        ],
        compiler_params=pltpu.CompilerParams(vmem_limit_bytes=VMEM),
        cost_estimate=pl.CostEstimate(
            flops=2 * npairs * rows * rows * depth,
            bytes_accessed=2 * nloads * rows * depth,
            transcendentals=0,
        ),
        name="scored",
    )(jnp.asarray(np.array(table, np.int32)), best, *found, *given)


def placed_kernel(taken, pads, order, best, *refs):
    found, out = refs[:-1], refs[-1]
    rows = order.shape[1]
    here = lax.axis_index("blk")
    total = best[pl.ds(here, 1), :]
    for index, row in enumerate(found):
        total = jnp.where(taken[here * len(found) + index] > 0, jnp.maximum(total, row[...]), total)
    column = jnp.broadcast_to(total, (128, rows)).T[:, :1]
    row = lax.broadcasted_iota(jnp.int32, (rows, 1), 0)
    in_order = jnp.max(jnp.where(order[...] == row, column, FLOOR), axis=0, keepdims=True)
    position = lax.broadcasted_iota(jnp.int32, (1, rows), 1)
    out[...] = jnp.where(position < rows - pads[here], in_order, 0.0)


def placed(best, found, permutes, order, pad_counts):
    rows = order.shape[0]
    taken = np.zeros((best.shape[0], len(permutes)), np.int32)
    for index, permute in enumerate(permutes):
        taken[[to for _, to in permute], index] = 1
    whole, scalars = pl.BlockSpec(memory_space=pltpu.VMEM), pl.BlockSpec(memory_space=pltpu.SMEM)
    return pl.pallas_call(
        placed_kernel,
        out_shape=jax.ShapeDtypeStruct((1, rows), jnp.float32),
        in_specs=[scalars, scalars] + [whole] * (2 + len(found)),
        out_specs=whole,
        compiler_params=pltpu.CompilerParams(vmem_limit_bytes=VMEM),
        name="placed",
    )(jnp.asarray(taken.reshape(-1)), pad_counts, order.reshape(1, rows), best, *found).reshape(rows)


def local(embeddings, order, pad_counts):
    nblocks = lax.axis_size("blk")
    moves, work, sending = planned(nblocks)
    unit = normalized(embeddings, order, pad_counts)
    slots, best = {"own": unit}, None
    rank = dict({"own": -1}, **{move.name: move.stage for move in moves})
    edges = {}
    for stage, pairs in enumerate(work):
        due = edges.setdefault(min(last for last in sending if last >= stage), set())
        due |= {(of, to) for of in range(nblocks) for pair in pairs[of] for to in pair[2:] if to != of}
    if len(sending) == 2:
        edges = dict(zip(sending, in_two(*[edges[stage] for stage in sending], nblocks)))
    permutes, found = [], []
    for stage, pairs in enumerate(work):
        starting = [move for move in moves if move.begins == stage]
        for needs in sorted({move.needs for move in starting}):
            values = [slots[name] for name in needs]
            if best is not None:
                *values, best = lax.optimization_barrier((*values, best))
            for move in starting:
                if move.needs == needs:
                    value = values[needs.index(move.source)]
                    slots[move.name] = lax.ppermute(value, "blk", move.pairs)
        if stage == 0:
            best = own_block(unit, order, pad_counts, nblocks)
        sends = colored(sorted(edges[stage]), nblocks) if stage in sending else []
        if any(pairs):
            best, *rows = scored(best, found, permutes, slots, rank, pairs, sends)
            found = [lax.ppermute(row, "blk", permute) for row, permute in zip(rows, sends)]
            permutes = sends
    return placed(best, found, permutes, order, pad_counts)


def solution(mesh):
    in_specs = (P(("groups", "blk"), None), P(("groups", "blk")), P("groups"))
    out_specs = P(("groups", "blk"))
    return jax.shard_map(local, mesh=mesh, in_specs=in_specs, out_specs=out_specs, check_vma=False)
```

```python
import functools

import jax
import jax.numpy as jnp
import numpy as np
from jax import lax
from jax.experimental import pallas as pl
from jax.experimental.pallas import tpu as pltpu
from jax.sharding import PartitionSpec as P

STEPS = 6
VMEM = 62 * 2**20
FLOOR = -2.0
MOST_PADS = 256
AHEAD = 3


class Move:
    def __init__(self, name, source, pairs, begins, stage, *after):
        self.name, self.source, self.pairs = name, source, pairs
        self.begins, self.stage, self.needs = begins, stage, (source, *after)


def grid_moves():
    def at(z, y, lane):
        return 4 * z + 2 * y + (y if lane == 0 else 1 - y)

    def rows(links):
        return [
            (at(z, y, lane), at(to, y, land)) for y in (0, 1) for (z, lane), (to, land) in links
        ]

    def across(planes):
        return [(at(z, y, lane), at(z, 1 - y, lane)) for z, lane in planes for y in (0, 1)]

    every = [(z, lane) for z in range(4) for lane in (0, 1)]
    swap = rows([((z, lane), (z, 1 - lane)) for z, lane in every])
    crossed = [(at(1, y, lane), at(1, 1 - y, 1 - lane)) for y in (0, 1) for lane in (0, 1)]
    first = [((0, 0), (2, 1)), ((2, 0), (3, 1)), ((3, 0), (1, 0)), ((1, 0), (0, 0)), ((0, 1), (1, 1))]
    second = [((3, 1), (1, 1)), ((1, 1), (0, 1)), ((2, 1), (3, 0)), ((1, 0), (2, 1))]
    return [
        Move("R1", "own", rows(first), 0, 1),
        Move("R2", "own", rows(second), 0, 1, "best"),
        Move("Y", "own", across([place for place in every if place[0] != 1]) + crossed, 0, 1),
        Move("A", "own", swap, 0, 0),
        Move("R3", "own", rows([((1, 1), (2, 0)), ((2, 0), (1, 1))]), 1, 2, "R1"),
        Move("V", "R1", [(at(2, y, 1), at(3, y, 1 - y)) for y in (0, 1)] + across([(1, 1)]), 1, 2),
        Move("F", "Y", swap, 2, 2),
        Move("W", "R1", rows([((1, 0), (1, 1)), ((1, 1), (1, 0))]), 2, 2),
    ]


GRID_PAIRS = (
    ((0, 2), (0, 4), (1, 4), (2, 4), (3, 4)),
    ((0, 1), (0, 5), (1, 3), (1, 5), (3, 5)),
    ((0, 3), (0, 6), (1, 6), (2, 3), (2, 6), (3, 6)),
    ((1, 2), (1, 7), (2, 7), (3, 7)),
    ((1, 12), (4, 5), (4, 6), (4, 7), (6, 12), (7, 12)),
    ((1, 13), (2, 8), (2, 12), (2, 13), (5, 8), (7, 13)),
    ((1, 11), (1, 14), (1, 15), (2, 14), (4, 14)),
    ((2, 5), (2, 15), (4, 15), (5, 6), (5, 7), (5, 15), (6, 7)),
    ((5, 9), (5, 10), (5, 11), (9, 10), (9, 11)),
    ((0, 10), (0, 11), (4, 8), (4, 9), (4, 10), (8, 9), (8, 11)),
    ((3, 8), (3, 9), (7, 8), (7, 9), (7, 10), (7, 11)),
    ((6, 8), (6, 9), (6, 10), (6, 11), (8, 10), (10, 11)),
    ((9, 12), (9, 13), (9, 14), (9, 15), (12, 13), (12, 14), (13, 14), (13, 15)),
    ((0, 12), (0, 13), (0, 14), (0, 15), (8, 12), (8, 13), (8, 14)),
    ((11, 12), (11, 13), (11, 14), (11, 15), (12, 15)),
    ((3, 13), (3, 14), (3, 15), (10, 12), (10, 13), (10, 14), (10, 15), (14, 15)),
)


def ring_moves(count):
    return [
        Move("N%d" % k, "own", [((i + k) % count, i) for i in range(count)], 0, k)
        for k in range(1, STEPS + 1)
    ]


def planned(count):
    if count == 16:
        moves, placed_pairs, sending = grid_moves(), GRID_PAIRS, (1, 2)
    else:
        moves, sending = ring_moves(count), (STEPS,)
        placed_pairs = [[(b, (b + k) % count) for k in range(1, STEPS + 1)] for b in range(count)]
    holds = {"own": {d: d for d in range(count)}}
    stage_of = {"own": 0}
    for move in moves:
        holds[move.name] = {to: holds[move.source][of] for of, to in move.pairs}
        stage_of[move.name] = move.stage
    stages = 1 + max(stage_of.values())
    work = [[[] for _ in range(count)] for _ in range(stages)]
    for device, pairs in enumerate(placed_pairs):
        slot_of = {}
        for slot in sorted(stage_of, key=stage_of.get):
            if device in holds[slot]:
                slot_of.setdefault(holds[slot][device], slot)
        for block, visitor in pairs:
            slot, other = slot_of[block], slot_of[visitor]
            stage = max(stage_of[slot], stage_of[other])
            work[stage][device].append((slot, other, block, visitor))
    scored_pairs = sorted(tuple(sorted(pair)) for pairs in placed_pairs for pair in pairs)
    needed = {tuple(sorted((b, (b + k) % count))) for b in range(count) for k in range(1, STEPS + 1)}
    assert scored_pairs == sorted(needed)
    return moves, work, sending


def colored(edges, count):
    ends = [of for of, _ in edges], [to for _, to in edges]
    most = max((side.count(device) for side in ends for device in range(count)), default=0)
    sends, takes = [{} for _ in range(count)], [{} for _ in range(count)]
    for of, to in sorted(edges, key=lambda edge: (edge[0] ^ edge[1], edge)):
        a = next(c for c in range(len(edges)) if c not in sends[of])
        b = next(c for c in range(len(edges)) if c not in takes[to])
        both = next(c for c in range(2 * len(edges)) if c not in sends[of] and c not in takes[to])
        if both < most:
            a = b = both
        path, node, tables, colour = [], to, (takes, sends), a
        while a != b and colour in tables[0][node]:
            end = tables[0][node][colour]
            path.append(((end, node) if tables[0] is takes else (node, end), colour))
            node, tables, colour = end, tables[::-1], a + b - colour
        for (first, second), colour in path:
            del sends[first][colour], takes[second][colour]
        for (first, second), colour in path:
            sends[first][a + b - colour], takes[second][a + b - colour] = second, first
        sends[of][a], takes[to][a] = to, of
    return [
        [(of, to[c]) for of, to in enumerate(sends) if c in to]
        for c in range(max((c + 1 for to in sends for c in to), default=0))
    ]


def in_two(early, late, count):
    early, late = set(early) - set(late), set(late)

    def degrees(edges):
        return [
            [sum(edge[side] == device for edge in edges) for device in range(count)] for side in (0, 1)
        ]

    most = max(degrees(late)[0] + degrees(late)[1])
    while early:
        busy, taken = degrees(early), degrees(late)
        top = max(busy[0] + busy[1])
        free = [
            (max(busy[0][of], busy[1][to]), busy[0][of] + busy[1][to], of, to)
            for of, to in sorted(early)
            if max(taken[0][of], taken[1][to]) < most and max(busy[0][of], busy[1][to]) == top
        ]
        if not free:
            break
        early.remove(max(free)[2:])
        late.add(max(free)[2:])
    return sorted(early), sorted(late)


def unit_kernel(pads, order, embeddings, unit, value, result, tile, scalars, line, into, out, sems):
    rows = unit.shape[0]
    count = rows // into.shape[0]
    parts = [pl.ds(start, count) for start in range(0, rows, count)]
    loads = [
        pltpu.make_async_copy(embeddings.at[part], value.at[part], into.at[index])
        for index, part in enumerate(parts)
    ]
    stores = [
        pltpu.make_async_copy(result.at[part], unit.at[part], out.at[index])
        for index, part in enumerate(parts)
    ]
    to_scalars = pltpu.make_async_copy(order, scalars, sems.at[0])
    to_line = pltpu.make_async_copy(order, line, sems.at[1])
    to_scalars.start()
    to_line.start()
    for load in loads:
        load.start()
    to_scalars.wait()
    first = scalars[0, 0]
    base = pl.multiple_of((first // 16) * 16, 16)
    filling = pltpu.make_async_copy(embeddings.at[pl.ds(base, 16)], tile, sems.at[2])
    filling.start()
    to_line.wait()
    found = [valid_rows(pads, line, index * count, count) for index in range(len(parts))]
    among = lax.broadcasted_iota(jnp.int32, (16, 1), 0) == first - base
    filling.wait()
    filler = jnp.sum(jnp.where(among, tile[...].astype(jnp.float32), 0.0), axis=0, keepdims=True)
    for index, part in enumerate(parts):
        loads[index].wait()
        chunk = jnp.where(found[index], value[part, :].astype(jnp.float32), filler)
        scale = lax.rsqrt(jnp.sum(chunk * chunk, axis=1, keepdims=True) + 1e-06)
        result[part, :] = (chunk * scale).astype(jnp.bfloat16)
        stores[index].start()
    for store in stores:
        store.wait()


def valid_rows(pads, order, start, count):
    rows = order.shape[1]
    most = min(rows, MOST_PADS)
    valid_count = rows - pads[lax.axis_index("blk")]
    position = rows - most + lax.broadcasted_iota(jnp.int32, (1, most), 1)
    padding = jnp.where(position < valid_count, -1, order[:, rows - most :])
    row = start + lax.broadcasted_iota(jnp.int32, (count, 1), 0)
    return jnp.max(jnp.where(padding == row, 1.0, 0.0), axis=1, keepdims=True) < 1.0


def normalized(embeddings, order, pad_counts):
    rows, depth = embeddings.shape
    chunks = 8
    anywhere = pl.BlockSpec(memory_space=pl.ANY)
    return pl.pallas_call(
        unit_kernel,
        out_shape=jax.ShapeDtypeStruct((rows, depth), jnp.bfloat16),
        in_specs=[pl.BlockSpec(memory_space=pltpu.SMEM), anywhere, anywhere],
        out_specs=anywhere,
        scratch_shapes=[
            pltpu.VMEM((rows, depth), jnp.bfloat16),
            pltpu.VMEM((rows, depth), jnp.bfloat16),
            pltpu.VMEM((16, depth), jnp.bfloat16),
            pltpu.SMEM((1, rows), jnp.int32),
            pltpu.VMEM((1, rows), jnp.int32),
            pltpu.SemaphoreType.DMA((chunks,)),
            pltpu.SemaphoreType.DMA((chunks,)),
            pltpu.SemaphoreType.DMA((3,)),
        ],
        compiler_params=pltpu.CompilerParams(vmem_limit_bytes=VMEM),
        cost_estimate=pl.CostEstimate(
            flops=4 * rows * depth, bytes_accessed=4 * rows * depth, transcendentals=rows
        ),
        name="normalized",
    )(pad_counts, order.reshape(1, rows), embeddings)


def product(left, right):
    return lax.dot_general(left, right, (((1,), (1,)), ((), ())), preferred_element_type=jnp.float32)


def own_kernel(pads, order, unit, best):
    rows = unit.shape[0]
    best[...] = jnp.full(best.shape, FLOOR, jnp.float32)
    valid = valid_rows(pads, order, 0, rows)
    row = lax.broadcasted_iota(jnp.int32, (rows, 1), 0)
    here = pl.ds(lax.axis_index("blk"), 1)
    for start in range(0, rows, 256):
        part = pl.ds(start, 256)
        scores = product(unit[...], unit[part, :])
        column = start + lax.broadcasted_iota(jnp.int32, (1, 256), 1)
        scores = jnp.where(valid & (row != column), scores, FLOOR)
        best[here, part] = jnp.max(scores, axis=0, keepdims=True)


def own_block(unit, order, pad_counts, nblocks):
    rows, depth = unit.shape
    whole = pl.BlockSpec(memory_space=pltpu.VMEM)
    return pl.pallas_call(
        own_kernel,
        out_shape=jax.ShapeDtypeStruct((nblocks, rows), jnp.float32),
        in_specs=[pl.BlockSpec(memory_space=pltpu.SMEM), whole, whole],
        out_specs=whole,
        compiler_params=pltpu.CompilerParams(vmem_limit_bytes=VMEM),
        cost_estimate=pl.CostEstimate(
            flops=2 * rows * rows * depth, bytes_accessed=2 * rows * depth, transcendentals=0
        ),
        name="own_block",
    )(pad_counts, order.reshape(1, rows), unit)


def pairs_kernel(nslots, nrows, ntaken, nloads, npairs, table, best, *refs):
    arrivals, slots, out = refs[:ntaken], refs[ntaken : ntaken + nslots], refs[ntaken + nslots]
    sent, (held, across, sems) = refs[ntaken + nslots + 1 : -3], refs[-3:]
    rows = out.shape[1]
    here = lax.axis_index("blk")
    loads_at = here * (2 + nrows + ntaken + nloads + 5 * npairs) + 2 + nrows + ntaken
    pairs_at = loads_at + nloads
    rows_at = loads_at - nrows - ntaken
    loads, pairs = table[rows_at - 2], table[rows_at - 1]

    def fetch(load):
        @pl.when(load < loads)
        def _():
            wanted = table[loads_at + jnp.minimum(load, nloads - 1)]
            for index, slot in enumerate(slots):
                @pl.when(wanted == index)
                def _(slot=slot):
                    for start in range(0, rows, 256):
                        part = pl.ds(start, 256)
                        pltpu.make_async_copy(slot.at[part], held.at[load, part], sems.at[load]).start()

    for load in range(min(AHEAD, nloads)):
        fetch(load)
    out[...] = best[...]
    own = pl.ds(here, 1)
    for index, row in enumerate(arrivals):
        handed = table[rows_at + nrows + index] > 0
        out[own, :] = jnp.where(handed, jnp.maximum(out[own, :], row[...]), out[own, :])

    @pl.loop(0, pairs)
    def _(step):
        at = pairs_at + 5 * step
        before = jnp.where(step == 0, 0, table[jnp.maximum(at - 1, 0)])

        @pl.loop(before, table[at + 4])
        def _(load):
            pltpu.make_async_copy(slots[0], held.at[load], sems.at[load]).wait()
            fetch(load + AHEAD)

        left, right = table[at], table[at + 1]
        first, second = pl.ds(table[at + 2], 1), pl.ds(table[at + 3], 1)
        for start in range(0, rows, 256):
            part = pl.ds(start, 256)
            scores = product(held[left], held[right, part, :])
            down = jnp.max(scores, axis=0, keepdims=True)
            out[second, part] = jnp.maximum(out[second, part], down)
            along = jnp.maximum(scores[:, :128], scores[:, 128:])
            across[...] = along if start == 0 else jnp.maximum(across[...], along)
        found = jnp.max(across[...].T, axis=0, keepdims=True)
        out[first, :] = jnp.maximum(out[first, :], found)

    for index, row in enumerate(sent):
        row[...] = out[pl.ds(table[rows_at + index], 1), :]


def in_order_of_loads(pairs, rank):
    left, loaded, ordered = list(pairs), [], []
    while left:
        pair = min(
            left,
            key=lambda p: (sum(s not in loaded for s in p[:2]), max(rank[s] for s in p[:2]), p[2:]),
        )
        left.remove(pair)
        loaded += [slot for slot in pair[:2] if slot not in loaded]
        ordered.append((pair, len(loaded)))
    return loaded, ordered


def scored(best, found, permutes, slots, rank, work, sends):
    names = sorted({slot for pairs in work for pair in pairs for slot in pair[:2]})
    plans = [in_order_of_loads(pairs, rank) for pairs in work]
    nloads = max(len(loaded) for loaded, _ in plans)
    npairs = max(len(pairs) for pairs in work)
    table = []
    for device, (loaded, ordered) in enumerate(plans):
        table += [len(loaded), len(ordered)]
        table += [dict(permute).get(device, device) for permute in sends]
        table += [int(device in dict(permute).values()) for permute in permutes]
        table += [names.index(slot) for slot in loaded] + [0] * (nloads - len(loaded))
        for (slot, other, block, visitor), need in ordered:
            table += [loaded.index(slot), loaded.index(other), block, visitor, need]
        table += [0] * (5 * (npairs - len(ordered)))
    given = [slots[name] for name in names]
    rows, depth = given[0].shape
    whole = pl.BlockSpec(memory_space=pltpu.VMEM)
    return pl.pallas_call(
        functools.partial(pairs_kernel, len(given), len(sends), len(found), nloads, npairs),
        out_shape=[jax.ShapeDtypeStruct(best.shape, jnp.float32)]
        + [jax.ShapeDtypeStruct((1, rows), jnp.float32)] * len(sends),
        in_specs=[pl.BlockSpec(memory_space=pltpu.SMEM)]
        + [whole] * (1 + len(found))
        + [pl.BlockSpec(memory_space=pl.ANY)] * len(given),
        out_specs=[whole] * (1 + len(sends)),
        scratch_shapes=[
            pltpu.VMEM((nloads, rows, depth), jnp.bfloat16),
            pltpu.VMEM((rows, 128), jnp.float32),
            pltpu.SemaphoreType.DMA((nloads,)),
        ],
        compiler_params=pltpu.CompilerParams(vmem_limit_bytes=VMEM),
        cost_estimate=pl.CostEstimate(
            flops=2 * npairs * rows * rows * depth,
            bytes_accessed=2 * nloads * rows * depth,
            transcendentals=0,
        ),
        name="scored",
    )(jnp.asarray(np.array(table, np.int32)), best, *found, *given)


def placed_kernel(taken, pads, order, best, *refs):
    found, out = refs[:-1], refs[-1]
    rows = order.shape[1]
    here = lax.axis_index("blk")
    total = best[pl.ds(here, 1), :]
    for index, row in enumerate(found):
        total = jnp.where(taken[here * len(found) + index] > 0, jnp.maximum(total, row[...]), total)
    column = jnp.broadcast_to(total, (128, rows)).T[:, :1]
    row = lax.broadcasted_iota(jnp.int32, (rows, 1), 0)
    in_order = jnp.max(jnp.where(order[...] == row, column, FLOOR), axis=0, keepdims=True)
    position = lax.broadcasted_iota(jnp.int32, (1, rows), 1)
    out[...] = jnp.where(position < rows - pads[here], in_order, 0.0)


def placed(best, found, permutes, order, pad_counts):
    rows = order.shape[0]
    taken = np.zeros((best.shape[0], len(permutes)), np.int32)
    for index, permute in enumerate(permutes):
        taken[[to for _, to in permute], index] = 1
    whole, scalars = pl.BlockSpec(memory_space=pltpu.VMEM), pl.BlockSpec(memory_space=pltpu.SMEM)
    return pl.pallas_call(
        placed_kernel,
        out_shape=jax.ShapeDtypeStruct((1, rows), jnp.float32),
        in_specs=[scalars, scalars] + [whole] * (2 + len(found)),
        out_specs=whole,
        compiler_params=pltpu.CompilerParams(vmem_limit_bytes=VMEM),
        name="placed",
    )(jnp.asarray(taken.reshape(-1)), pad_counts, order.reshape(1, rows), best, *found).reshape(rows)


def local(embeddings, order, pad_counts):
    nblocks = lax.axis_size("blk")
    moves, work, sending = planned(nblocks)
    unit = normalized(embeddings, order, pad_counts)
    slots, best = {"own": unit}, None
    rank = dict({"own": -1}, **{move.name: move.stage for move in moves})
    edges = {}
    for stage, pairs in enumerate(work):
        due = edges.setdefault(min(last for last in sending if last >= stage), set())
        due |= {(of, to) for of in range(nblocks) for pair in pairs[of] for to in pair[2:] if to != of}
    if len(sending) == 2:
        edges = dict(zip(sending, in_two(*[edges[stage] for stage in sending], nblocks)))
    permutes, found = [], []
    for stage, pairs in enumerate(work):
        starting = [move for move in moves if move.begins == stage]
        for needs in sorted({move.needs for move in starting}, key=lambda needs: ("best" in needs, needs)):
            if stage == 0 and "best" in needs:
                best = own_block(unit, order, pad_counts, nblocks)
            values = [slots[name] for name in needs if name != "best"]
            if best is not None:
                *values, best = lax.optimization_barrier((*values, best))
            for move in starting:
                if move.needs == needs:
                    value = values[needs.index(move.source)]
                    slots[move.name] = lax.ppermute(value, "blk", move.pairs)
        if best is None:
            best = own_block(unit, order, pad_counts, nblocks)
        sends = colored(sorted(edges[stage]), nblocks) if stage in sending else []
        if any(pairs):
            best, *rows = scored(best, found, permutes, slots, rank, pairs, sends)
            found = [lax.ppermute(row, "blk", permute) for row, permute in zip(rows, sends)]
            permutes = sends
    return placed(best, found, permutes, order, pad_counts)


def solution(mesh):
    in_specs = (P(("groups", "blk"), None), P(("groups", "blk")), P("groups"))
    out_specs = P(("groups", "blk"))
    return jax.shard_map(local, mesh=mesh, in_specs=in_specs, out_specs=out_specs, check_vma=False)
```

```python
import functools

import jax
import jax.numpy as jnp
import numpy as np
from jax import lax
from jax.experimental import pallas as pl
from jax.experimental.pallas import tpu as pltpu
from jax.sharding import PartitionSpec as P

STEPS = 6
VMEM = 62 * 2**20
FLOOR = -2.0
MOST_PADS = 256
AHEAD = 3


class Move:
    def __init__(self, name, source, pairs, begins, stage, *after):
        self.name, self.source, self.pairs = name, source, pairs
        self.begins, self.stage, self.needs = begins, stage, (source, *after)


def grid_moves():
    def at(z, y, lane):
        return 4 * z + 2 * y + (y if lane == 0 else 1 - y)

    def rows(links):
        return [
            (at(z, y, lane), at(to, y, land)) for y in (0, 1) for (z, lane), (to, land) in links
        ]

    def across(planes):
        return [(at(z, y, lane), at(z, 1 - y, lane)) for z, lane in planes for y in (0, 1)]

    every = [(z, lane) for z in range(4) for lane in (0, 1)]
    swap = rows([((z, lane), (z, 1 - lane)) for z, lane in every])
    crossed = [(at(1, y, lane), at(1, 1 - y, 1 - lane)) for y in (0, 1) for lane in (0, 1)]
    first = [((0, 0), (2, 1)), ((2, 0), (3, 1)), ((3, 0), (1, 0)), ((1, 0), (0, 0)), ((0, 1), (1, 1))]
    second = [((3, 1), (1, 1)), ((1, 1), (0, 1)), ((2, 1), (3, 0)), ((1, 0), (2, 1))]
    return [
        Move("R1", "own", rows(first), 0, 1),
        Move("R2", "own", rows(second), 0, 1),
        Move("Y", "own", across([place for place in every if place[0] != 1]) + crossed, 0, 1),
        Move("A", "own", swap, 0, 0),
        Move("R3", "own", rows([((1, 1), (2, 0)), ((2, 0), (1, 1))]), 1, 2, "R1"),
        Move("V", "R1", [(at(2, y, 1), at(3, y, 1 - y)) for y in (0, 1)] + across([(1, 1)]), 1, 2),
        Move("F", "Y", swap, 2, 2),
        Move("W", "R1", rows([((1, 0), (1, 1)), ((1, 1), (1, 0))]), 2, 2),
    ]


GRID_PAIRS = (
    ((0, 2), (0, 4), (1, 4), (2, 4), (3, 4)),
    ((0, 1), (0, 5), (1, 3), (1, 5), (3, 5)),
    ((0, 3), (0, 6), (1, 6), (2, 3), (2, 6), (3, 6)),
    ((1, 2), (1, 7), (2, 7), (3, 7)),
    ((1, 12), (4, 5), (4, 6), (4, 7), (6, 12), (7, 12)),
    ((1, 13), (2, 8), (2, 12), (2, 13), (5, 8), (7, 13)),
    ((1, 11), (1, 14), (1, 15), (2, 14), (4, 14)),
    ((2, 5), (2, 15), (4, 15), (5, 6), (5, 7), (5, 15), (6, 7)),
    ((5, 9), (5, 10), (5, 11), (9, 10), (9, 11)),
    ((0, 10), (0, 11), (4, 8), (4, 9), (4, 10), (8, 9), (8, 11)),
    ((3, 8), (3, 9), (7, 8), (7, 9), (7, 10), (7, 11)),
    ((6, 8), (6, 9), (6, 10), (6, 11), (8, 10), (10, 11)),
    ((9, 12), (9, 13), (9, 14), (9, 15), (12, 13), (12, 14), (13, 14), (13, 15)),
    ((0, 12), (0, 13), (0, 14), (0, 15), (8, 12), (8, 13), (8, 14)),
    ((11, 12), (11, 13), (11, 14), (11, 15), (12, 15)),
    ((3, 13), (3, 14), (3, 15), (10, 12), (10, 13), (10, 14), (10, 15), (14, 15)),
)


def ring_moves(count):
    return [
        Move("N%d" % k, "own", [((i + k) % count, i) for i in range(count)], 0, k)
        for k in range(1, STEPS + 1)
    ]


def planned(count):
    if count == 16:
        moves, placed_pairs, sending = grid_moves(), GRID_PAIRS, (1, 2)
    else:
        moves, sending = ring_moves(count), (STEPS,)
        placed_pairs = [[(b, (b + k) % count) for k in range(1, STEPS + 1)] for b in range(count)]
    holds = {"own": {d: d for d in range(count)}}
    stage_of = {"own": 0}
    for move in moves:
        holds[move.name] = {to: holds[move.source][of] for of, to in move.pairs}
        stage_of[move.name] = move.stage
    stages = 1 + max(stage_of.values())
    work = [[[] for _ in range(count)] for _ in range(stages)]
    for device, pairs in enumerate(placed_pairs):
        slot_of = {}
        for slot in sorted(stage_of, key=stage_of.get):
            if device in holds[slot]:
                slot_of.setdefault(holds[slot][device], slot)
        for block, visitor in pairs:
            slot, other = slot_of[block], slot_of[visitor]
            stage = max(stage_of[slot], stage_of[other])
            work[stage][device].append((slot, other, block, visitor))
    scored_pairs = sorted(tuple(sorted(pair)) for pairs in placed_pairs for pair in pairs)
    needed = {tuple(sorted((b, (b + k) % count))) for b in range(count) for k in range(1, STEPS + 1)}
    assert scored_pairs == sorted(needed)
    return moves, work, sending


def colored(edges, count):
    sends, takes = [{} for _ in range(count)], [{} for _ in range(count)]
    for of, to in edges:
        a = next(c for c in range(len(edges)) if c not in sends[of])
        b = next(c for c in range(len(edges)) if c not in takes[to])
        path, node, tables, colour = [], to, (takes, sends), a
        while a != b and colour in tables[0][node]:
            end = tables[0][node][colour]
            path.append(((end, node) if tables[0] is takes else (node, end), colour))
            node, tables, colour = end, tables[::-1], a + b - colour
        for (first, second), colour in path:
            del sends[first][colour], takes[second][colour]
        for (first, second), colour in path:
            sends[first][a + b - colour], takes[second][a + b - colour] = second, first
        sends[of][a], takes[to][a] = to, of
    return [
        [(of, to[c]) for of, to in enumerate(sends) if c in to]
        for c in range(max((c + 1 for to in sends for c in to), default=0))
    ]


def in_two(early, late, count):
    early, late = set(early) - set(late), set(late)

    def degrees(edges):
        return [
            [sum(edge[side] == device for edge in edges) for device in range(count)] for side in (0, 1)
        ]

    most = max(degrees(late)[0] + degrees(late)[1])
    while early:
        busy, taken = degrees(early), degrees(late)
        top = max(busy[0] + busy[1])
        free = [
            (max(busy[0][of], busy[1][to]), busy[0][of] + busy[1][to], of, to)
            for of, to in sorted(early)
            if max(taken[0][of], taken[1][to]) < most and max(busy[0][of], busy[1][to]) == top
        ]
        if not free:
            break
        early.remove(max(free)[2:])
        late.add(max(free)[2:])
    return sorted(early), sorted(late)


def unit_kernel(pads, order_smem, order, embeddings, unit, value, result, tile, into, out, sem):
    rows = unit.shape[0]
    count = rows // into.shape[0]
    parts = [pl.ds(start, count) for start in range(0, rows, count)]
    loads = [
        pltpu.make_async_copy(embeddings.at[part], value.at[part], into.at[index])
        for index, part in enumerate(parts)
    ]
    stores = [
        pltpu.make_async_copy(result.at[part], unit.at[part], out.at[index])
        for index, part in enumerate(parts)
    ]
    first = order_smem[0]
    base = pl.multiple_of((first // 16) * 16, 16)
    filling = pltpu.make_async_copy(embeddings.at[pl.ds(base, 16)], tile, sem)
    filling.start()
    for load in loads:
        load.start()
    filling.wait()
    among = lax.broadcasted_iota(jnp.int32, (16, 1), 0) == first - base
    filler = jnp.sum(jnp.where(among, tile[...].astype(jnp.float32), 0.0), axis=0, keepdims=True)
    for index, part in enumerate(parts):
        found = valid_rows(pads, order, index * count, count)
        loads[index].wait()
        chunk = jnp.where(found, value[part, :].astype(jnp.float32), filler)
        scale = lax.rsqrt(jnp.sum(chunk * chunk, axis=1, keepdims=True) + 1e-06)
        result[part, :] = (chunk * scale).astype(jnp.bfloat16)
        stores[index].start()
    for store in stores:
        store.wait()


def valid_rows(pads, order, start, count):
    rows = order.shape[1]
    most = min(rows, MOST_PADS)
    valid_count = rows - pads[lax.axis_index("blk")]
    position = rows - most + lax.broadcasted_iota(jnp.int32, (1, most), 1)
    padding = jnp.where(position < valid_count, -1, order[:, rows - most :])
    row = start + lax.broadcasted_iota(jnp.int32, (count, 1), 0)
    return jnp.max(jnp.where(padding == row, 1.0, 0.0), axis=1, keepdims=True) < 1.0


def normalized(embeddings, order, pad_counts):
    rows, depth = embeddings.shape
    chunks = 4
    scalars = pl.BlockSpec(memory_space=pltpu.SMEM)
    return pl.pallas_call(
        unit_kernel,
        out_shape=jax.ShapeDtypeStruct((rows, depth), jnp.bfloat16),
        in_specs=[
            scalars,
            scalars,
            pl.BlockSpec(memory_space=pltpu.VMEM),
            pl.BlockSpec(memory_space=pl.ANY),
        ],
        out_specs=pl.BlockSpec(memory_space=pl.ANY),
        scratch_shapes=[
            pltpu.VMEM((rows, depth), jnp.bfloat16),
            pltpu.VMEM((rows, depth), jnp.bfloat16),
            pltpu.VMEM((16, depth), jnp.bfloat16),
            pltpu.SemaphoreType.DMA((chunks,)),
            pltpu.SemaphoreType.DMA((chunks,)),
            pltpu.SemaphoreType.DMA,
        ],
        compiler_params=pltpu.CompilerParams(vmem_limit_bytes=VMEM),
        cost_estimate=pl.CostEstimate(
            flops=4 * rows * depth, bytes_accessed=4 * rows * depth, transcendentals=rows
        ),
        name="normalized",
    )(pad_counts, order, order.reshape(1, rows), embeddings)


def product(left, right):
    return lax.dot_general(left, right, (((1,), (1,)), ((), ())), preferred_element_type=jnp.float32)


def own_kernel(pads, order, unit, best):
    rows = unit.shape[0]
    best[...] = jnp.full(best.shape, FLOOR, jnp.float32)
    valid = valid_rows(pads, order, 0, rows)
    row = lax.broadcasted_iota(jnp.int32, (rows, 1), 0)
    here = pl.ds(lax.axis_index("blk"), 1)
    for start in range(0, rows, 256):
        part = pl.ds(start, 256)
        scores = product(unit[...], unit[part, :])
        column = start + lax.broadcasted_iota(jnp.int32, (1, 256), 1)
        scores = jnp.where(valid & (row != column), scores, FLOOR)
        best[here, part] = jnp.max(scores, axis=0, keepdims=True)


def own_block(unit, order, pad_counts, nblocks):
    rows, depth = unit.shape
    whole = pl.BlockSpec(memory_space=pltpu.VMEM)
    return pl.pallas_call(
        own_kernel,
        out_shape=jax.ShapeDtypeStruct((nblocks, rows), jnp.float32),
        in_specs=[pl.BlockSpec(memory_space=pltpu.SMEM), whole, whole],
        out_specs=whole,
        compiler_params=pltpu.CompilerParams(vmem_limit_bytes=VMEM),
        cost_estimate=pl.CostEstimate(
            flops=2 * rows * rows * depth, bytes_accessed=2 * rows * depth, transcendentals=0
        ),
        name="own_block",
    )(pad_counts, order.reshape(1, rows), unit)


def pairs_kernel(nslots, nrows, ntaken, nloads, npairs, table, best, *refs):
    arrivals, slots, out = refs[:ntaken], refs[ntaken : ntaken + nslots], refs[ntaken + nslots]
    sent, (held, turned, across, sems) = refs[ntaken + nslots + 1 : -4], refs[-4:]
    rows = out.shape[1]
    here = lax.axis_index("blk")
    loads_at = here * (2 + nrows + ntaken + nloads + 6 * npairs) + 2 + nrows + ntaken
    pairs_at = loads_at + nloads
    rows_at = loads_at - nrows - ntaken
    loads, pairs = table[rows_at - 2], table[rows_at - 1]

    def fetch(load):
        @pl.when(load < loads)
        def _():
            wanted = table[loads_at + jnp.minimum(load, nloads - 1)]
            for index, slot in enumerate(slots):
                @pl.when(wanted == index)
                def _(slot=slot):
                    for start in range(0, rows, 256):
                        part = pl.ds(start, 256)
                        pltpu.make_async_copy(slot.at[part], held.at[load, part], sems.at[load]).start()

    for load in range(min(AHEAD, nloads)):
        fetch(load)
    out[...] = best[...]
    own = pl.ds(here, 1)
    for index, row in enumerate(arrivals):
        handed = table[rows_at + nrows + index] > 0
        out[own, :] = jnp.where(handed, jnp.maximum(out[own, :], row[...]), out[own, :])

    @pl.loop(0, pairs)
    def _(step):
        at = pairs_at + 6 * step
        before = jnp.where(step == 0, 0, table[jnp.maximum(at - 2, 0)])
        turn = table[at + 5]

        def arrived(load):
            pltpu.make_async_copy(slots[0], held.at[load], sems.at[load]).wait()
            fetch(load + AHEAD)

        pl.loop(before, jnp.maximum(before, turn))(arrived)

        @pl.when(turn > 0)
        def _():
            for start in range(0, rows, 256):
                part = pl.ds(start, 256)
                turned[:, part] = held[table[at + 1], part, :].T

        pl.loop(jnp.maximum(before, turn), table[at + 4])(arrived)
        left, right = table[at], table[at + 1]
        first, second = pl.ds(table[at + 2], 1), pl.ds(table[at + 3], 1)
        for start in range(0, rows, 256):
            part = pl.ds(start, 256)
            scores = jnp.dot(held[left], turned[:, part], preferred_element_type=jnp.float32)
            down = jnp.max(scores, axis=0, keepdims=True)
            out[second, part] = jnp.maximum(out[second, part], down)
            along = jnp.maximum(scores[:, :128], scores[:, 128:])
            across[...] = along if start == 0 else jnp.maximum(across[...], along)
        found = jnp.max(across[...].T, axis=0, keepdims=True)
        out[first, :] = jnp.maximum(out[first, :], found)

    for index, row in enumerate(sent):
        row[...] = out[pl.ds(table[rows_at + index], 1), :]


def in_order_of_loads(pairs, rank):
    waiting, loaded, ordered, right = list(pairs), [], [], None
    while waiting:
        pair = min(
            waiting,
            key=lambda p: (
                right not in p[:2],
                sum(s not in loaded for s in p[:2]),
                max(rank[s] for s in p[:2]),
                p[2:],
            ),
        )
        turn = right not in pair[:2]
        if turn:
            uses = [sum(slot in p[:2] for p in waiting) for slot in pair[:2]]
            right = pair[0] if uses[0] > uses[1] else pair[1]
        waiting.remove(pair)
        if pair[1] != right:
            pair = (pair[1], pair[0], pair[3], pair[2])
        loaded += [slot for slot in pair[1::-1] if slot not in loaded]
        index = [loaded.index(slot) for slot in pair[:2]]
        ordered.append((*index, *pair[2:], len(loaded), (index[1] + 1) * turn))
    return loaded, ordered


def scored(best, found, permutes, slots, rank, work, sends):
    names = sorted({slot for pairs in work for pair in pairs for slot in pair[:2]})
    plans = [in_order_of_loads(pairs, rank) for pairs in work]
    nloads = max(len(loaded) for loaded, _ in plans)
    npairs = max(len(pairs) for pairs in work)
    table = []
    for device, (loaded, ordered) in enumerate(plans):
        table += [len(loaded), len(ordered)]
        table += [dict(permute).get(device, device) for permute in sends]
        table += [int(device in dict(permute).values()) for permute in permutes]
        table += [names.index(slot) for slot in loaded] + [0] * (nloads - len(loaded))
        for entry in ordered:
            table += entry
        table += [0] * (6 * (npairs - len(ordered)))
    given = [slots[name] for name in names]
    rows, depth = given[0].shape
    whole = pl.BlockSpec(memory_space=pltpu.VMEM)
    return pl.pallas_call(
        functools.partial(pairs_kernel, len(given), len(sends), len(found), nloads, npairs),
        out_shape=[jax.ShapeDtypeStruct(best.shape, jnp.float32)]
        + [jax.ShapeDtypeStruct((1, rows), jnp.float32)] * len(sends),
        in_specs=[pl.BlockSpec(memory_space=pltpu.SMEM)]
        + [whole] * (1 + len(found))
        + [pl.BlockSpec(memory_space=pl.ANY)] * len(given),
        out_specs=[whole] * (1 + len(sends)),
        scratch_shapes=[
            pltpu.VMEM((nloads, rows, depth), jnp.bfloat16),
            pltpu.VMEM((depth, rows), jnp.bfloat16),
            pltpu.VMEM((rows, 128), jnp.float32),
            pltpu.SemaphoreType.DMA((nloads,)),
        ],
        compiler_params=pltpu.CompilerParams(vmem_limit_bytes=VMEM),
        cost_estimate=pl.CostEstimate(
            flops=2 * npairs * rows * rows * depth,
            bytes_accessed=2 * nloads * rows * depth,
            transcendentals=0,
        ),
        name="scored",
    )(jnp.asarray(np.array(table, np.int32)), best, *found, *given)


def placed_kernel(taken, pads, order, best, *refs):
    found, out = refs[:-1], refs[-1]
    rows = order.shape[1]
    here = lax.axis_index("blk")
    total = best[pl.ds(here, 1), :]
    for index, row in enumerate(found):
        total = jnp.where(taken[here * len(found) + index] > 0, jnp.maximum(total, row[...]), total)
    column = jnp.broadcast_to(total, (128, rows)).T[:, :1]
    row = lax.broadcasted_iota(jnp.int32, (rows, 1), 0)
    in_order = jnp.max(jnp.where(order[...] == row, column, FLOOR), axis=0, keepdims=True)
    position = lax.broadcasted_iota(jnp.int32, (1, rows), 1)
    out[...] = jnp.where(position < rows - pads[here], in_order, 0.0)


def placed(best, found, permutes, order, pad_counts):
    rows = order.shape[0]
    taken = np.zeros((best.shape[0], len(permutes)), np.int32)
    for index, permute in enumerate(permutes):
        taken[[to for _, to in permute], index] = 1
    whole, scalars = pl.BlockSpec(memory_space=pltpu.VMEM), pl.BlockSpec(memory_space=pltpu.SMEM)
    return pl.pallas_call(
        placed_kernel,
        out_shape=jax.ShapeDtypeStruct((1, rows), jnp.float32),
        in_specs=[scalars, scalars] + [whole] * (2 + len(found)),
        out_specs=whole,
        compiler_params=pltpu.CompilerParams(vmem_limit_bytes=VMEM),
        name="placed",
    )(jnp.asarray(taken.reshape(-1)), pad_counts, order.reshape(1, rows), best, *found).reshape(rows)


def local(embeddings, order, pad_counts):
    nblocks = lax.axis_size("blk")
    moves, work, sending = planned(nblocks)
    unit = normalized(embeddings, order, pad_counts)
    slots, best = {"own": unit}, None
    rank = dict({"own": -1}, **{move.name: move.stage for move in moves})
    edges = {}
    for stage, pairs in enumerate(work):
        due = edges.setdefault(min(last for last in sending if last >= stage), set())
        due |= {(of, to) for of in range(nblocks) for pair in pairs[of] for to in pair[2:] if to != of}
    if len(sending) == 2:
        edges = dict(zip(sending, in_two(*[edges[stage] for stage in sending], nblocks)))
    permutes, found = [], []
    for stage, pairs in enumerate(work):
        starting = [move for move in moves if move.begins == stage]
        for needs in sorted({move.needs for move in starting}):
            values = [slots[name] for name in needs]
            if best is not None:
                *values, best = lax.optimization_barrier((*values, best))
            for move in starting:
                if move.needs == needs:
                    value = values[needs.index(move.source)]
                    slots[move.name] = lax.ppermute(value, "blk", move.pairs)
        if stage == 0:
            best = own_block(unit, order, pad_counts, nblocks)
        sends = colored(sorted(edges[stage]), nblocks) if stage in sending else []
        if any(pairs):
            best, *rows = scored(best, found, permutes, slots, rank, pairs, sends)
            found = [lax.ppermute(row, "blk", permute) for row, permute in zip(rows, sends)]
            permutes = sends
    return placed(best, found, permutes, order, pad_counts)


def solution(mesh):
    in_specs = (P(("groups", "blk"), None), P(("groups", "blk")), P("groups"))
    out_specs = P(("groups", "blk"))
    return jax.shard_map(local, mesh=mesh, in_specs=in_specs, out_specs=out_specs, check_vma=False)
```

```python
import functools

import jax
import jax.numpy as jnp
import numpy as np
from jax import lax
from jax.experimental import pallas as pl
from jax.experimental.pallas import tpu as pltpu
from jax.sharding import PartitionSpec as P

STEPS = 6
VMEM = 64 * 2**20 - 2**16
FLOOR = -2.0
MOST_PADS = 256
AHEAD = 2


class Move:
    def __init__(self, name, source, pairs, begins, stage, *after):
        self.name, self.source, self.pairs = name, source, pairs
        self.begins, self.stage, self.needs = begins, stage, (source, *after)


def grid_moves():
    def at(z, y, lane):
        return 4 * z + 2 * y + (y if lane == 0 else 1 - y)

    def rows(links):
        return [
            (at(z, y, lane), at(to, y, land)) for y in (0, 1) for (z, lane), (to, land) in links
        ]

    def across(planes):
        return [(at(z, y, lane), at(z, 1 - y, lane)) for z, lane in planes for y in (0, 1)]

    every = [(z, lane) for z in range(4) for lane in (0, 1)]
    swap = rows([((z, lane), (z, 1 - lane)) for z, lane in every])
    crossed = [(at(1, y, lane), at(1, 1 - y, 1 - lane)) for y in (0, 1) for lane in (0, 1)]
    first = [((0, 0), (2, 1)), ((2, 0), (3, 1)), ((3, 0), (1, 0)), ((1, 0), (0, 0)), ((0, 1), (1, 1))]
    second = [((3, 1), (1, 1)), ((1, 1), (0, 1)), ((2, 1), (3, 0)), ((1, 0), (2, 1))]
    return [
        Move("R1", "own", rows(first), 0, 1),
        Move("R2", "own", rows(second), 0, 1),
        Move("Y", "own", across([place for place in every if place[0] != 1]) + crossed, 0, 1),
        Move("A", "own", swap, 0, 0),
        Move("R3", "own", rows([((1, 1), (2, 0)), ((2, 0), (1, 1))]), 1, 2, "R1"),
        Move("V", "R1", [(at(2, y, 1), at(3, y, 1 - y)) for y in (0, 1)] + across([(1, 1)]), 1, 2),
        Move("F", "Y", swap, 2, 2),
        Move("W", "R1", rows([((1, 0), (1, 1)), ((1, 1), (1, 0))]), 2, 2),
    ]


GRID_PAIRS = (
    ((0, 2), (0, 4), (1, 4), (2, 4), (3, 4)),
    ((0, 1), (0, 5), (1, 3), (1, 5), (3, 5)),
    ((0, 3), (0, 6), (1, 6), (2, 3), (2, 6), (3, 6)),
    ((1, 2), (1, 7), (2, 7), (3, 7)),
    ((1, 12), (4, 5), (4, 6), (4, 7), (6, 12), (7, 12)),
    ((1, 13), (2, 8), (2, 12), (2, 13), (5, 8), (7, 13)),
    ((1, 11), (1, 14), (1, 15), (2, 14), (4, 14)),
    ((2, 5), (2, 15), (4, 15), (5, 6), (5, 7), (5, 15), (6, 7)),
    ((5, 9), (5, 10), (5, 11), (9, 10), (9, 11)),
    ((0, 10), (0, 11), (4, 8), (4, 9), (4, 10), (8, 9), (8, 11)),
    ((3, 8), (3, 9), (7, 8), (7, 9), (7, 10), (7, 11)),
    ((6, 8), (6, 9), (6, 10), (6, 11), (8, 10), (10, 11)),
    ((9, 12), (9, 13), (9, 14), (9, 15), (12, 13), (12, 14), (13, 14), (13, 15)),
    ((0, 12), (0, 13), (0, 14), (0, 15), (8, 12), (8, 13), (8, 14)),
    ((11, 12), (11, 13), (11, 14), (11, 15), (12, 15)),
    ((3, 13), (3, 14), (3, 15), (10, 12), (10, 13), (10, 14), (10, 15), (14, 15)),
)


def ring_moves(count):
    return [
        Move("N%d" % k, "own", [((i + k) % count, i) for i in range(count)], 0, k)
        for k in range(1, STEPS + 1)
    ]


def planned(count):
    if count == 16:
        moves, placed_pairs, sending = grid_moves(), GRID_PAIRS, (1, 2)
    else:
        moves, sending = ring_moves(count), (STEPS,)
        placed_pairs = [[(b, (b + k) % count) for k in range(1, STEPS + 1)] for b in range(count)]
    holds = {"own": {d: d for d in range(count)}}
    stage_of = {"own": 0}
    for move in moves:
        holds[move.name] = {to: holds[move.source][of] for of, to in move.pairs}
        stage_of[move.name] = move.stage
    stages = 1 + max(stage_of.values())
    work = [[[] for _ in range(count)] for _ in range(stages)]
    for device, pairs in enumerate(placed_pairs):
        slot_of = {}
        for slot in sorted(stage_of, key=stage_of.get):
            if device in holds[slot]:
                slot_of.setdefault(holds[slot][device], slot)
        for block, visitor in pairs:
            slot, other = slot_of[block], slot_of[visitor]
            stage = max(stage_of[slot], stage_of[other])
            work[stage][device].append((slot, other, block, visitor))
    scored_pairs = sorted(tuple(sorted(pair)) for pairs in placed_pairs for pair in pairs)
    needed = {tuple(sorted((b, (b + k) % count))) for b in range(count) for k in range(1, STEPS + 1)}
    assert scored_pairs == sorted(needed)
    return moves, work, sending


def colored(edges, count):
    sends, takes = [{} for _ in range(count)], [{} for _ in range(count)]
    for of, to in edges:
        a = next(c for c in range(len(edges)) if c not in sends[of])
        b = next(c for c in range(len(edges)) if c not in takes[to])
        path, node, tables, colour = [], to, (takes, sends), a
        while a != b and colour in tables[0][node]:
            end = tables[0][node][colour]
            path.append(((end, node) if tables[0] is takes else (node, end), colour))
            node, tables, colour = end, tables[::-1], a + b - colour
        for (first, second), colour in path:
            del sends[first][colour], takes[second][colour]
        for (first, second), colour in path:
            sends[first][a + b - colour], takes[second][a + b - colour] = second, first
        sends[of][a], takes[to][a] = to, of
    return [
        [(of, to[c]) for of, to in enumerate(sends) if c in to]
        for c in range(max((c + 1 for to in sends for c in to), default=0))
    ]


def in_two(early, late, count):
    early, late = set(early) - set(late), set(late)

    def degrees(edges):
        return [
            [sum(edge[side] == device for edge in edges) for device in range(count)] for side in (0, 1)
        ]

    most = max(degrees(late)[0] + degrees(late)[1])
    while early:
        busy, taken = degrees(early), degrees(late)
        top = max(busy[0] + busy[1])
        free = [
            (max(busy[0][of], busy[1][to]), busy[0][of] + busy[1][to], of, to)
            for of, to in sorted(early)
            if max(taken[0][of], taken[1][to]) < most and max(busy[0][of], busy[1][to]) == top
        ]
        if not free:
            break
        early.remove(max(free)[2:])
        late.add(max(free)[2:])
    return sorted(early), sorted(late)


def unit_kernel(pads, order, embeddings, unit, value, result, tile, scalars, line, into, out, sems):
    rows = unit.shape[0]
    count = rows // into.shape[0]
    parts = [pl.ds(start, count) for start in range(0, rows, count)]
    loads = [
        pltpu.make_async_copy(embeddings.at[part], value.at[part], into.at[index])
        for index, part in enumerate(parts)
    ]
    stores = [
        pltpu.make_async_copy(result.at[part], unit.at[part], out.at[index])
        for index, part in enumerate(parts)
    ]
    to_scalars = pltpu.make_async_copy(order, scalars, sems.at[0])
    to_line = pltpu.make_async_copy(order, line, sems.at[1])
    to_scalars.start()
    to_line.start()
    for load in loads:
        load.start()
    to_scalars.wait()
    first = scalars[0, 0]
    base = pl.multiple_of((first // 16) * 16, 16)
    filling = pltpu.make_async_copy(embeddings.at[pl.ds(base, 16)], tile, sems.at[2])
    filling.start()
    to_line.wait()
    found = [valid_rows(pads, line, index * count, count) for index in range(len(parts))]
    among = lax.broadcasted_iota(jnp.int32, (16, 1), 0) == first - base
    filling.wait()
    filler = jnp.sum(jnp.where(among, tile[...].astype(jnp.float32), 0.0), axis=0, keepdims=True)
    for index, part in enumerate(parts):
        loads[index].wait()
        chunk = jnp.where(found[index], value[part, :].astype(jnp.float32), filler)
        scale = lax.rsqrt(jnp.sum(chunk * chunk, axis=1, keepdims=True) + 1e-06)
        result[part, :] = (chunk * scale).astype(jnp.bfloat16)
        stores[index].start()
    for store in stores:
        store.wait()


def valid_rows(pads, order, start, count):
    rows = order.shape[1]
    most = min(rows, MOST_PADS)
    valid_count = rows - pads[lax.axis_index("blk")]
    position = rows - most + lax.broadcasted_iota(jnp.int32, (1, most), 1)
    padding = jnp.where(position < valid_count, -1, order[:, rows - most :])
    row = start + lax.broadcasted_iota(jnp.int32, (count, 1), 0)
    return jnp.max(jnp.where(padding == row, 1.0, 0.0), axis=1, keepdims=True) < 1.0


def normalized(embeddings, order, pad_counts):
    rows, depth = embeddings.shape
    chunks = 4
    anywhere = pl.BlockSpec(memory_space=pl.ANY)
    return pl.pallas_call(
        unit_kernel,
        out_shape=jax.ShapeDtypeStruct((rows, depth), jnp.bfloat16),
        in_specs=[pl.BlockSpec(memory_space=pltpu.SMEM), anywhere, anywhere],
        out_specs=anywhere,
        scratch_shapes=[
            pltpu.VMEM((rows, depth), jnp.bfloat16),
            pltpu.VMEM((rows, depth), jnp.bfloat16),
            pltpu.VMEM((16, depth), jnp.bfloat16),
            pltpu.SMEM((1, rows), jnp.int32),
            pltpu.VMEM((1, rows), jnp.int32),
            pltpu.SemaphoreType.DMA((chunks,)),
            pltpu.SemaphoreType.DMA((chunks,)),
            pltpu.SemaphoreType.DMA((3,)),
        ],
        compiler_params=pltpu.CompilerParams(vmem_limit_bytes=VMEM),
        cost_estimate=pl.CostEstimate(
            flops=4 * rows * depth, bytes_accessed=4 * rows * depth, transcendentals=rows
        ),
        name="normalized",
    )(pad_counts, order.reshape(1, rows), embeddings)


def product(left, right):
    return lax.dot_general(left, right, (((1,), (1,)), ((), ())), preferred_element_type=jnp.float32)


def own_kernel(pads, order, unit, best):
    rows = unit.shape[0]
    best[...] = jnp.full(best.shape, FLOOR, jnp.float32)
    valid = valid_rows(pads, order, 0, rows)
    row = lax.broadcasted_iota(jnp.int32, (rows, 1), 0)
    here = pl.ds(lax.axis_index("blk"), 1)
    for start in range(0, rows, 256):
        part = pl.ds(start, 256)
        scores = product(unit[...], unit[part, :])
        column = start + lax.broadcasted_iota(jnp.int32, (1, 256), 1)
        scores = jnp.where(valid & (row != column), scores, FLOOR)
        best[here, part] = jnp.max(scores, axis=0, keepdims=True)


def own_block(unit, order, pad_counts, nblocks):
    rows, depth = unit.shape
    whole = pl.BlockSpec(memory_space=pltpu.VMEM)
    return pl.pallas_call(
        own_kernel,
        out_shape=jax.ShapeDtypeStruct((nblocks, rows), jnp.float32),
        in_specs=[pl.BlockSpec(memory_space=pltpu.SMEM), whole, whole],
        out_specs=whole,
        compiler_params=pltpu.CompilerParams(vmem_limit_bytes=VMEM),
        cost_estimate=pl.CostEstimate(
            flops=2 * rows * rows * depth, bytes_accessed=2 * rows * depth, transcendentals=0
        ),
        name="own_block",
    )(pad_counts, order.reshape(1, rows), unit)


def pairs_kernel(nslots, nrows, ntaken, nloads, npairs, table, best, *refs):
    arrivals, slots, out = refs[:ntaken], refs[ntaken : ntaken + nslots], refs[ntaken + nslots]
    sent, (held, across, sems) = refs[ntaken + nslots + 1 : -3], refs[-3:]
    rows = out.shape[1]
    here = lax.axis_index("blk")
    loads_at = here * (2 + nrows + ntaken + nloads + 5 * npairs) + 2 + nrows + ntaken
    pairs_at = loads_at + nloads
    rows_at = loads_at - nrows - ntaken
    loads, pairs = table[rows_at - 2], table[rows_at - 1]

    def fetch(load):
        @pl.when(load < loads)
        def _():
            wanted = table[loads_at + jnp.minimum(load, nloads - 1)]
            for index, slot in enumerate(slots):
                @pl.when(wanted == index)
                def _(slot=slot):
                    for start in range(0, rows, 256):
                        part = pl.ds(start, 256)
                        pltpu.make_async_copy(slot.at[part], held.at[load, part], sems.at[load]).start()

    for load in range(min(AHEAD, nloads)):
        fetch(load)
    out[...] = best[...]
    own = pl.ds(here, 1)
    for index, row in enumerate(arrivals):
        handed = table[rows_at + nrows + index] > 0
        out[own, :] = jnp.where(handed, jnp.maximum(out[own, :], row[...]), out[own, :])

    @pl.loop(0, pairs)
    def _(step):
        at = pairs_at + 5 * step
        before = jnp.where(step == 0, 0, table[jnp.maximum(at - 1, 0)])

        @pl.loop(before, table[at + 4])
        def _(load):
            pltpu.make_async_copy(slots[0], held.at[load], sems.at[load]).wait()
            fetch(load + AHEAD)

        left, right = table[at], table[at + 1]
        first, second = pl.ds(table[at + 2], 1), pl.ds(table[at + 3], 1)
        for start in range(0, rows, 256):
            part = pl.ds(start, 256)
            scores = product(held[left], held[right, part, :])
            down = jnp.max(scores, axis=0, keepdims=True)
            out[second, part] = jnp.maximum(out[second, part], down)
            along = jnp.maximum(scores[:, :128], scores[:, 128:])
            across[...] = along if start == 0 else jnp.maximum(across[...], along)
        found = jnp.max(across[...].T, axis=0, keepdims=True)
        out[first, :] = jnp.maximum(out[first, :], found)

    for index, row in enumerate(sent):
        row[...] = out[pl.ds(table[rows_at + index], 1), :]


def in_order_of_loads(pairs, rank):
    left, loaded, ordered = list(pairs), [], []
    while left:
        pair = min(
            left,
            key=lambda p: (sum(s not in loaded for s in p[:2]), max(rank[s] for s in p[:2]), p[2:]),
        )
        left.remove(pair)
        loaded += [slot for slot in pair[:2] if slot not in loaded]
        ordered.append((pair, len(loaded)))
    return loaded, ordered


def scored(best, found, permutes, slots, rank, work, sends):
    names = sorted({slot for pairs in work for pair in pairs for slot in pair[:2]})
    plans = [in_order_of_loads(pairs, rank) for pairs in work]
    nloads = max(len(loaded) for loaded, _ in plans)
    npairs = max(len(pairs) for pairs in work)
    table = []
    for device, (loaded, ordered) in enumerate(plans):
        table += [len(loaded), len(ordered)]
        table += [dict(permute).get(device, device) for permute in sends]
        table += [int(device in dict(permute).values()) for permute in permutes]
        table += [names.index(slot) for slot in loaded] + [0] * (nloads - len(loaded))
        for (slot, other, block, visitor), need in ordered:
            table += [loaded.index(slot), loaded.index(other), block, visitor, need]
        table += [0] * (5 * (npairs - len(ordered)))
    given = [slots[name] for name in names]
    rows, depth = given[0].shape
    whole = pl.BlockSpec(memory_space=pltpu.VMEM)
    return pl.pallas_call(
        functools.partial(pairs_kernel, len(given), len(sends), len(found), nloads, npairs),
        out_shape=[jax.ShapeDtypeStruct(best.shape, jnp.float32)]
        + [jax.ShapeDtypeStruct((1, rows), jnp.float32)] * len(sends),
        in_specs=[pl.BlockSpec(memory_space=pltpu.SMEM)]
        + [whole] * (1 + len(found))
        + [pl.BlockSpec(memory_space=pl.ANY)] * len(given),
        out_specs=[whole] * (1 + len(sends)),
        scratch_shapes=[
            pltpu.VMEM((nloads, rows, depth), jnp.bfloat16),
            pltpu.VMEM((rows, 128), jnp.float32),
            pltpu.SemaphoreType.DMA((nloads,)),
        ],
        compiler_params=pltpu.CompilerParams(vmem_limit_bytes=VMEM),
        cost_estimate=pl.CostEstimate(
            flops=2 * npairs * rows * rows * depth,
            bytes_accessed=2 * nloads * rows * depth,
            transcendentals=0,
        ),
        name="scored",
    )(jnp.asarray(np.array(table, np.int32)), best, *found, *given)


def placed_kernel(taken, pads, order, best, *refs):
    found, out = refs[:-1], refs[-1]
    rows = order.shape[1]
    here = lax.axis_index("blk")
    total = best[pl.ds(here, 1), :]
    for index, row in enumerate(found):
        total = jnp.where(taken[here * len(found) + index] > 0, jnp.maximum(total, row[...]), total)
    column = jnp.broadcast_to(total, (128, rows)).T[:, :1]
    row = lax.broadcasted_iota(jnp.int32, (rows, 1), 0)
    in_order = jnp.max(jnp.where(order[...] == row, column, FLOOR), axis=0, keepdims=True)
    position = lax.broadcasted_iota(jnp.int32, (1, rows), 1)
    out[...] = jnp.where(position < rows - pads[here], in_order, 0.0)


def placed(best, found, permutes, order, pad_counts):
    rows = order.shape[0]
    taken = np.zeros((best.shape[0], len(permutes)), np.int32)
    for index, permute in enumerate(permutes):
        taken[[to for _, to in permute], index] = 1
    whole, scalars = pl.BlockSpec(memory_space=pltpu.VMEM), pl.BlockSpec(memory_space=pltpu.SMEM)
    return pl.pallas_call(
        placed_kernel,
        out_shape=jax.ShapeDtypeStruct((1, rows), jnp.float32),
        in_specs=[scalars, scalars] + [whole] * (2 + len(found)),
        out_specs=whole,
        compiler_params=pltpu.CompilerParams(vmem_limit_bytes=VMEM),
        name="placed",
    )(jnp.asarray(taken.reshape(-1)), pad_counts, order.reshape(1, rows), best, *found).reshape(rows)


def local(embeddings, order, pad_counts):
    nblocks = lax.axis_size("blk")
    moves, work, sending = planned(nblocks)
    unit = normalized(embeddings, order, pad_counts)
    slots, best = {"own": unit}, None
    rank = dict({"own": -1}, **{move.name: move.stage for move in moves})
    edges = {}
    for stage, pairs in enumerate(work):
        due = edges.setdefault(min(last for last in sending if last >= stage), set())
        due |= {(of, to) for of in range(nblocks) for pair in pairs[of] for to in pair[2:] if to != of}
    if len(sending) == 2:
        edges = dict(zip(sending, in_two(*[edges[stage] for stage in sending], nblocks)))
    permutes, found = [], []
    for stage, pairs in enumerate(work):
        starting = [move for move in moves if move.begins == stage]
        for needs in sorted({move.needs for move in starting}):
            values = [slots[name] for name in needs]
            if best is not None:
                *values, best = lax.optimization_barrier((*values, best))
            for move in starting:
                if move.needs == needs:
                    value = values[needs.index(move.source)]
                    slots[move.name] = lax.ppermute(value, "blk", move.pairs)
        if stage == 0:
            best = own_block(unit, order, pad_counts, nblocks)
        sends = colored(sorted(edges[stage]), nblocks) if stage in sending else []
        if any(pairs):
            if found:
                *found, best = lax.optimization_barrier((*found, best))
            best, *rows = scored(best, [], [], slots, rank, pairs, sends)
            found += [lax.ppermute(row, "blk", permute) for row, permute in zip(rows, sends)]
            permutes += sends
    return placed(best, found, permutes, order, pad_counts)


def solution(mesh):
    in_specs = (P(("groups", "blk"), None), P(("groups", "blk")), P("groups"))
    out_specs = P(("groups", "blk"))
    return jax.shard_map(local, mesh=mesh, in_specs=in_specs, out_specs=out_specs, check_vma=False)
```

```python
import functools

import jax
import jax.numpy as jnp
import numpy as np
from jax import lax
from jax.experimental import pallas as pl
from jax.experimental.pallas import tpu as pltpu
from jax.sharding import PartitionSpec as P

STEPS = 6
VMEM = 64 * 2**20 - 2**16
FLOOR = -2.0
MOST_PADS = 256
AHEAD = 2


class Move:
    def __init__(self, name, source, pairs, begins, stage, *after):
        self.name, self.source, self.pairs = name, source, pairs
        self.begins, self.stage, self.needs = begins, stage, (source, *after)


def grid_moves():
    def at(z, y, lane):
        return 4 * z + 2 * y + (y if lane == 0 else 1 - y)

    def rows(links):
        return [
            (at(z, y, lane), at(to, y, land)) for y in (0, 1) for (z, lane), (to, land) in links
        ]

    def across(planes):
        return [(at(z, y, lane), at(z, 1 - y, lane)) for z, lane in planes for y in (0, 1)]

    every = [(z, lane) for z in range(4) for lane in (0, 1)]
    swap = rows([((z, lane), (z, 1 - lane)) for z, lane in every])
    crossed = [(at(1, y, lane), at(1, 1 - y, 1 - lane)) for y in (0, 1) for lane in (0, 1)]
    first = [((0, 0), (2, 1)), ((2, 0), (3, 1)), ((3, 0), (1, 0)), ((1, 0), (0, 0)), ((0, 1), (1, 1))]
    second = [((3, 1), (1, 1)), ((1, 1), (0, 1)), ((2, 1), (3, 0)), ((1, 0), (2, 1))]
    return [
        Move("R1", "own", rows(first), 0, 1),
        Move("R2", "own", rows(second), 0, 1),
        Move("Y", "own", across([place for place in every if place[0] != 1]) + crossed, 0, 1),
        Move("A", "own", swap, 0, 0),
        Move("R3", "own", rows([((1, 1), (2, 0)), ((2, 0), (1, 1))]), 1, 2, "R1"),
        Move("V", "R1", [(at(2, y, 1), at(3, y, 1 - y)) for y in (0, 1)] + across([(1, 1)]), 1, 2),
        Move("F", "Y", swap, 2, 2),
        Move("W", "R1", rows([((1, 0), (1, 1)), ((1, 1), (1, 0))]), 2, 2),
    ]


GRID_PAIRS = (
    ((0, 2), (0, 4), (1, 4), (2, 4), (3, 4)),
    ((0, 1), (0, 5), (1, 3), (1, 5), (3, 5)),
    ((0, 3), (0, 6), (1, 6), (2, 3), (2, 6), (3, 6)),
    ((1, 2), (1, 7), (2, 7), (3, 7)),
    ((1, 12), (4, 5), (4, 6), (4, 7), (6, 12), (7, 12)),
    ((1, 13), (2, 8), (2, 12), (2, 13), (5, 8), (7, 13)),
    ((1, 11), (1, 14), (1, 15), (2, 14), (4, 14)),
    ((2, 5), (2, 15), (4, 15), (5, 6), (5, 7), (5, 15), (6, 7)),
    ((5, 9), (5, 10), (5, 11), (9, 10), (9, 11)),
    ((0, 10), (0, 11), (4, 8), (4, 9), (4, 10), (8, 9), (8, 11)),
    ((3, 8), (3, 9), (7, 8), (7, 9), (7, 10), (7, 11)),
    ((6, 8), (6, 9), (6, 10), (6, 11), (8, 10), (10, 11)),
    ((9, 12), (9, 13), (9, 14), (9, 15), (12, 13), (12, 14), (13, 14), (13, 15)),
    ((0, 12), (0, 13), (0, 14), (0, 15), (8, 12), (8, 13), (8, 14)),
    ((11, 12), (11, 13), (11, 14), (11, 15), (12, 15)),
    ((3, 13), (3, 14), (3, 15), (10, 12), (10, 13), (10, 14), (10, 15), (14, 15)),
)


def ring_moves(count):
    return [
        Move("N%d" % k, "own", [((i + k) % count, i) for i in range(count)], 0, k)
        for k in range(1, STEPS + 1)
    ]


def planned(count):
    if count == 16:
        moves, placed_pairs, sending = grid_moves(), GRID_PAIRS, (1, 2)
    else:
        moves, sending = ring_moves(count), (STEPS,)
        placed_pairs = [[(b, (b + k) % count) for k in range(1, STEPS + 1)] for b in range(count)]
    holds = {"own": {d: d for d in range(count)}}
    stage_of = {"own": 0}
    for move in moves:
        holds[move.name] = {to: holds[move.source][of] for of, to in move.pairs}
        stage_of[move.name] = move.stage
    stages = 1 + max(stage_of.values())
    work = [[[] for _ in range(count)] for _ in range(stages)]
    for device, pairs in enumerate(placed_pairs):
        slot_of = {}
        for slot in sorted(stage_of, key=stage_of.get):
            if device in holds[slot]:
                slot_of.setdefault(holds[slot][device], slot)
        for block, visitor in pairs:
            slot, other = slot_of[block], slot_of[visitor]
            stage = max(stage_of[slot], stage_of[other])
            work[stage][device].append((slot, other, block, visitor))
    scored_pairs = sorted(tuple(sorted(pair)) for pairs in placed_pairs for pair in pairs)
    needed = {tuple(sorted((b, (b + k) % count))) for b in range(count) for k in range(1, STEPS + 1)}
    assert scored_pairs == sorted(needed)
    return moves, work, sending


def colored(edges, count):
    sends, takes = [{} for _ in range(count)], [{} for _ in range(count)]
    for of, to in edges:
        a = next(c for c in range(len(edges)) if c not in sends[of])
        b = next(c for c in range(len(edges)) if c not in takes[to])
        path, node, tables, colour = [], to, (takes, sends), a
        while a != b and colour in tables[0][node]:
            end = tables[0][node][colour]
            path.append(((end, node) if tables[0] is takes else (node, end), colour))
            node, tables, colour = end, tables[::-1], a + b - colour
        for (first, second), colour in path:
            del sends[first][colour], takes[second][colour]
        for (first, second), colour in path:
            sends[first][a + b - colour], takes[second][a + b - colour] = second, first
        sends[of][a], takes[to][a] = to, of
    return [
        [(of, to[c]) for of, to in enumerate(sends) if c in to]
        for c in range(max((c + 1 for to in sends for c in to), default=0))
    ]


def in_two(early, late, count):
    early, late = set(early) - set(late), set(late)

    def degrees(edges):
        return [
            [sum(edge[side] == device for edge in edges) for device in range(count)] for side in (0, 1)
        ]

    most = max(degrees(late)[0] + degrees(late)[1])
    while early:
        busy, taken = degrees(early), degrees(late)
        top = max(busy[0] + busy[1])
        free = [
            (max(busy[0][of], busy[1][to]), busy[0][of] + busy[1][to], of, to)
            for of, to in sorted(early)
            if max(taken[0][of], taken[1][to]) < most and max(busy[0][of], busy[1][to]) == top
        ]
        if not free:
            break
        early.remove(max(free)[2:])
        late.add(max(free)[2:])
    return sorted(early), sorted(late)


def unit_kernel(pads, order_smem, order, embeddings, unit, value, result, tile, into, out, sem):
    rows = unit.shape[0]
    count = rows // into.shape[0]
    parts = [pl.ds(start, count) for start in range(0, rows, count)]
    loads = [
        pltpu.make_async_copy(embeddings.at[part], value.at[part], into.at[index])
        for index, part in enumerate(parts)
    ]
    stores = [
        pltpu.make_async_copy(result.at[part], unit.at[part], out.at[index])
        for index, part in enumerate(parts)
    ]
    first = order_smem[0]
    base = pl.multiple_of((first // 16) * 16, 16)
    filling = pltpu.make_async_copy(embeddings.at[pl.ds(base, 16)], tile, sem)
    filling.start()
    for load in loads:
        load.start()
    filling.wait()
    among = lax.broadcasted_iota(jnp.int32, (16, 1), 0) == first - base
    filler = jnp.sum(jnp.where(among, tile[...].astype(jnp.float32), 0.0), axis=0, keepdims=True)
    for index, part in enumerate(parts):
        found = valid_rows(pads, order, index * count, count)
        loads[index].wait()
        chunk = jnp.where(found, value[part, :].astype(jnp.float32), filler)
        scale = lax.rsqrt(jnp.sum(chunk * chunk, axis=1, keepdims=True) + 1e-06)
        result[part, :] = (chunk * scale).astype(jnp.bfloat16)
        stores[index].start()
    for store in stores:
        store.wait()


def valid_rows(pads, order, start, count):
    rows = order.shape[1]
    most = min(rows, MOST_PADS)
    valid_count = rows - pads[lax.axis_index("blk")]
    position = rows - most + lax.broadcasted_iota(jnp.int32, (1, most), 1)
    padding = jnp.where(position < valid_count, -1, order[:, rows - most :])
    row = start + lax.broadcasted_iota(jnp.int32, (count, 1), 0)
    return jnp.max(jnp.where(padding == row, 1.0, 0.0), axis=1, keepdims=True) < 1.0


def normalized(embeddings, order, pad_counts):
    rows, depth = embeddings.shape
    chunks = 4
    scalars = pl.BlockSpec(memory_space=pltpu.SMEM)
    return pl.pallas_call(
        unit_kernel,
        out_shape=jax.ShapeDtypeStruct((rows, depth), jnp.bfloat16),
        in_specs=[
            scalars,
            scalars,
            pl.BlockSpec(memory_space=pltpu.VMEM),
            pl.BlockSpec(memory_space=pl.ANY),
        ],
        out_specs=pl.BlockSpec(memory_space=pl.ANY),
        scratch_shapes=[
            pltpu.VMEM((rows, depth), jnp.bfloat16),
            pltpu.VMEM((rows, depth), jnp.bfloat16),
            pltpu.VMEM((16, depth), jnp.bfloat16),
            pltpu.SemaphoreType.DMA((chunks,)),
            pltpu.SemaphoreType.DMA((chunks,)),
            pltpu.SemaphoreType.DMA,
        ],
        compiler_params=pltpu.CompilerParams(vmem_limit_bytes=VMEM),
        cost_estimate=pl.CostEstimate(
            flops=4 * rows * depth, bytes_accessed=4 * rows * depth, transcendentals=rows
        ),
        name="normalized",
    )(pad_counts, order, order.reshape(1, rows), embeddings)


def product(left, right):
    return lax.dot_general(left, right, (((1,), (1,)), ((), ())), preferred_element_type=jnp.float32)


def own_kernel(pads, order, unit, best):
    rows = unit.shape[0]
    best[...] = jnp.full(best.shape, FLOOR, jnp.float32)
    valid = valid_rows(pads, order, 0, rows)
    row = lax.broadcasted_iota(jnp.int32, (rows, 1), 0)
    here = pl.ds(lax.axis_index("blk"), 1)
    for start in range(0, rows, 256):
        part = pl.ds(start, 256)
        scores = product(unit[...], unit[part, :])
        column = start + lax.broadcasted_iota(jnp.int32, (1, 256), 1)
        scores = jnp.where(valid & (row != column), scores, FLOOR)
        best[here, part] = jnp.max(scores, axis=0, keepdims=True)


def own_block(unit, order, pad_counts, nblocks):
    rows, depth = unit.shape
    whole = pl.BlockSpec(memory_space=pltpu.VMEM)
    return pl.pallas_call(
        own_kernel,
        out_shape=jax.ShapeDtypeStruct((nblocks, rows), jnp.float32),
        in_specs=[pl.BlockSpec(memory_space=pltpu.SMEM), whole, whole],
        out_specs=whole,
        compiler_params=pltpu.CompilerParams(vmem_limit_bytes=VMEM),
        cost_estimate=pl.CostEstimate(
            flops=2 * rows * rows * depth, bytes_accessed=2 * rows * depth, transcendentals=0
        ),
        name="own_block",
    )(pad_counts, order.reshape(1, rows), unit)


def pairs_kernel(nslots, nrows, ntaken, nloads, npairs, table, best, *refs):
    arrivals, slots, out = refs[:ntaken], refs[ntaken : ntaken + nslots], refs[ntaken + nslots]
    sent, (held, across, sems) = refs[ntaken + nslots + 1 : -3], refs[-3:]
    rows = out.shape[1]
    here = lax.axis_index("blk")
    loads_at = here * (2 + nrows + ntaken + nloads + 5 * npairs) + 2 + nrows + ntaken
    pairs_at = loads_at + nloads
    rows_at = loads_at - nrows - ntaken
    loads, pairs = table[rows_at - 2], table[rows_at - 1]

    def fetch(load):
        @pl.when(load < loads)
        def _():
            wanted = table[loads_at + jnp.minimum(load, nloads - 1)]
            for index, slot in enumerate(slots):
                @pl.when(wanted == index)
                def _(slot=slot):
                    for start in range(0, rows, 256):
                        part = pl.ds(start, 256)
                        pltpu.make_async_copy(slot.at[part], held.at[load, part], sems.at[load]).start()

    for load in range(min(AHEAD, nloads)):
        fetch(load)
    out[...] = best[...]
    own = pl.ds(here, 1)
    for index, row in enumerate(arrivals):
        handed = table[rows_at + nrows + index] > 0
        out[own, :] = jnp.where(handed, jnp.maximum(out[own, :], row[...]), out[own, :])

    @pl.loop(0, pairs)
    def _(step):
        at = pairs_at + 5 * step
        before = jnp.where(step == 0, 0, table[jnp.maximum(at - 1, 0)])

        @pl.loop(before, table[at + 4])
        def _(load):
            pltpu.make_async_copy(slots[0], held.at[load], sems.at[load]).wait()
            fetch(load + AHEAD)

        left, right = table[at], table[at + 1]
        first, second = pl.ds(table[at + 2], 1), pl.ds(table[at + 3], 1)
        for start in range(0, rows, 256):
            part = pl.ds(start, 256)
            scores = product(held[left], held[right, part, :])
            down = jnp.max(scores, axis=0, keepdims=True)
            out[second, part] = jnp.maximum(out[second, part], down)
            along = jnp.maximum(scores[:, :128], scores[:, 128:])
            across[...] = along if start == 0 else jnp.maximum(across[...], along)
        found = jnp.max(across[...].T, axis=0, keepdims=True)
        out[first, :] = jnp.maximum(out[first, :], found)

    for index, row in enumerate(sent):
        row[...] = out[pl.ds(table[rows_at + index], 1), :]


def in_order_of_loads(pairs, rank):
    left, loaded, ordered = list(pairs), [], []
    while left:
        pair = min(
            left,
            key=lambda p: (sum(s not in loaded for s in p[:2]), max(rank[s] for s in p[:2]), p[2:]),
        )
        left.remove(pair)
        loaded += [slot for slot in pair[:2] if slot not in loaded]
        ordered.append((pair, len(loaded)))
    return loaded, ordered


def scored(best, found, permutes, slots, rank, work, sends):
    names = sorted({slot for pairs in work for pair in pairs for slot in pair[:2]})
    plans = [in_order_of_loads(pairs, rank) for pairs in work]
    nloads = max(len(loaded) for loaded, _ in plans)
    npairs = max(len(pairs) for pairs in work)
    table = []
    for device, (loaded, ordered) in enumerate(plans):
        table += [len(loaded), len(ordered)]
        table += [dict(permute).get(device, device) for permute in sends]
        table += [int(device in dict(permute).values()) for permute in permutes]
        table += [names.index(slot) for slot in loaded] + [0] * (nloads - len(loaded))
        for (slot, other, block, visitor), need in ordered:
            table += [loaded.index(slot), loaded.index(other), block, visitor, need]
        table += [0] * (5 * (npairs - len(ordered)))
    given = [slots[name] for name in names]
    rows, depth = given[0].shape
    whole = pl.BlockSpec(memory_space=pltpu.VMEM)
    return pl.pallas_call(
        functools.partial(pairs_kernel, len(given), len(sends), len(found), nloads, npairs),
        out_shape=[jax.ShapeDtypeStruct(best.shape, jnp.float32)]
        + [jax.ShapeDtypeStruct((1, rows), jnp.float32)] * len(sends),
        in_specs=[pl.BlockSpec(memory_space=pltpu.SMEM)]
        + [whole] * (1 + len(found))
        + [pl.BlockSpec(memory_space=pl.ANY)] * len(given),
        out_specs=[whole] * (1 + len(sends)),
        scratch_shapes=[
            pltpu.VMEM((nloads, rows, depth), jnp.bfloat16),
            pltpu.VMEM((rows, 128), jnp.float32),
            pltpu.SemaphoreType.DMA((nloads,)),
        ],
        compiler_params=pltpu.CompilerParams(vmem_limit_bytes=VMEM),
        cost_estimate=pl.CostEstimate(
            flops=2 * npairs * rows * rows * depth,
            bytes_accessed=2 * nloads * rows * depth,
            transcendentals=0,
        ),
        name="scored",
    )(jnp.asarray(np.array(table, np.int32)), best, *found, *given)


def placed_kernel(taken, pads, order, best, *refs):
    found, out = refs[:-1], refs[-1]
    rows = order.shape[1]
    here = lax.axis_index("blk")
    total = best[pl.ds(here, 1), :]
    for index, row in enumerate(found):
        total = jnp.where(taken[here * len(found) + index] > 0, jnp.maximum(total, row[...]), total)
    column = jnp.broadcast_to(total, (128, rows)).T[:, :1]
    row = lax.broadcasted_iota(jnp.int32, (rows, 1), 0)
    in_order = jnp.max(jnp.where(order[...] == row, column, FLOOR), axis=0, keepdims=True)
    position = lax.broadcasted_iota(jnp.int32, (1, rows), 1)
    out[...] = jnp.where(position < rows - pads[here], in_order, 0.0)


def placed(best, found, permutes, order, pad_counts):
    rows = order.shape[0]
    taken = np.zeros((best.shape[0], len(permutes)), np.int32)
    for index, permute in enumerate(permutes):
        taken[[to for _, to in permute], index] = 1
    whole, scalars = pl.BlockSpec(memory_space=pltpu.VMEM), pl.BlockSpec(memory_space=pltpu.SMEM)
    return pl.pallas_call(
        placed_kernel,
        out_shape=jax.ShapeDtypeStruct((1, rows), jnp.float32),
        in_specs=[scalars, scalars] + [whole] * (2 + len(found)),
        out_specs=whole,
        compiler_params=pltpu.CompilerParams(vmem_limit_bytes=VMEM),
        name="placed",
    )(jnp.asarray(taken.reshape(-1)), pad_counts, order.reshape(1, rows), best, *found).reshape(rows)


def local(embeddings, order, pad_counts):
    nblocks = lax.axis_size("blk")
    moves, work, sending = planned(nblocks)
    unit = normalized(embeddings, order, pad_counts)
    slots, best = {"own": unit}, None
    rank = dict({"own": -1}, **{move.name: move.stage for move in moves})
    edges = {}
    for stage, pairs in enumerate(work):
        due = edges.setdefault(min(last for last in sending if last >= stage), set())
        due |= {(of, to) for of in range(nblocks) for pair in pairs[of] for to in pair[2:] if to != of}
    if len(sending) == 2:
        edges = dict(zip(sending, in_two(*[edges[stage] for stage in sending], nblocks)))
    permutes, found = [], []
    for stage, pairs in enumerate(work):
        starting = [move for move in moves if move.begins == stage]
        for needs in sorted({move.needs for move in starting}):
            values = [slots[name] for name in needs]
            if best is not None:
                *values, best = lax.optimization_barrier((*values, best))
            for move in starting:
                if move.needs == needs:
                    value = values[needs.index(move.source)]
                    slots[move.name] = lax.ppermute(value, "blk", move.pairs)
        if stage == 0:
            best = own_block(unit, order, pad_counts, nblocks)
        sends = colored(sorted(edges[stage]), nblocks) if stage in sending else []
        if any(pairs):
            best, *rows = scored(best, found, permutes, slots, rank, pairs, sends)
            found = [lax.ppermute(row, "blk", permute) for row, permute in zip(rows, sends)]
            permutes = sends
    return placed(best, found, permutes, order, pad_counts)


def solution(mesh):
    in_specs = (P(("groups", "blk"), None), P(("groups", "blk")), P("groups"))
    out_specs = P(("groups", "blk"))
    return jax.shard_map(local, mesh=mesh, in_specs=in_specs, out_specs=out_specs, check_vma=False)
```

```python
import functools

import jax
import jax.numpy as jnp
import numpy as np
from jax import lax
from jax.experimental import pallas as pl
from jax.experimental.pallas import tpu as pltpu
from jax.sharding import PartitionSpec as P

STEPS = 6
VMEM = 64 * 2**20 - 2**16
FLOOR = -2.0
MOST_PADS = 256
AHEAD = 2
FIRST, EARLY = 4, 3


class Move:
    def __init__(self, name, source, pairs, begins, stage, *after):
        self.name, self.source, self.pairs = name, source, pairs
        self.begins, self.stage, self.needs = begins, stage, (source, *after)


def grid_moves():
    def at(z, y, lane):
        return 4 * z + 2 * y + (y if lane == 0 else 1 - y)

    def rows(links):
        return [
            (at(z, y, lane), at(to, y, land)) for y in (0, 1) for (z, lane), (to, land) in links
        ]

    def across(planes):
        return [(at(z, y, lane), at(z, 1 - y, lane)) for z, lane in planes for y in (0, 1)]

    every = [(z, lane) for z in range(4) for lane in (0, 1)]
    swap = rows([((z, lane), (z, 1 - lane)) for z, lane in every])
    crossed = [(at(1, y, lane), at(1, 1 - y, 1 - lane)) for y in (0, 1) for lane in (0, 1)]
    first = [((0, 0), (2, 1)), ((2, 0), (3, 1)), ((3, 0), (1, 0)), ((1, 0), (0, 0)), ((0, 1), (1, 1))]
    second = [((3, 1), (1, 1)), ((1, 1), (0, 1)), ((2, 1), (3, 0)), ((1, 0), (2, 1))]
    return [
        Move("R1", "own", rows(first), 0, 1),
        Move("R2", "own", rows(second), 0, 1),
        Move("Y", "own", across([place for place in every if place[0] != 1]) + crossed, 0, 1),
        Move("A", "own", swap, 0, 0),
        Move("R3", "own", rows([((1, 1), (2, 0)), ((2, 0), (1, 1))]), 1, 2, "R1"),
        Move("V", "R1", [(at(2, y, 1), at(3, y, 1 - y)) for y in (0, 1)] + across([(1, 1)]), 1, 2),
        Move("F", "Y", swap, 2, 2),
        Move("W", "R1", rows([((1, 0), (1, 1)), ((1, 1), (1, 0))]), 2, 2),
    ]


GRID_PAIRS = (
    ((0, 2), (0, 4), (1, 4), (2, 4), (3, 4)),
    ((0, 1), (0, 5), (1, 3), (1, 5), (3, 5)),
    ((0, 3), (0, 6), (1, 6), (2, 3), (2, 6), (3, 6)),
    ((1, 2), (1, 7), (2, 7), (3, 7)),
    ((1, 12), (4, 5), (4, 6), (4, 7), (6, 12), (7, 12)),
    ((1, 13), (2, 8), (2, 12), (2, 13), (5, 8), (7, 13)),
    ((1, 11), (1, 14), (1, 15), (2, 14), (4, 14)),
    ((2, 5), (2, 15), (4, 15), (5, 6), (5, 7), (5, 15), (6, 7)),
    ((5, 9), (5, 10), (5, 11), (9, 10), (9, 11)),
    ((0, 10), (0, 11), (4, 8), (4, 9), (4, 10), (8, 9), (8, 11)),
    ((3, 8), (3, 9), (7, 8), (7, 9), (7, 10), (7, 11)),
    ((6, 8), (6, 9), (6, 10), (6, 11), (8, 10), (10, 11)),
    ((9, 12), (9, 13), (9, 14), (9, 15), (12, 13), (12, 14), (13, 14), (13, 15)),
    ((0, 12), (0, 13), (0, 14), (0, 15), (8, 12), (8, 13), (8, 14)),
    ((11, 12), (11, 13), (11, 14), (11, 15), (12, 15)),
    ((3, 13), (3, 14), (3, 15), (10, 12), (10, 13), (10, 14), (10, 15), (14, 15)),
)


def ring_moves(count):
    return [
        Move("N%d" % k, "own", [((i + k) % count, i) for i in range(count)], 0, k)
        for k in range(1, STEPS + 1)
    ]


def planned(count):
    if count == 16:
        moves, placed_pairs, sending = grid_moves(), GRID_PAIRS, (1, 2)
    else:
        moves, sending = ring_moves(count), (STEPS,)
        placed_pairs = [[(b, (b + k) % count) for k in range(1, STEPS + 1)] for b in range(count)]
    holds = {"own": {d: d for d in range(count)}}
    stage_of = {"own": 0}
    for move in moves:
        holds[move.name] = {to: holds[move.source][of] for of, to in move.pairs}
        stage_of[move.name] = move.stage
    stages = 1 + max(stage_of.values())
    work = [[[] for _ in range(count)] for _ in range(stages)]
    for device, pairs in enumerate(placed_pairs):
        slot_of = {}
        for slot in sorted(stage_of, key=stage_of.get):
            if device in holds[slot]:
                slot_of.setdefault(holds[slot][device], slot)
        for block, visitor in pairs:
            slot, other = slot_of[block], slot_of[visitor]
            stage = max(stage_of[slot], stage_of[other])
            work[stage][device].append((slot, other, block, visitor))
    scored_pairs = sorted(tuple(sorted(pair)) for pairs in placed_pairs for pair in pairs)
    needed = {tuple(sorted((b, (b + k) % count))) for b in range(count) for k in range(1, STEPS + 1)}
    assert scored_pairs == sorted(needed)
    return moves, work, sending


def colored(edges, count):
    ends = [of for of, _ in edges], [to for _, to in edges]
    most = max((side.count(device) for side in ends for device in range(count)), default=0)
    sends, takes = [{} for _ in range(count)], [{} for _ in range(count)]
    for of, to in sorted(edges, key=lambda edge: (min(edge) >= FIRST, edge)):
        both = next(c for c in range(2 * len(edges)) if c not in sends[of] and c not in takes[to])
        a = next(c for c in range(len(edges)) if c not in sends[of])
        b = next(c for c in range(len(edges)) if c not in takes[to])
        if both < most:
            a = b = both
        path, node, tables, colour = [], to, (takes, sends), a
        while a != b and colour in tables[0][node]:
            end = tables[0][node][colour]
            path.append(((end, node) if tables[0] is takes else (node, end), colour))
            node, tables, colour = end, tables[::-1], a + b - colour
        for (first, second), colour in path:
            del sends[first][colour], takes[second][colour]
        for (first, second), colour in path:
            sends[first][a + b - colour], takes[second][a + b - colour] = second, first
        sends[of][a], takes[to][a] = to, of
    return [
        [(of, to[c]) for of, to in enumerate(sends) if c in to]
        for c in range(max((c + 1 for to in sends for c in to), default=0))
    ]


def in_two(early, late, count):
    early, late = set(early) - set(late), set(late)

    def degrees(edges):
        return [
            [sum(edge[side] == device for edge in edges) for device in range(count)] for side in (0, 1)
        ]

    most = max(degrees(late)[0] + degrees(late)[1])
    while early:
        busy, taken = degrees(early), degrees(late)
        top = max(busy[0] + busy[1])
        free = [
            (min(of, to) >= FIRST, max(busy[0][of], busy[1][to]), busy[0][of] + busy[1][to], of, to)
            for of, to in sorted(early)
            if max(taken[0][of], taken[1][to]) < most and max(busy[0][of], busy[1][to]) == top
        ]
        if not free or top <= EARLY:
            break
        early.remove(max(free)[3:])
        late.add(max(free)[3:])
    return sorted(early), sorted(late)


def unit_kernel(pads, order_smem, order, embeddings, unit, value, result, tile, into, out, sem):
    rows = unit.shape[0]
    count = rows // into.shape[0]
    parts = [pl.ds(start, count) for start in range(0, rows, count)]
    loads = [
        pltpu.make_async_copy(embeddings.at[part], value.at[part], into.at[index])
        for index, part in enumerate(parts)
    ]
    stores = [
        pltpu.make_async_copy(result.at[part], unit.at[part], out.at[index])
        for index, part in enumerate(parts)
    ]
    first = order_smem[0]
    base = pl.multiple_of((first // 16) * 16, 16)
    filling = pltpu.make_async_copy(embeddings.at[pl.ds(base, 16)], tile, sem)
    filling.start()
    for load in loads:
        load.start()
    filling.wait()
    among = lax.broadcasted_iota(jnp.int32, (16, 1), 0) == first - base
    filler = jnp.sum(jnp.where(among, tile[...].astype(jnp.float32), 0.0), axis=0, keepdims=True)
    for index, part in enumerate(parts):
        found = valid_rows(pads, order, index * count, count)
        loads[index].wait()
        chunk = jnp.where(found, value[part, :].astype(jnp.float32), filler)
        scale = lax.rsqrt(jnp.sum(chunk * chunk, axis=1, keepdims=True) + 1e-06)
        result[part, :] = (chunk * scale).astype(jnp.bfloat16)
        stores[index].start()
    for store in stores:
        store.wait()


def valid_rows(pads, order, start, count):
    rows = order.shape[1]
    most = min(rows, MOST_PADS)
    valid_count = rows - pads[lax.axis_index("blk")]
    position = rows - most + lax.broadcasted_iota(jnp.int32, (1, most), 1)
    padding = jnp.where(position < valid_count, -1, order[:, rows - most :])
    row = start + lax.broadcasted_iota(jnp.int32, (count, 1), 0)
    return jnp.max(jnp.where(padding == row, 1.0, 0.0), axis=1, keepdims=True) < 1.0


def normalized(embeddings, order, pad_counts):
    rows, depth = embeddings.shape
    chunks = 4
    scalars = pl.BlockSpec(memory_space=pltpu.SMEM)
    return pl.pallas_call(
        unit_kernel,
        out_shape=jax.ShapeDtypeStruct((rows, depth), jnp.bfloat16),
        in_specs=[
            scalars,
            scalars,
            pl.BlockSpec(memory_space=pltpu.VMEM),
            pl.BlockSpec(memory_space=pl.ANY),
        ],
        out_specs=pl.BlockSpec(memory_space=pl.ANY),
        scratch_shapes=[
            pltpu.VMEM((rows, depth), jnp.bfloat16),
            pltpu.VMEM((rows, depth), jnp.bfloat16),
            pltpu.VMEM((16, depth), jnp.bfloat16),
            pltpu.SemaphoreType.DMA((chunks,)),
            pltpu.SemaphoreType.DMA((chunks,)),
            pltpu.SemaphoreType.DMA,
        ],
        compiler_params=pltpu.CompilerParams(vmem_limit_bytes=VMEM),
        cost_estimate=pl.CostEstimate(
            flops=4 * rows * depth, bytes_accessed=4 * rows * depth, transcendentals=rows
        ),
        name="normalized",
    )(pad_counts, order, order.reshape(1, rows), embeddings)


def product(left, right):
    return lax.dot_general(left, right, (((1,), (1,)), ((), ())), preferred_element_type=jnp.float32)


def own_kernel(pads, order, unit, best):
    rows = unit.shape[0]
    best[...] = jnp.full(best.shape, FLOOR, jnp.float32)
    valid = valid_rows(pads, order, 0, rows)
    row = lax.broadcasted_iota(jnp.int32, (rows, 1), 0)
    here = pl.ds(lax.axis_index("blk"), 1)
    for start in range(0, rows, 256):
        part = pl.ds(start, 256)
        scores = product(unit[...], unit[part, :])
        column = start + lax.broadcasted_iota(jnp.int32, (1, 256), 1)
        scores = jnp.where(valid & (row != column), scores, FLOOR)
        best[here, part] = jnp.max(scores, axis=0, keepdims=True)


def own_block(unit, order, pad_counts, nblocks):
    rows, depth = unit.shape
    whole = pl.BlockSpec(memory_space=pltpu.VMEM)
    return pl.pallas_call(
        own_kernel,
        out_shape=jax.ShapeDtypeStruct((nblocks, rows), jnp.float32),
        in_specs=[pl.BlockSpec(memory_space=pltpu.SMEM), whole, whole],
        out_specs=whole,
        compiler_params=pltpu.CompilerParams(vmem_limit_bytes=VMEM),
        cost_estimate=pl.CostEstimate(
            flops=2 * rows * rows * depth, bytes_accessed=2 * rows * depth, transcendentals=0
        ),
        name="own_block",
    )(pad_counts, order.reshape(1, rows), unit)


def pairs_kernel(nslots, nrows, ntaken, nloads, npairs, table, best, *refs):
    arrivals, slots, out = refs[:ntaken], refs[ntaken : ntaken + nslots], refs[ntaken + nslots]
    sent, (held, across, sems) = refs[ntaken + nslots + 1 : -3], refs[-3:]
    rows = out.shape[1]
    here = lax.axis_index("blk")
    loads_at = here * (2 + nrows + ntaken + nloads + 5 * npairs) + 2 + nrows + ntaken
    pairs_at = loads_at + nloads
    rows_at = loads_at - nrows - ntaken
    loads, pairs = table[rows_at - 2], table[rows_at - 1]

    def fetch(load):
        @pl.when(load < loads)
        def _():
            wanted = table[loads_at + jnp.minimum(load, nloads - 1)]
            for index, slot in enumerate(slots):
                @pl.when(wanted == index)
                def _(slot=slot):
                    for start in range(0, rows, 256):
                        part = pl.ds(start, 256)
                        pltpu.make_async_copy(slot.at[part], held.at[load, part], sems.at[load]).start()

    for load in range(min(AHEAD, nloads)):
        fetch(load)
    out[...] = best[...]
    own = pl.ds(here, 1)
    for index, row in enumerate(arrivals):
        handed = table[rows_at + nrows + index] > 0
        out[own, :] = jnp.where(handed, jnp.maximum(out[own, :], row[...]), out[own, :])

    @pl.loop(0, pairs)
    def _(step):
        at = pairs_at + 5 * step
        before = jnp.where(step == 0, 0, table[jnp.maximum(at - 1, 0)])

        @pl.loop(before, table[at + 4])
        def _(load):
            pltpu.make_async_copy(slots[0], held.at[load], sems.at[load]).wait()
            fetch(load + AHEAD)

        left, right = table[at], table[at + 1]
        first, second = pl.ds(table[at + 2], 1), pl.ds(table[at + 3], 1)
        for start in range(0, rows, 256):
            part = pl.ds(start, 256)
            scores = product(held[left], held[right, part, :])
            down = jnp.max(scores, axis=0, keepdims=True)
            out[second, part] = jnp.maximum(out[second, part], down)
            along = jnp.maximum(scores[:, :128], scores[:, 128:])
            across[...] = along if start == 0 else jnp.maximum(across[...], along)
        found = jnp.max(across[...].T, axis=0, keepdims=True)
        out[first, :] = jnp.maximum(out[first, :], found)

    for index, row in enumerate(sent):
        row[...] = out[pl.ds(table[rows_at + index], 1), :]


def in_order_of_loads(pairs, rank):
    left, loaded, ordered = list(pairs), [], []
    while left:
        pair = min(
            left,
            key=lambda p: (sum(s not in loaded for s in p[:2]), max(rank[s] for s in p[:2]), p[2:]),
        )
        left.remove(pair)
        loaded += [slot for slot in pair[:2] if slot not in loaded]
        ordered.append((pair, len(loaded)))
    return loaded, ordered


def scored(best, found, permutes, slots, rank, work, sends):
    names = sorted({slot for pairs in work for pair in pairs for slot in pair[:2]})
    plans = [in_order_of_loads(pairs, rank) for pairs in work]
    nloads = max(len(loaded) for loaded, _ in plans)
    npairs = max(len(pairs) for pairs in work)
    table = []
    for device, (loaded, ordered) in enumerate(plans):
        table += [len(loaded), len(ordered)]
        table += [dict(permute).get(device, device) for permute in sends]
        table += [int(device in dict(permute).values()) for permute in permutes]
        table += [names.index(slot) for slot in loaded] + [0] * (nloads - len(loaded))
        for (slot, other, block, visitor), need in ordered:
            table += [loaded.index(slot), loaded.index(other), block, visitor, need]
        table += [0] * (5 * (npairs - len(ordered)))
    given = [slots[name] for name in names]
    rows, depth = given[0].shape
    whole = pl.BlockSpec(memory_space=pltpu.VMEM)
    return pl.pallas_call(
        functools.partial(pairs_kernel, len(given), len(sends), len(found), nloads, npairs),
        out_shape=[jax.ShapeDtypeStruct(best.shape, jnp.float32)]
        + [jax.ShapeDtypeStruct((1, rows), jnp.float32)] * len(sends),
        in_specs=[pl.BlockSpec(memory_space=pltpu.SMEM)]
        + [whole] * (1 + len(found))
        + [pl.BlockSpec(memory_space=pl.ANY)] * len(given),
        out_specs=[whole] * (1 + len(sends)),
        scratch_shapes=[
            pltpu.VMEM((nloads, rows, depth), jnp.bfloat16),
            pltpu.VMEM((rows, 128), jnp.float32),
            pltpu.SemaphoreType.DMA((nloads,)),
        ],
        compiler_params=pltpu.CompilerParams(vmem_limit_bytes=VMEM),
        cost_estimate=pl.CostEstimate(
            flops=2 * npairs * rows * rows * depth,
            bytes_accessed=2 * nloads * rows * depth,
            transcendentals=0,
        ),
        name="scored",
    )(jnp.asarray(np.array(table, np.int32)), best, *found, *given)


def placed_kernel(taken, pads, order, best, *refs):
    found, out = refs[:-1], refs[-1]
    rows = order.shape[1]
    here = lax.axis_index("blk")
    total = best[pl.ds(here, 1), :]
    for index, row in enumerate(found):
        total = jnp.where(taken[here * len(found) + index] > 0, jnp.maximum(total, row[...]), total)
    column = jnp.broadcast_to(total, (128, rows)).T[:, :1]
    row = lax.broadcasted_iota(jnp.int32, (rows, 1), 0)
    in_order = jnp.max(jnp.where(order[...] == row, column, FLOOR), axis=0, keepdims=True)
    position = lax.broadcasted_iota(jnp.int32, (1, rows), 1)
    out[...] = jnp.where(position < rows - pads[here], in_order, 0.0)


def placed(best, found, permutes, order, pad_counts):
    rows = order.shape[0]
    taken = np.zeros((best.shape[0], len(permutes)), np.int32)
    for index, permute in enumerate(permutes):
        taken[[to for _, to in permute], index] = 1
    whole, scalars = pl.BlockSpec(memory_space=pltpu.VMEM), pl.BlockSpec(memory_space=pltpu.SMEM)
    return pl.pallas_call(
        placed_kernel,
        out_shape=jax.ShapeDtypeStruct((1, rows), jnp.float32),
        in_specs=[scalars, scalars] + [whole] * (2 + len(found)),
        out_specs=whole,
        compiler_params=pltpu.CompilerParams(vmem_limit_bytes=VMEM),
        name="placed",
    )(jnp.asarray(taken.reshape(-1)), pad_counts, order.reshape(1, rows), best, *found).reshape(rows)


def local(embeddings, order, pad_counts):
    nblocks = lax.axis_size("blk")
    moves, work, sending = planned(nblocks)
    unit = normalized(embeddings, order, pad_counts)
    slots, best = {"own": unit}, None
    rank = dict({"own": -1}, **{move.name: move.stage for move in moves})
    edges = {}
    for stage, pairs in enumerate(work):
        due = edges.setdefault(min(last for last in sending if last >= stage), set())
        due |= {(of, to) for of in range(nblocks) for pair in pairs[of] for to in pair[2:] if to != of}
    if len(sending) == 2:
        edges = dict(zip(sending, in_two(*[edges[stage] for stage in sending], nblocks)))
    permutes, found = [], []
    for stage, pairs in enumerate(work):
        starting = [move for move in moves if move.begins == stage]
        for needs in sorted({move.needs for move in starting}):
            values = [slots[name] for name in needs]
            if best is not None:
                *values, best = lax.optimization_barrier((*values, best))
            for move in starting:
                if move.needs == needs:
                    value = values[needs.index(move.source)]
                    slots[move.name] = lax.ppermute(value, "blk", move.pairs)
        if stage == 0:
            best = own_block(unit, order, pad_counts, nblocks)
        sends = colored(sorted(edges[stage]), nblocks) if stage in sending else []
        if any(pairs):
            best, *rows = scored(best, found, permutes, slots, rank, pairs, sends)
            found = [lax.ppermute(row, "blk", permute) for row, permute in zip(rows, sends)]
            permutes = sends
    return placed(best, found, permutes, order, pad_counts)


def solution(mesh):
    in_specs = (P(("groups", "blk"), None), P(("groups", "blk")), P("groups"))
    out_specs = P(("groups", "blk"))
    return jax.shard_map(local, mesh=mesh, in_specs=in_specs, out_specs=out_specs, check_vma=False)
```

```python
import functools

import jax
import jax.numpy as jnp
import numpy as np
from jax import lax
from jax.experimental import pallas as pl
from jax.experimental.pallas import tpu as pltpu
from jax.sharding import PartitionSpec as P

STEPS = 6
VMEM = 64 * 2**20 - 2**16
FLOOR = -2.0
MOST_PADS = 256
AHEAD = 2
FIRST, EARLY = 2, 2


class Move:
    def __init__(self, name, source, pairs, begins, stage, *after):
        self.name, self.source, self.pairs = name, source, pairs
        self.begins, self.stage, self.needs = begins, stage, (source, *after)


def grid_moves():
    def at(z, y, lane):
        return 4 * z + 2 * y + (y if lane == 0 else 1 - y)

    def rows(links):
        return [
            (at(z, y, lane), at(to, y, land)) for y in (0, 1) for (z, lane), (to, land) in links
        ]

    def across(planes):
        return [(at(z, y, lane), at(z, 1 - y, lane)) for z, lane in planes for y in (0, 1)]

    every = [(z, lane) for z in range(4) for lane in (0, 1)]
    swap = rows([((z, lane), (z, 1 - lane)) for z, lane in every])
    crossed = [(at(1, y, lane), at(1, 1 - y, 1 - lane)) for y in (0, 1) for lane in (0, 1)]
    first = [((0, 0), (2, 1)), ((2, 0), (3, 1)), ((3, 0), (1, 0)), ((1, 0), (0, 0)), ((0, 1), (1, 1))]
    second = [((3, 1), (1, 1)), ((1, 1), (0, 1)), ((2, 1), (3, 0)), ((1, 0), (2, 1))]
    return [
        Move("R1", "own", rows(first), 0, 1),
        Move("R2", "own", rows(second), 0, 1),
        Move("Y", "own", across([place for place in every if place[0] != 1]) + crossed, 0, 1),
        Move("A", "own", swap, 0, 0),
        Move("R3", "own", rows([((1, 1), (2, 0)), ((2, 0), (1, 1))]), 1, 2, "R1"),
        Move("V", "R1", [(at(2, y, 1), at(3, y, 1 - y)) for y in (0, 1)] + across([(1, 1)]), 1, 2),
        Move("F", "Y", swap, 2, 2),
        Move("W", "R1", rows([((1, 0), (1, 1)), ((1, 1), (1, 0))]), 2, 2),
    ]


GRID_PAIRS = (
    ((0, 2), (0, 4), (1, 4), (2, 4), (3, 4)),
    ((0, 1), (0, 5), (1, 3), (1, 5), (3, 5)),
    ((0, 3), (0, 6), (1, 6), (2, 3), (2, 6), (3, 6)),
    ((1, 2), (1, 7), (2, 7), (3, 7)),
    ((1, 12), (4, 5), (4, 6), (4, 7), (6, 12), (7, 12)),
    ((1, 13), (2, 8), (2, 12), (2, 13), (5, 8), (7, 13)),
    ((1, 11), (1, 14), (1, 15), (2, 14), (4, 14)),
    ((2, 5), (2, 15), (4, 15), (5, 6), (5, 7), (5, 15), (6, 7)),
    ((5, 9), (5, 10), (5, 11), (9, 10), (9, 11)),
    ((0, 10), (0, 11), (4, 8), (4, 9), (4, 10), (8, 9), (8, 11)),
    ((3, 8), (3, 9), (7, 8), (7, 9), (7, 10), (7, 11)),
    ((6, 8), (6, 9), (6, 10), (6, 11), (8, 10), (10, 11)),
    ((9, 12), (9, 13), (9, 14), (9, 15), (12, 13), (12, 14), (13, 14), (13, 15)),
    ((0, 12), (0, 13), (0, 14), (0, 15), (8, 12), (8, 13), (8, 14)),
    ((11, 12), (11, 13), (11, 14), (11, 15), (12, 15)),
    ((3, 13), (3, 14), (3, 15), (10, 12), (10, 13), (10, 14), (10, 15), (14, 15)),
)


def ring_moves(count):
    return [
        Move("N%d" % k, "own", [((i + k) % count, i) for i in range(count)], 0, k)
        for k in range(1, STEPS + 1)
    ]


def planned(count):
    if count == 16:
        moves, placed_pairs, sending = grid_moves(), GRID_PAIRS, (1, 2)
    else:
        moves, sending = ring_moves(count), (STEPS,)
        placed_pairs = [[(b, (b + k) % count) for k in range(1, STEPS + 1)] for b in range(count)]
    holds = {"own": {d: d for d in range(count)}}
    stage_of = {"own": 0}
    for move in moves:
        holds[move.name] = {to: holds[move.source][of] for of, to in move.pairs}
        stage_of[move.name] = move.stage
    stages = 1 + max(stage_of.values())
    work = [[[] for _ in range(count)] for _ in range(stages)]
    for device, pairs in enumerate(placed_pairs):
        slot_of = {}
        for slot in sorted(stage_of, key=stage_of.get):
            if device in holds[slot]:
                slot_of.setdefault(holds[slot][device], slot)
        for block, visitor in pairs:
            slot, other = slot_of[block], slot_of[visitor]
            stage = max(stage_of[slot], stage_of[other])
            work[stage][device].append((slot, other, block, visitor))
    scored_pairs = sorted(tuple(sorted(pair)) for pairs in placed_pairs for pair in pairs)
    needed = {tuple(sorted((b, (b + k) % count))) for b in range(count) for k in range(1, STEPS + 1)}
    assert scored_pairs == sorted(needed)
    return moves, work, sending


def colored(edges, count):
    ends = [of for of, _ in edges], [to for _, to in edges]
    most = max((side.count(device) for side in ends for device in range(count)), default=0)
    sends, takes = [{} for _ in range(count)], [{} for _ in range(count)]
    for of, to in sorted(edges, key=lambda edge: (min(edge) >= FIRST, edge)):
        both = next(c for c in range(2 * len(edges)) if c not in sends[of] and c not in takes[to])
        a = next(c for c in range(len(edges)) if c not in sends[of])
        b = next(c for c in range(len(edges)) if c not in takes[to])
        if both < most:
            a = b = both
        path, node, tables, colour = [], to, (takes, sends), a
        while a != b and colour in tables[0][node]:
            end = tables[0][node][colour]
            path.append(((end, node) if tables[0] is takes else (node, end), colour))
            node, tables, colour = end, tables[::-1], a + b - colour
        for (first, second), colour in path:
            del sends[first][colour], takes[second][colour]
        for (first, second), colour in path:
            sends[first][a + b - colour], takes[second][a + b - colour] = second, first
        sends[of][a], takes[to][a] = to, of
    return [
        [(of, to[c]) for of, to in enumerate(sends) if c in to]
        for c in range(max((c + 1 for to in sends for c in to), default=0))
    ]


def in_two(early, late, count):
    early, late = set(early) - set(late), set(late)

    def degrees(edges):
        return [
            [sum(edge[side] == device for edge in edges) for device in range(count)] for side in (0, 1)
        ]

    most = max(degrees(late)[0] + degrees(late)[1])
    while early:
        busy, taken = degrees(early), degrees(late)
        top = max(busy[0] + busy[1])
        free = [
            (min(of, to) >= FIRST, max(busy[0][of], busy[1][to]), busy[0][of] + busy[1][to], of, to)
            for of, to in sorted(early)
            if max(taken[0][of], taken[1][to]) < most and max(busy[0][of], busy[1][to]) == top
        ]
        if not free or top <= EARLY:
            break
        early.remove(max(free)[3:])
        late.add(max(free)[3:])
    return sorted(early), sorted(late)


def unit_kernel(pads, order_smem, order, embeddings, unit, value, result, tile, into, out, sem):
    rows = unit.shape[0]
    count = rows // into.shape[0]
    parts = [pl.ds(start, count) for start in range(0, rows, count)]
    loads = [
        pltpu.make_async_copy(embeddings.at[part], value.at[part], into.at[index])
        for index, part in enumerate(parts)
    ]
    stores = [
        pltpu.make_async_copy(result.at[part], unit.at[part], out.at[index])
        for index, part in enumerate(parts)
    ]
    first = order_smem[0]
    base = pl.multiple_of((first // 16) * 16, 16)
    filling = pltpu.make_async_copy(embeddings.at[pl.ds(base, 16)], tile, sem)
    filling.start()
    for load in loads:
        load.start()
    filling.wait()
    among = lax.broadcasted_iota(jnp.int32, (16, 1), 0) == first - base
    filler = jnp.sum(jnp.where(among, tile[...].astype(jnp.float32), 0.0), axis=0, keepdims=True)
    for index, part in enumerate(parts):
        found = valid_rows(pads, order, index * count, count)
        loads[index].wait()
        chunk = jnp.where(found, value[part, :].astype(jnp.float32), filler)
        scale = lax.rsqrt(jnp.sum(chunk * chunk, axis=1, keepdims=True) + 1e-06)
        result[part, :] = (chunk * scale).astype(jnp.bfloat16)
        stores[index].start()
    for store in stores:
        store.wait()


def valid_rows(pads, order, start, count):
    rows = order.shape[1]
    most = min(rows, MOST_PADS)
    valid_count = rows - pads[lax.axis_index("blk")]
    position = rows - most + lax.broadcasted_iota(jnp.int32, (1, most), 1)
    padding = jnp.where(position < valid_count, -1, order[:, rows - most :])
    row = start + lax.broadcasted_iota(jnp.int32, (count, 1), 0)
    return jnp.max(jnp.where(padding == row, 1.0, 0.0), axis=1, keepdims=True) < 1.0


def normalized(embeddings, order, pad_counts):
    rows, depth = embeddings.shape
    chunks = 4
    scalars = pl.BlockSpec(memory_space=pltpu.SMEM)
    return pl.pallas_call(
        unit_kernel,
        out_shape=jax.ShapeDtypeStruct((rows, depth), jnp.bfloat16),
        in_specs=[
            scalars,
            scalars,
            pl.BlockSpec(memory_space=pltpu.VMEM),
            pl.BlockSpec(memory_space=pl.ANY),
        ],
        out_specs=pl.BlockSpec(memory_space=pl.ANY),
        scratch_shapes=[
            pltpu.VMEM((rows, depth), jnp.bfloat16),
            pltpu.VMEM((rows, depth), jnp.bfloat16),
            pltpu.VMEM((16, depth), jnp.bfloat16),
            pltpu.SemaphoreType.DMA((chunks,)),
            pltpu.SemaphoreType.DMA((chunks,)),
            pltpu.SemaphoreType.DMA,
        ],
        compiler_params=pltpu.CompilerParams(vmem_limit_bytes=VMEM),
        cost_estimate=pl.CostEstimate(
            flops=4 * rows * depth, bytes_accessed=4 * rows * depth, transcendentals=rows
        ),
        name="normalized",
    )(pad_counts, order, order.reshape(1, rows), embeddings)


def product(left, right):
    return lax.dot_general(left, right, (((1,), (1,)), ((), ())), preferred_element_type=jnp.float32)


def own_kernel(pads, order, unit, best):
    rows = unit.shape[0]
    best[...] = jnp.full(best.shape, FLOOR, jnp.float32)
    valid = valid_rows(pads, order, 0, rows)
    row = lax.broadcasted_iota(jnp.int32, (rows, 1), 0)
    here = pl.ds(lax.axis_index("blk"), 1)
    for start in range(0, rows, 256):
        part = pl.ds(start, 256)
        scores = product(unit[...], unit[part, :])
        column = start + lax.broadcasted_iota(jnp.int32, (1, 256), 1)
        scores = jnp.where(valid & (row != column), scores, FLOOR)
        best[here, part] = jnp.max(scores, axis=0, keepdims=True)


def own_block(unit, order, pad_counts, nblocks):
    rows, depth = unit.shape
    whole = pl.BlockSpec(memory_space=pltpu.VMEM)
    return pl.pallas_call(
        own_kernel,
        out_shape=jax.ShapeDtypeStruct((nblocks, rows), jnp.float32),
        in_specs=[pl.BlockSpec(memory_space=pltpu.SMEM), whole, whole],
        out_specs=whole,
        compiler_params=pltpu.CompilerParams(vmem_limit_bytes=VMEM),
        cost_estimate=pl.CostEstimate(
            flops=2 * rows * rows * depth, bytes_accessed=2 * rows * depth, transcendentals=0
        ),
        name="own_block",
    )(pad_counts, order.reshape(1, rows), unit)


def pairs_kernel(nslots, nrows, ntaken, nloads, npairs, table, best, *refs):
    arrivals, slots, out = refs[:ntaken], refs[ntaken : ntaken + nslots], refs[ntaken + nslots]
    sent, (held, across, sems) = refs[ntaken + nslots + 1 : -3], refs[-3:]
    rows = out.shape[1]
    here = lax.axis_index("blk")
    loads_at = here * (2 + nrows + ntaken + nloads + 5 * npairs) + 2 + nrows + ntaken
    pairs_at = loads_at + nloads
    rows_at = loads_at - nrows - ntaken
    loads, pairs = table[rows_at - 2], table[rows_at - 1]

    def fetch(load):
        @pl.when(load < loads)
        def _():
            wanted = table[loads_at + jnp.minimum(load, nloads - 1)]
            for index, slot in enumerate(slots):
                @pl.when(wanted == index)
                def _(slot=slot):
                    for start in range(0, rows, 256):
                        part = pl.ds(start, 256)
                        pltpu.make_async_copy(slot.at[part], held.at[load, part], sems.at[load]).start()

    for load in range(min(AHEAD, nloads)):
        fetch(load)
    out[...] = best[...]
    own = pl.ds(here, 1)
    for index, row in enumerate(arrivals):
        handed = table[rows_at + nrows + index] > 0
        out[own, :] = jnp.where(handed, jnp.maximum(out[own, :], row[...]), out[own, :])

    @pl.loop(0, pairs)
    def _(step):
        at = pairs_at + 5 * step
        before = jnp.where(step == 0, 0, table[jnp.maximum(at - 1, 0)])

        @pl.loop(before, table[at + 4])
        def _(load):
            pltpu.make_async_copy(slots[0], held.at[load], sems.at[load]).wait()
            fetch(load + AHEAD)

        left, right = table[at], table[at + 1]
        first, second = pl.ds(table[at + 2], 1), pl.ds(table[at + 3], 1)
        for start in range(0, rows, 256):
            part = pl.ds(start, 256)
            scores = product(held[left], held[right, part, :])
            down = jnp.max(scores, axis=0, keepdims=True)
            out[second, part] = jnp.maximum(out[second, part], down)
            along = jnp.maximum(scores[:, :128], scores[:, 128:])
            across[...] = along if start == 0 else jnp.maximum(across[...], along)
        found = jnp.max(across[...].T, axis=0, keepdims=True)
        out[first, :] = jnp.maximum(out[first, :], found)

    for index, row in enumerate(sent):
        row[...] = out[pl.ds(table[rows_at + index], 1), :]


def in_order_of_loads(pairs, rank):
    left, loaded, ordered = list(pairs), [], []
    while left:
        pair = min(
            left,
            key=lambda p: (sum(s not in loaded for s in p[:2]), max(rank[s] for s in p[:2]), p[2:]),
        )
        left.remove(pair)
        loaded += [slot for slot in pair[:2] if slot not in loaded]
        ordered.append((pair, len(loaded)))
    return loaded, ordered


def scored(best, found, permutes, slots, rank, work, sends):
    names = sorted({slot for pairs in work for pair in pairs for slot in pair[:2]})
    plans = [in_order_of_loads(pairs, rank) for pairs in work]
    nloads = max(len(loaded) for loaded, _ in plans)
    npairs = max(len(pairs) for pairs in work)
    table = []
    for device, (loaded, ordered) in enumerate(plans):
        table += [len(loaded), len(ordered)]
        table += [dict(permute).get(device, device) for permute in sends]
        table += [int(device in dict(permute).values()) for permute in permutes]
        table += [names.index(slot) for slot in loaded] + [0] * (nloads - len(loaded))
        for (slot, other, block, visitor), need in ordered:
            table += [loaded.index(slot), loaded.index(other), block, visitor, need]
        table += [0] * (5 * (npairs - len(ordered)))
    given = [slots[name] for name in names]
    rows, depth = given[0].shape
    whole = pl.BlockSpec(memory_space=pltpu.VMEM)
    return pl.pallas_call(
        functools.partial(pairs_kernel, len(given), len(sends), len(found), nloads, npairs),
        out_shape=[jax.ShapeDtypeStruct(best.shape, jnp.float32)]
        + [jax.ShapeDtypeStruct((1, rows), jnp.float32)] * len(sends),
        in_specs=[pl.BlockSpec(memory_space=pltpu.SMEM)]
        + [whole] * (1 + len(found))
        + [pl.BlockSpec(memory_space=pl.ANY)] * len(given),
        out_specs=[whole] * (1 + len(sends)),
        scratch_shapes=[
            pltpu.VMEM((nloads, rows, depth), jnp.bfloat16),
            pltpu.VMEM((rows, 128), jnp.float32),
            pltpu.SemaphoreType.DMA((nloads,)),
        ],
        compiler_params=pltpu.CompilerParams(vmem_limit_bytes=VMEM),
        cost_estimate=pl.CostEstimate(
            flops=2 * npairs * rows * rows * depth,
            bytes_accessed=2 * nloads * rows * depth,
            transcendentals=0,
        ),
        name="scored",
    )(jnp.asarray(np.array(table, np.int32)), best, *found, *given)


def placed_kernel(taken, pads, order, best, *refs):
    found, out = refs[:-1], refs[-1]
    rows = order.shape[1]
    here = lax.axis_index("blk")
    total = best[pl.ds(here, 1), :]
    for index, row in enumerate(found):
        total = jnp.where(taken[here * len(found) + index] > 0, jnp.maximum(total, row[...]), total)
    column = jnp.broadcast_to(total, (128, rows)).T[:, :1]
    row = lax.broadcasted_iota(jnp.int32, (rows, 1), 0)
    in_order = jnp.max(jnp.where(order[...] == row, column, FLOOR), axis=0, keepdims=True)
    position = lax.broadcasted_iota(jnp.int32, (1, rows), 1)
    out[...] = jnp.where(position < rows - pads[here], in_order, 0.0)


def placed(best, found, permutes, order, pad_counts):
    rows = order.shape[0]
    taken = np.zeros((best.shape[0], len(permutes)), np.int32)
    for index, permute in enumerate(permutes):
        taken[[to for _, to in permute], index] = 1
    whole, scalars = pl.BlockSpec(memory_space=pltpu.VMEM), pl.BlockSpec(memory_space=pltpu.SMEM)
    return pl.pallas_call(
        placed_kernel,
        out_shape=jax.ShapeDtypeStruct((1, rows), jnp.float32),
        in_specs=[scalars, scalars] + [whole] * (2 + len(found)),
        out_specs=whole,
        compiler_params=pltpu.CompilerParams(vmem_limit_bytes=VMEM),
        name="placed",
    )(jnp.asarray(taken.reshape(-1)), pad_counts, order.reshape(1, rows), best, *found).reshape(rows)


def local(embeddings, order, pad_counts):
    nblocks = lax.axis_size("blk")
    moves, work, sending = planned(nblocks)
    unit = normalized(embeddings, order, pad_counts)
    slots, best = {"own": unit}, None
    rank = dict({"own": -1}, **{move.name: move.stage for move in moves})
    edges = {}
    for stage, pairs in enumerate(work):
        due = edges.setdefault(min(last for last in sending if last >= stage), set())
        due |= {(of, to) for of in range(nblocks) for pair in pairs[of] for to in pair[2:] if to != of}
    if len(sending) == 2:
        edges = dict(zip(sending, in_two(*[edges[stage] for stage in sending], nblocks)))
    permutes, found = [], []
    for stage, pairs in enumerate(work):
        starting = [move for move in moves if move.begins == stage]
        for needs in sorted({move.needs for move in starting}):
            values = [slots[name] for name in needs]
            if best is not None:
                *values, best = lax.optimization_barrier((*values, best))
            for move in starting:
                if move.needs == needs:
                    value = values[needs.index(move.source)]
                    slots[move.name] = lax.ppermute(value, "blk", move.pairs)
        if stage == 0:
            best = own_block(unit, order, pad_counts, nblocks)
        sends = colored(sorted(edges[stage]), nblocks) if stage in sending else []
        if any(pairs):
            best, *rows = scored(best, found, permutes, slots, rank, pairs, sends)
            found = [lax.ppermute(row, "blk", permute) for row, permute in zip(rows, sends)]
            permutes = sends
    return placed(best, found, permutes, order, pad_counts)


def solution(mesh):
    in_specs = (P(("groups", "blk"), None), P(("groups", "blk")), P("groups"))
    out_specs = P(("groups", "blk"))
    return jax.shard_map(local, mesh=mesh, in_specs=in_specs, out_specs=out_specs, check_vma=False)
```

```python
import functools

import jax
import jax.numpy as jnp
import numpy as np
from jax import lax
from jax.experimental import pallas as pl
from jax.experimental.pallas import tpu as pltpu
from jax.sharding import PartitionSpec as P

STEPS = 6
VMEM = 64 * 2**20 - 2**16
FLOOR = -2.0
MOST_PADS = 256
AHEAD = 2
FIRST, EARLY = 4, 2


class Move:
    def __init__(self, name, source, pairs, begins, stage, *after):
        self.name, self.source, self.pairs = name, source, pairs
        self.begins, self.stage, self.needs = begins, stage, (source, *after)


def grid_moves():
    def at(z, y, lane):
        return 4 * z + 2 * y + (y if lane == 0 else 1 - y)

    def rows(links):
        return [
            (at(z, y, lane), at(to, y, land)) for y in (0, 1) for (z, lane), (to, land) in links
        ]

    def across(planes):
        return [(at(z, y, lane), at(z, 1 - y, lane)) for z, lane in planes for y in (0, 1)]

    every = [(z, lane) for z in range(4) for lane in (0, 1)]
    swap = rows([((z, lane), (z, 1 - lane)) for z, lane in every])
    crossed = [(at(1, y, lane), at(1, 1 - y, 1 - lane)) for y in (0, 1) for lane in (0, 1)]
    first = [((0, 0), (2, 1)), ((2, 0), (3, 1)), ((3, 0), (1, 0)), ((1, 0), (0, 0)), ((0, 1), (1, 1))]
    second = [((3, 1), (1, 1)), ((1, 1), (0, 1)), ((2, 1), (3, 0)), ((1, 0), (2, 1))]
    return [
        Move("R1", "own", rows(first), 0, 1),
        Move("R2", "own", rows(second), 0, 1),
        Move("Y", "own", across([place for place in every if place[0] != 1]) + crossed, 0, 1),
        Move("A", "own", swap, 0, 0),
        Move("R3", "own", rows([((1, 1), (2, 0)), ((2, 0), (1, 1))]), 1, 2, "R1"),
        Move("V", "R1", [(at(2, y, 1), at(3, y, 1 - y)) for y in (0, 1)] + across([(1, 1)]), 1, 2),
        Move("F", "Y", swap, 2, 2),
        Move("W", "R1", rows([((1, 0), (1, 1)), ((1, 1), (1, 0))]), 2, 2),
    ]


GRID_PAIRS = (
    ((0, 2), (0, 4), (1, 4), (2, 4), (3, 4)),
    ((0, 1), (0, 5), (1, 3), (1, 5), (3, 5)),
    ((0, 3), (0, 6), (1, 6), (2, 3), (2, 6), (3, 6)),
    ((1, 2), (1, 7), (2, 7), (3, 7)),
    ((1, 12), (4, 5), (4, 6), (4, 7), (6, 12), (7, 12)),
    ((1, 13), (2, 8), (2, 12), (2, 13), (5, 8), (7, 13)),
    ((1, 11), (1, 14), (1, 15), (2, 14), (4, 14)),
    ((2, 5), (2, 15), (4, 15), (5, 6), (5, 7), (5, 15), (6, 7)),
    ((5, 9), (5, 10), (5, 11), (9, 10), (9, 11)),
    ((0, 10), (0, 11), (4, 8), (4, 9), (4, 10), (8, 9), (8, 11)),
    ((3, 8), (3, 9), (7, 8), (7, 9), (7, 10), (7, 11)),
    ((6, 8), (6, 9), (6, 10), (6, 11), (8, 10), (10, 11)),
    ((9, 12), (9, 13), (9, 14), (9, 15), (12, 13), (12, 14), (13, 14), (13, 15)),
    ((0, 12), (0, 13), (0, 14), (0, 15), (8, 12), (8, 13), (8, 14)),
    ((11, 12), (11, 13), (11, 14), (11, 15), (12, 15)),
    ((3, 13), (3, 14), (3, 15), (10, 12), (10, 13), (10, 14), (10, 15), (14, 15)),
)


def ring_moves(count):
    return [
        Move("N%d" % k, "own", [((i + k) % count, i) for i in range(count)], 0, k)
        for k in range(1, STEPS + 1)
    ]


def planned(count):
    if count == 16:
        moves, placed_pairs, sending = grid_moves(), GRID_PAIRS, (1, 2)
    else:
        moves, sending = ring_moves(count), (STEPS,)
        placed_pairs = [[(b, (b + k) % count) for k in range(1, STEPS + 1)] for b in range(count)]
    holds = {"own": {d: d for d in range(count)}}
    stage_of = {"own": 0}
    for move in moves:
        holds[move.name] = {to: holds[move.source][of] for of, to in move.pairs}
        stage_of[move.name] = move.stage
    stages = 1 + max(stage_of.values())
    work = [[[] for _ in range(count)] for _ in range(stages)]
    for device, pairs in enumerate(placed_pairs):
        slot_of = {}
        for slot in sorted(stage_of, key=stage_of.get):
            if device in holds[slot]:
                slot_of.setdefault(holds[slot][device], slot)
        for block, visitor in pairs:
            slot, other = slot_of[block], slot_of[visitor]
            stage = max(stage_of[slot], stage_of[other])
            work[stage][device].append((slot, other, block, visitor))
    scored_pairs = sorted(tuple(sorted(pair)) for pairs in placed_pairs for pair in pairs)
    needed = {tuple(sorted((b, (b + k) % count))) for b in range(count) for k in range(1, STEPS + 1)}
    assert scored_pairs == sorted(needed)
    return moves, work, sending


def colored(edges, count):
    ends = [of for of, _ in edges], [to for _, to in edges]
    most = max((side.count(device) for side in ends for device in range(count)), default=0)
    sends, takes = [{} for _ in range(count)], [{} for _ in range(count)]
    for of, to in sorted(edges, key=lambda edge: (-abs(edge[0] - edge[1]) * (min(edge) < FIRST), edge)):
        both = next(c for c in range(2 * len(edges)) if c not in sends[of] and c not in takes[to])
        a = next(c for c in range(len(edges)) if c not in sends[of])
        b = next(c for c in range(len(edges)) if c not in takes[to])
        if both < most:
            a = b = both
        path, node, tables, colour = [], to, (takes, sends), a
        while a != b and colour in tables[0][node]:
            end = tables[0][node][colour]
            path.append(((end, node) if tables[0] is takes else (node, end), colour))
            node, tables, colour = end, tables[::-1], a + b - colour
        for (first, second), colour in path:
            del sends[first][colour], takes[second][colour]
        for (first, second), colour in path:
            sends[first][a + b - colour], takes[second][a + b - colour] = second, first
        sends[of][a], takes[to][a] = to, of
    return [
        [(of, to[c]) for of, to in enumerate(sends) if c in to]
        for c in range(max((c + 1 for to in sends for c in to), default=0))
    ]


def in_two(early, late, count):
    early, late = set(early) - set(late), set(late)

    def degrees(edges):
        return [
            [sum(edge[side] == device for edge in edges) for device in range(count)] for side in (0, 1)
        ]

    most = max(degrees(late)[0] + degrees(late)[1])
    while early:
        busy, taken = degrees(early), degrees(late)
        top = max(busy[0] + busy[1])
        free = [
            (min(of, to) >= FIRST, max(busy[0][of], busy[1][to]), busy[0][of] + busy[1][to], of, to)
            for of, to in sorted(early)
            if max(taken[0][of], taken[1][to]) < most and max(busy[0][of], busy[1][to]) == top
        ]
        if not free or top <= EARLY:
            break
        early.remove(max(free)[3:])
        late.add(max(free)[3:])
    return sorted(early), sorted(late)


def unit_kernel(pads, order_smem, order, embeddings, unit, value, result, tile, into, out, sem):
    rows = unit.shape[0]
    count = rows // into.shape[0]
    parts = [pl.ds(start, count) for start in range(0, rows, count)]
    loads = [
        pltpu.make_async_copy(embeddings.at[part], value.at[part], into.at[index])
        for index, part in enumerate(parts)
    ]
    stores = [
        pltpu.make_async_copy(result.at[part], unit.at[part], out.at[index])
        for index, part in enumerate(parts)
    ]
    first = order_smem[0]
    base = pl.multiple_of((first // 16) * 16, 16)
    filling = pltpu.make_async_copy(embeddings.at[pl.ds(base, 16)], tile, sem)
    filling.start()
    for load in loads:
        load.start()
    filling.wait()
    among = lax.broadcasted_iota(jnp.int32, (16, 1), 0) == first - base
    filler = jnp.sum(jnp.where(among, tile[...].astype(jnp.float32), 0.0), axis=0, keepdims=True)
    for index, part in enumerate(parts):
        found = valid_rows(pads, order, index * count, count)
        loads[index].wait()
        chunk = jnp.where(found, value[part, :].astype(jnp.float32), filler)
        scale = lax.rsqrt(jnp.sum(chunk * chunk, axis=1, keepdims=True) + 1e-06)
        result[part, :] = (chunk * scale).astype(jnp.bfloat16)
        stores[index].start()
    for store in stores:
        store.wait()


def valid_rows(pads, order, start, count):
    rows = order.shape[1]
    most = min(rows, MOST_PADS)
    valid_count = rows - pads[lax.axis_index("blk")]
    position = rows - most + lax.broadcasted_iota(jnp.int32, (1, most), 1)
    padding = jnp.where(position < valid_count, -1, order[:, rows - most :])
    row = start + lax.broadcasted_iota(jnp.int32, (count, 1), 0)
    return jnp.max(jnp.where(padding == row, 1.0, 0.0), axis=1, keepdims=True) < 1.0


def normalized(embeddings, order, pad_counts):
    rows, depth = embeddings.shape
    chunks = 4
    scalars = pl.BlockSpec(memory_space=pltpu.SMEM)
    return pl.pallas_call(
        unit_kernel,
        out_shape=jax.ShapeDtypeStruct((rows, depth), jnp.bfloat16),
        in_specs=[
            scalars,
            scalars,
            pl.BlockSpec(memory_space=pltpu.VMEM),
            pl.BlockSpec(memory_space=pl.ANY),
        ],
        out_specs=pl.BlockSpec(memory_space=pl.ANY),
        scratch_shapes=[
            pltpu.VMEM((rows, depth), jnp.bfloat16),
            pltpu.VMEM((rows, depth), jnp.bfloat16),
            pltpu.VMEM((16, depth), jnp.bfloat16),
            pltpu.SemaphoreType.DMA((chunks,)),
            pltpu.SemaphoreType.DMA((chunks,)),
            pltpu.SemaphoreType.DMA,
        ],
        compiler_params=pltpu.CompilerParams(vmem_limit_bytes=VMEM),
        cost_estimate=pl.CostEstimate(
            flops=4 * rows * depth, bytes_accessed=4 * rows * depth, transcendentals=rows
        ),
        name="normalized",
    )(pad_counts, order, order.reshape(1, rows), embeddings)


def product(left, right):
    return lax.dot_general(left, right, (((1,), (1,)), ((), ())), preferred_element_type=jnp.float32)


def own_kernel(pads, order, unit, best):
    rows = unit.shape[0]
    best[...] = jnp.full(best.shape, FLOOR, jnp.float32)
    valid = valid_rows(pads, order, 0, rows)
    row = lax.broadcasted_iota(jnp.int32, (rows, 1), 0)
    here = pl.ds(lax.axis_index("blk"), 1)
    for start in range(0, rows, 256):
        part = pl.ds(start, 256)
        scores = product(unit[...], unit[part, :])
        column = start + lax.broadcasted_iota(jnp.int32, (1, 256), 1)
        scores = jnp.where(valid & (row != column), scores, FLOOR)
        best[here, part] = jnp.max(scores, axis=0, keepdims=True)


def own_block(unit, order, pad_counts, nblocks):
    rows, depth = unit.shape
    whole = pl.BlockSpec(memory_space=pltpu.VMEM)
    return pl.pallas_call(
        own_kernel,
        out_shape=jax.ShapeDtypeStruct((nblocks, rows), jnp.float32),
        in_specs=[pl.BlockSpec(memory_space=pltpu.SMEM), whole, whole],
        out_specs=whole,
        compiler_params=pltpu.CompilerParams(vmem_limit_bytes=VMEM),
        cost_estimate=pl.CostEstimate(
            flops=2 * rows * rows * depth, bytes_accessed=2 * rows * depth, transcendentals=0
        ),
        name="own_block",
    )(pad_counts, order.reshape(1, rows), unit)


def pairs_kernel(nslots, nrows, ntaken, nloads, npairs, table, best, *refs):
    arrivals, slots, out = refs[:ntaken], refs[ntaken : ntaken + nslots], refs[ntaken + nslots]
    sent, (held, across, sems) = refs[ntaken + nslots + 1 : -3], refs[-3:]
    rows = out.shape[1]
    here = lax.axis_index("blk")
    loads_at = here * (2 + nrows + ntaken + nloads + 5 * npairs) + 2 + nrows + ntaken
    pairs_at = loads_at + nloads
    rows_at = loads_at - nrows - ntaken
    loads, pairs = table[rows_at - 2], table[rows_at - 1]

    def fetch(load):
        @pl.when(load < loads)
        def _():
            wanted = table[loads_at + jnp.minimum(load, nloads - 1)]
            for index, slot in enumerate(slots):
                @pl.when(wanted == index)
                def _(slot=slot):
                    for start in range(0, rows, 256):
                        part = pl.ds(start, 256)
                        pltpu.make_async_copy(slot.at[part], held.at[load, part], sems.at[load]).start()

    for load in range(min(AHEAD, nloads)):
        fetch(load)
    out[...] = best[...]
    own = pl.ds(here, 1)
    for index, row in enumerate(arrivals):
        handed = table[rows_at + nrows + index] > 0
        out[own, :] = jnp.where(handed, jnp.maximum(out[own, :], row[...]), out[own, :])

    @pl.loop(0, pairs)
    def _(step):
        at = pairs_at + 5 * step
        before = jnp.where(step == 0, 0, table[jnp.maximum(at - 1, 0)])

        @pl.loop(before, table[at + 4])
        def _(load):
            pltpu.make_async_copy(slots[0], held.at[load], sems.at[load]).wait()
            fetch(load + AHEAD)

        left, right = table[at], table[at + 1]
        first, second = pl.ds(table[at + 2], 1), pl.ds(table[at + 3], 1)
        for start in range(0, rows, 256):
            part = pl.ds(start, 256)
            scores = product(held[left], held[right, part, :])
            down = jnp.max(scores, axis=0, keepdims=True)
            out[second, part] = jnp.maximum(out[second, part], down)
            along = jnp.maximum(scores[:, :128], scores[:, 128:])
            across[...] = along if start == 0 else jnp.maximum(across[...], along)
        found = jnp.max(across[...].T, axis=0, keepdims=True)
        out[first, :] = jnp.maximum(out[first, :], found)

    for index, row in enumerate(sent):
        row[...] = out[pl.ds(table[rows_at + index], 1), :]


def in_order_of_loads(pairs, rank):
    left, loaded, ordered = list(pairs), [], []
    while left:
        pair = min(
            left,
            key=lambda p: (sum(s not in loaded for s in p[:2]), max(rank[s] for s in p[:2]), p[2:]),
        )
        left.remove(pair)
        loaded += [slot for slot in pair[:2] if slot not in loaded]
        ordered.append((pair, len(loaded)))
    return loaded, ordered


def scored(best, found, permutes, slots, rank, work, sends):
    names = sorted({slot for pairs in work for pair in pairs for slot in pair[:2]})
    plans = [in_order_of_loads(pairs, rank) for pairs in work]
    nloads = max(len(loaded) for loaded, _ in plans)
    npairs = max(len(pairs) for pairs in work)
    table = []
    for device, (loaded, ordered) in enumerate(plans):
        table += [len(loaded), len(ordered)]
        table += [dict(permute).get(device, device) for permute in sends]
        table += [int(device in dict(permute).values()) for permute in permutes]
        table += [names.index(slot) for slot in loaded] + [0] * (nloads - len(loaded))
        for (slot, other, block, visitor), need in ordered:
            table += [loaded.index(slot), loaded.index(other), block, visitor, need]
        table += [0] * (5 * (npairs - len(ordered)))
    given = [slots[name] for name in names]
    rows, depth = given[0].shape
    whole = pl.BlockSpec(memory_space=pltpu.VMEM)
    return pl.pallas_call(
        functools.partial(pairs_kernel, len(given), len(sends), len(found), nloads, npairs),
        out_shape=[jax.ShapeDtypeStruct(best.shape, jnp.float32)]
        + [jax.ShapeDtypeStruct((1, rows), jnp.float32)] * len(sends),
        in_specs=[pl.BlockSpec(memory_space=pltpu.SMEM)]
        + [whole] * (1 + len(found))
        + [pl.BlockSpec(memory_space=pl.ANY)] * len(given),
        out_specs=[whole] * (1 + len(sends)),
        scratch_shapes=[
            pltpu.VMEM((nloads, rows, depth), jnp.bfloat16),
            pltpu.VMEM((rows, 128), jnp.float32),
            pltpu.SemaphoreType.DMA((nloads,)),
        ],
        compiler_params=pltpu.CompilerParams(vmem_limit_bytes=VMEM),
        cost_estimate=pl.CostEstimate(
            flops=2 * npairs * rows * rows * depth,
            bytes_accessed=2 * nloads * rows * depth,
            transcendentals=0,
        ),
        name="scored",
    )(jnp.asarray(np.array(table, np.int32)), best, *found, *given)


def placed_kernel(taken, pads, order, best, *refs):
    found, out = refs[:-1], refs[-1]
    rows = order.shape[1]
    here = lax.axis_index("blk")
    total = best[pl.ds(here, 1), :]
    for index, row in enumerate(found):
        total = jnp.where(taken[here * len(found) + index] > 0, jnp.maximum(total, row[...]), total)
    column = jnp.broadcast_to(total, (128, rows)).T[:, :1]
    row = lax.broadcasted_iota(jnp.int32, (rows, 1), 0)
    in_order = jnp.max(jnp.where(order[...] == row, column, FLOOR), axis=0, keepdims=True)
    position = lax.broadcasted_iota(jnp.int32, (1, rows), 1)
    out[...] = jnp.where(position < rows - pads[here], in_order, 0.0)


def placed(best, found, permutes, order, pad_counts):
    rows = order.shape[0]
    taken = np.zeros((best.shape[0], len(permutes)), np.int32)
    for index, permute in enumerate(permutes):
        taken[[to for _, to in permute], index] = 1
    whole, scalars = pl.BlockSpec(memory_space=pltpu.VMEM), pl.BlockSpec(memory_space=pltpu.SMEM)
    return pl.pallas_call(
        placed_kernel,
        out_shape=jax.ShapeDtypeStruct((1, rows), jnp.float32),
        in_specs=[scalars, scalars] + [whole] * (2 + len(found)),
        out_specs=whole,
        compiler_params=pltpu.CompilerParams(vmem_limit_bytes=VMEM),
        name="placed",
    )(jnp.asarray(taken.reshape(-1)), pad_counts, order.reshape(1, rows), best, *found).reshape(rows)


def local(embeddings, order, pad_counts):
    nblocks = lax.axis_size("blk")
    moves, work, sending = planned(nblocks)
    unit = normalized(embeddings, order, pad_counts)
    slots, best = {"own": unit}, None
    rank = dict({"own": -1}, **{move.name: move.stage for move in moves})
    edges = {}
    for stage, pairs in enumerate(work):
        due = edges.setdefault(min(last for last in sending if last >= stage), set())
        due |= {(of, to) for of in range(nblocks) for pair in pairs[of] for to in pair[2:] if to != of}
    if len(sending) == 2:
        edges = dict(zip(sending, in_two(*[edges[stage] for stage in sending], nblocks)))
    permutes, found = [], []
    for stage, pairs in enumerate(work):
        starting = [move for move in moves if move.begins == stage]
        for needs in sorted({move.needs for move in starting}):
            values = [slots[name] for name in needs]
            if best is not None:
                *values, best = lax.optimization_barrier((*values, best))
            for move in starting:
                if move.needs == needs:
                    value = values[needs.index(move.source)]
                    slots[move.name] = lax.ppermute(value, "blk", move.pairs)
        if stage == 0:
            best = own_block(unit, order, pad_counts, nblocks)
        sends = colored(sorted(edges[stage]), nblocks) if stage in sending else []
        if any(pairs):
            best, *rows = scored(best, found, permutes, slots, rank, pairs, sends)
            found = [lax.ppermute(row, "blk", permute) for row, permute in zip(rows, sends)]
            permutes = sends
    return placed(best, found, permutes, order, pad_counts)


def solution(mesh):
    in_specs = (P(("groups", "blk"), None), P(("groups", "blk")), P("groups"))
    out_specs = P(("groups", "blk"))
    return jax.shard_map(local, mesh=mesh, in_specs=in_specs, out_specs=out_specs, check_vma=False)
```

```python
import functools

import jax
import jax.numpy as jnp
import numpy as np
from jax import lax
from jax.experimental import pallas as pl
from jax.experimental.pallas import tpu as pltpu
from jax.sharding import PartitionSpec as P

STEPS = 6
VMEM = 64 * 2**20 - 2**16
FLOOR = -2.0
MOST_PADS = 256
AHEAD = 2
FIRST, EARLY = 4, 2


class Move:
    def __init__(self, name, source, pairs, begins, stage, *after):
        self.name, self.source, self.pairs = name, source, pairs
        self.begins, self.stage, self.needs = begins, stage, (source, *after)


def grid_moves():
    def at(z, y, lane):
        return 4 * z + 2 * y + (y if lane == 0 else 1 - y)

    def rows(links):
        return [
            (at(z, y, lane), at(to, y, land)) for y in (0, 1) for (z, lane), (to, land) in links
        ]

    def across(planes):
        return [(at(z, y, lane), at(z, 1 - y, lane)) for z, lane in planes for y in (0, 1)]

    every = [(z, lane) for z in range(4) for lane in (0, 1)]
    swap = rows([((z, lane), (z, 1 - lane)) for z, lane in every])
    crossed = [(at(1, y, lane), at(1, 1 - y, 1 - lane)) for y in (0, 1) for lane in (0, 1)]
    first = [((0, 0), (2, 1)), ((2, 0), (3, 1)), ((3, 0), (1, 0)), ((1, 0), (0, 0)), ((0, 1), (1, 1))]
    second = [((3, 1), (1, 1)), ((1, 1), (0, 1)), ((2, 1), (3, 0)), ((1, 0), (2, 1))]
    return [
        Move("R1", "own", rows(first), 0, 1),
        Move("R2", "own", rows(second), 0, 1),
        Move("Y", "own", across([place for place in every if place[0] != 1]) + crossed, 0, 1),
        Move("A", "own", swap, 0, 0),
        Move("R3", "own", rows([((1, 1), (2, 0)), ((2, 0), (1, 1))]), 1, 2, "R1"),
        Move("V", "R1", [(at(2, y, 1), at(3, y, 1 - y)) for y in (0, 1)] + across([(1, 1)]), 1, 2),
        Move("F", "Y", swap, 2, 2),
        Move("W", "R1", rows([((1, 0), (1, 1)), ((1, 1), (1, 0))]), 2, 2),
    ]


GRID_PAIRS = (
    ((0, 2), (0, 4), (1, 4), (2, 4), (3, 4)),
    ((0, 1), (0, 5), (1, 3), (1, 5), (3, 5)),
    ((0, 3), (0, 6), (1, 6), (2, 3), (2, 6), (3, 6)),
    ((1, 2), (1, 7), (2, 7), (3, 7)),
    ((1, 12), (4, 5), (4, 6), (4, 7), (6, 12), (7, 12)),
    ((1, 13), (2, 8), (2, 12), (2, 13), (5, 8), (7, 13)),
    ((1, 11), (1, 14), (1, 15), (2, 14), (4, 14)),
    ((2, 5), (2, 15), (4, 15), (5, 6), (5, 7), (5, 15), (6, 7)),
    ((5, 9), (5, 10), (5, 11), (9, 10), (9, 11)),
    ((0, 10), (0, 11), (4, 8), (4, 9), (4, 10), (8, 9), (8, 11)),
    ((3, 8), (3, 9), (7, 8), (7, 9), (7, 10), (7, 11)),
    ((6, 8), (6, 9), (6, 10), (6, 11), (8, 10), (10, 11)),
    ((9, 12), (9, 13), (9, 14), (9, 15), (12, 13), (12, 14), (13, 14), (13, 15)),
    ((0, 12), (0, 13), (0, 14), (0, 15), (8, 12), (8, 13), (8, 14)),
    ((11, 12), (11, 13), (11, 14), (11, 15), (12, 15)),
    ((3, 13), (3, 14), (3, 15), (10, 12), (10, 13), (10, 14), (10, 15), (14, 15)),
)


def ring_moves(count):
    return [
        Move("N%d" % k, "own", [((i + k) % count, i) for i in range(count)], 0, k)
        for k in range(1, STEPS + 1)
    ]


def planned(count):
    if count == 16:
        moves, placed_pairs, sending = grid_moves(), GRID_PAIRS, (1, 2)
    else:
        moves, sending = ring_moves(count), (STEPS,)
        placed_pairs = [[(b, (b + k) % count) for k in range(1, STEPS + 1)] for b in range(count)]
    holds = {"own": {d: d for d in range(count)}}
    stage_of = {"own": 0}
    for move in moves:
        holds[move.name] = {to: holds[move.source][of] for of, to in move.pairs}
        stage_of[move.name] = move.stage
    stages = 1 + max(stage_of.values())
    work = [[[] for _ in range(count)] for _ in range(stages)]
    for device, pairs in enumerate(placed_pairs):
        slot_of = {}
        for slot in sorted(stage_of, key=stage_of.get):
            if device in holds[slot]:
                slot_of.setdefault(holds[slot][device], slot)
        for block, visitor in pairs:
            slot, other = slot_of[block], slot_of[visitor]
            stage = max(stage_of[slot], stage_of[other])
            work[stage][device].append((slot, other, block, visitor))
    scored_pairs = sorted(tuple(sorted(pair)) for pairs in placed_pairs for pair in pairs)
    needed = {tuple(sorted((b, (b + k) % count))) for b in range(count) for k in range(1, STEPS + 1)}
    assert scored_pairs == sorted(needed)
    return moves, work, sending


def colored(edges, count):
    ends = [of for of, _ in edges], [to for _, to in edges]
    most = max((side.count(device) for side in ends for device in range(count)), default=0)
    sends, takes = [{} for _ in range(count)], [{} for _ in range(count)]
    for of, to in sorted(edges, key=lambda edge: (min(edge) >= FIRST, -abs(edge[0] - edge[1]), edge)):
        both = next(c for c in range(2 * len(edges)) if c not in sends[of] and c not in takes[to])
        a = next(c for c in range(len(edges)) if c not in sends[of])
        b = next(c for c in range(len(edges)) if c not in takes[to])
        if both < most:
            a = b = both
        path, node, tables, colour = [], to, (takes, sends), a
        while a != b and colour in tables[0][node]:
            end = tables[0][node][colour]
            path.append(((end, node) if tables[0] is takes else (node, end), colour))
            node, tables, colour = end, tables[::-1], a + b - colour
        for (first, second), colour in path:
            del sends[first][colour], takes[second][colour]
        for (first, second), colour in path:
            sends[first][a + b - colour], takes[second][a + b - colour] = second, first
        sends[of][a], takes[to][a] = to, of
    return [
        [(of, to[c]) for of, to in enumerate(sends) if c in to]
        for c in range(max((c + 1 for to in sends for c in to), default=0))
    ]


def in_two(early, late, count):
    early, late = set(early) - set(late), set(late)

    def degrees(edges):
        return [
            [sum(edge[side] == device for edge in edges) for device in range(count)] for side in (0, 1)
        ]

    most = max(degrees(late)[0] + degrees(late)[1])
    while early:
        busy, taken = degrees(early), degrees(late)
        top = max(busy[0] + busy[1])
        free = [
            (min(of, to) >= FIRST, max(busy[0][of], busy[1][to]), busy[0][of] + busy[1][to], of, to)
            for of, to in sorted(early)
            if max(taken[0][of], taken[1][to]) < most and max(busy[0][of], busy[1][to]) == top
        ]
        if not free or top <= EARLY:
            break
        early.remove(max(free)[3:])
        late.add(max(free)[3:])
    return sorted(early), sorted(late)


def unit_kernel(pads, order_smem, order, embeddings, unit, value, result, tile, into, out, sem):
    rows = unit.shape[0]
    count = rows // into.shape[0]
    parts = [pl.ds(start, count) for start in range(0, rows, count)]
    loads = [
        pltpu.make_async_copy(embeddings.at[part], value.at[part], into.at[index])
        for index, part in enumerate(parts)
    ]
    stores = [
        pltpu.make_async_copy(result.at[part], unit.at[part], out.at[index])
        for index, part in enumerate(parts)
    ]
    first = order_smem[0]
    base = pl.multiple_of((first // 16) * 16, 16)
    filling = pltpu.make_async_copy(embeddings.at[pl.ds(base, 16)], tile, sem)
    filling.start()
    for load in loads:
        load.start()
    filling.wait()
    among = lax.broadcasted_iota(jnp.int32, (16, 1), 0) == first - base
    filler = jnp.sum(jnp.where(among, tile[...].astype(jnp.float32), 0.0), axis=0, keepdims=True)
    for index, part in enumerate(parts):
        found = valid_rows(pads, order, index * count, count)
        loads[index].wait()
        chunk = jnp.where(found, value[part, :].astype(jnp.float32), filler)
        scale = lax.rsqrt(jnp.sum(chunk * chunk, axis=1, keepdims=True) + 1e-06)
        result[part, :] = (chunk * scale).astype(jnp.bfloat16)
        stores[index].start()
    for store in stores:
        store.wait()


def valid_rows(pads, order, start, count):
    rows = order.shape[1]
    most = min(rows, MOST_PADS)
    valid_count = rows - pads[lax.axis_index("blk")]
    position = rows - most + lax.broadcasted_iota(jnp.int32, (1, most), 1)
    padding = jnp.where(position < valid_count, -1, order[:, rows - most :])
    row = start + lax.broadcasted_iota(jnp.int32, (count, 1), 0)
    return jnp.max(jnp.where(padding == row, 1.0, 0.0), axis=1, keepdims=True) < 1.0


def normalized(embeddings, order, pad_counts):
    rows, depth = embeddings.shape
    chunks = 4
    scalars = pl.BlockSpec(memory_space=pltpu.SMEM)
    return pl.pallas_call(
        unit_kernel,
        out_shape=jax.ShapeDtypeStruct((rows, depth), jnp.bfloat16),
        in_specs=[
            scalars,
            scalars,
            pl.BlockSpec(memory_space=pltpu.VMEM),
            pl.BlockSpec(memory_space=pl.ANY),
        ],
        out_specs=pl.BlockSpec(memory_space=pl.ANY),
        scratch_shapes=[
            pltpu.VMEM((rows, depth), jnp.bfloat16),
            pltpu.VMEM((rows, depth), jnp.bfloat16),
            pltpu.VMEM((16, depth), jnp.bfloat16),
            pltpu.SemaphoreType.DMA((chunks,)),
            pltpu.SemaphoreType.DMA((chunks,)),
            pltpu.SemaphoreType.DMA,
        ],
        compiler_params=pltpu.CompilerParams(vmem_limit_bytes=VMEM),
        cost_estimate=pl.CostEstimate(
            flops=4 * rows * depth, bytes_accessed=4 * rows * depth, transcendentals=rows
        ),
        name="normalized",
    )(pad_counts, order, order.reshape(1, rows), embeddings)


def product(left, right):
    return lax.dot_general(left, right, (((1,), (1,)), ((), ())), preferred_element_type=jnp.float32)


def own_kernel(pads, order, unit, best):
    rows = unit.shape[0]
    best[...] = jnp.full(best.shape, FLOOR, jnp.float32)
    valid = valid_rows(pads, order, 0, rows)
    row = lax.broadcasted_iota(jnp.int32, (rows, 1), 0)
    here = pl.ds(lax.axis_index("blk"), 1)
    for start in range(0, rows, 256):
        part = pl.ds(start, 256)
        scores = product(unit[...], unit[part, :])
        column = start + lax.broadcasted_iota(jnp.int32, (1, 256), 1)
        scores = jnp.where(valid & (row != column), scores, FLOOR)
        best[here, part] = jnp.max(scores, axis=0, keepdims=True)


def own_block(unit, order, pad_counts, nblocks):
    rows, depth = unit.shape
    whole = pl.BlockSpec(memory_space=pltpu.VMEM)
    return pl.pallas_call(
        own_kernel,
        out_shape=jax.ShapeDtypeStruct((nblocks, rows), jnp.float32),
        in_specs=[pl.BlockSpec(memory_space=pltpu.SMEM), whole, whole],
        out_specs=whole,
        compiler_params=pltpu.CompilerParams(vmem_limit_bytes=VMEM),
        cost_estimate=pl.CostEstimate(
            flops=2 * rows * rows * depth, bytes_accessed=2 * rows * depth, transcendentals=0
        ),
        name="own_block",
    )(pad_counts, order.reshape(1, rows), unit)


def pairs_kernel(nslots, nrows, ntaken, nloads, npairs, table, best, *refs):
    arrivals, slots, out = refs[:ntaken], refs[ntaken : ntaken + nslots], refs[ntaken + nslots]
    sent, (held, across, sems) = refs[ntaken + nslots + 1 : -3], refs[-3:]
    rows = out.shape[1]
    here = lax.axis_index("blk")
    loads_at = here * (2 + nrows + ntaken + nloads + 5 * npairs) + 2 + nrows + ntaken
    pairs_at = loads_at + nloads
    rows_at = loads_at - nrows - ntaken
    loads, pairs = table[rows_at - 2], table[rows_at - 1]

    def fetch(load):
        @pl.when(load < loads)
        def _():
            wanted = table[loads_at + jnp.minimum(load, nloads - 1)]
            for index, slot in enumerate(slots):
                @pl.when(wanted == index)
                def _(slot=slot):
                    for start in range(0, rows, 256):
                        part = pl.ds(start, 256)
                        pltpu.make_async_copy(slot.at[part], held.at[load, part], sems.at[load]).start()

    for load in range(min(AHEAD, nloads)):
        fetch(load)
    out[...] = best[...]
    own = pl.ds(here, 1)
    for index, row in enumerate(arrivals):
        handed = table[rows_at + nrows + index] > 0
        out[own, :] = jnp.where(handed, jnp.maximum(out[own, :], row[...]), out[own, :])

    @pl.loop(0, pairs)
    def _(step):
        at = pairs_at + 5 * step
        before = jnp.where(step == 0, 0, table[jnp.maximum(at - 1, 0)])

        @pl.loop(before, table[at + 4])
        def _(load):
            pltpu.make_async_copy(slots[0], held.at[load], sems.at[load]).wait()
            fetch(load + AHEAD)

        left, right = table[at], table[at + 1]
        first, second = pl.ds(table[at + 2], 1), pl.ds(table[at + 3], 1)
        for start in range(0, rows, 256):
            part = pl.ds(start, 256)
            scores = product(held[left], held[right, part, :])
            down = jnp.max(scores, axis=0, keepdims=True)
            out[second, part] = jnp.maximum(out[second, part], down)
            along = jnp.maximum(scores[:, :128], scores[:, 128:])
            across[...] = along if start == 0 else jnp.maximum(across[...], along)
        found = jnp.max(across[...].T, axis=0, keepdims=True)
        out[first, :] = jnp.maximum(out[first, :], found)

    for index, row in enumerate(sent):
        row[...] = out[pl.ds(table[rows_at + index], 1), :]


def in_order_of_loads(pairs, rank):
    left, loaded, ordered = list(pairs), [], []
    while left:
        pair = min(
            left,
            key=lambda p: (sum(s not in loaded for s in p[:2]), max(rank[s] for s in p[:2]), p[2:]),
        )
        left.remove(pair)
        loaded += [slot for slot in pair[:2] if slot not in loaded]
        ordered.append((pair, len(loaded)))
    return loaded, ordered


def scored(best, found, permutes, slots, rank, work, sends):
    names = sorted({slot for pairs in work for pair in pairs for slot in pair[:2]})
    plans = [in_order_of_loads(pairs, rank) for pairs in work]
    nloads = max(len(loaded) for loaded, _ in plans)
    npairs = max(len(pairs) for pairs in work)
    table = []
    for device, (loaded, ordered) in enumerate(plans):
        table += [len(loaded), len(ordered)]
        table += [dict(permute).get(device, device) for permute in sends]
        table += [int(device in dict(permute).values()) for permute in permutes]
        table += [names.index(slot) for slot in loaded] + [0] * (nloads - len(loaded))
        for (slot, other, block, visitor), need in ordered:
            table += [loaded.index(slot), loaded.index(other), block, visitor, need]
        table += [0] * (5 * (npairs - len(ordered)))
    given = [slots[name] for name in names]
    rows, depth = given[0].shape
    whole = pl.BlockSpec(memory_space=pltpu.VMEM)
    return pl.pallas_call(
        functools.partial(pairs_kernel, len(given), len(sends), len(found), nloads, npairs),
        out_shape=[jax.ShapeDtypeStruct(best.shape, jnp.float32)]
        + [jax.ShapeDtypeStruct((1, rows), jnp.float32)] * len(sends),
        in_specs=[pl.BlockSpec(memory_space=pltpu.SMEM)]
        + [whole] * (1 + len(found))
        + [pl.BlockSpec(memory_space=pl.ANY)] * len(given),
        out_specs=[whole] * (1 + len(sends)),
        scratch_shapes=[
            pltpu.VMEM((nloads, rows, depth), jnp.bfloat16),
            pltpu.VMEM((rows, 128), jnp.float32),
            pltpu.SemaphoreType.DMA((nloads,)),
        ],
        compiler_params=pltpu.CompilerParams(vmem_limit_bytes=VMEM),
        cost_estimate=pl.CostEstimate(
            flops=2 * npairs * rows * rows * depth,
            bytes_accessed=2 * nloads * rows * depth,
            transcendentals=0,
        ),
        name="scored",
    )(jnp.asarray(np.array(table, np.int32)), best, *found, *given)


def placed_kernel(taken, pads, order, best, *refs):
    found, out = refs[:-1], refs[-1]
    rows = order.shape[1]
    here = lax.axis_index("blk")
    total = best[pl.ds(here, 1), :]
    for index, row in enumerate(found):
        total = jnp.where(taken[here * len(found) + index] > 0, jnp.maximum(total, row[...]), total)
    column = jnp.broadcast_to(total, (128, rows)).T[:, :1]
    row = lax.broadcasted_iota(jnp.int32, (rows, 1), 0)
    in_order = jnp.max(jnp.where(order[...] == row, column, FLOOR), axis=0, keepdims=True)
    position = lax.broadcasted_iota(jnp.int32, (1, rows), 1)
    out[...] = jnp.where(position < rows - pads[here], in_order, 0.0)


def placed(best, found, permutes, order, pad_counts):
    rows = order.shape[0]
    taken = np.zeros((best.shape[0], len(permutes)), np.int32)
    for index, permute in enumerate(permutes):
        taken[[to for _, to in permute], index] = 1
    whole, scalars = pl.BlockSpec(memory_space=pltpu.VMEM), pl.BlockSpec(memory_space=pltpu.SMEM)
    return pl.pallas_call(
        placed_kernel,
        out_shape=jax.ShapeDtypeStruct((1, rows), jnp.float32),
        in_specs=[scalars, scalars] + [whole] * (2 + len(found)),
        out_specs=whole,
        compiler_params=pltpu.CompilerParams(vmem_limit_bytes=VMEM),
        name="placed",
    )(jnp.asarray(taken.reshape(-1)), pad_counts, order.reshape(1, rows), best, *found).reshape(rows)


def local(embeddings, order, pad_counts):
    nblocks = lax.axis_size("blk")
    moves, work, sending = planned(nblocks)
    unit = normalized(embeddings, order, pad_counts)
    slots, best = {"own": unit}, None
    rank = dict({"own": -1}, **{move.name: move.stage for move in moves})
    edges = {}
    for stage, pairs in enumerate(work):
        due = edges.setdefault(min(last for last in sending if last >= stage), set())
        due |= {(of, to) for of in range(nblocks) for pair in pairs[of] for to in pair[2:] if to != of}
    if len(sending) == 2:
        edges = dict(zip(sending, in_two(*[edges[stage] for stage in sending], nblocks)))
    permutes, found = [], []
    for stage, pairs in enumerate(work):
        starting = [move for move in moves if move.begins == stage]
        for needs in sorted({move.needs for move in starting}):
            values = [slots[name] for name in needs]
            if best is not None:
                *values, best = lax.optimization_barrier((*values, best))
            for move in starting:
                if move.needs == needs:
                    value = values[needs.index(move.source)]
                    slots[move.name] = lax.ppermute(value, "blk", move.pairs)
        if stage == 0:
            best = own_block(unit, order, pad_counts, nblocks)
        sends = colored(sorted(edges[stage]), nblocks) if stage in sending else []
        if any(pairs):
            best, *rows = scored(best, found, permutes, slots, rank, pairs, sends)
            found = [lax.ppermute(row, "blk", permute) for row, permute in zip(rows, sends)]
            permutes = sends
    return placed(best, found, permutes, order, pad_counts)


def solution(mesh):
    in_specs = (P(("groups", "blk"), None), P(("groups", "blk")), P("groups"))
    out_specs = P(("groups", "blk"))
    return jax.shard_map(local, mesh=mesh, in_specs=in_specs, out_specs=out_specs, check_vma=False)
```

```python
import functools

import jax
import jax.numpy as jnp
import numpy as np
from jax import lax
from jax.experimental import pallas as pl
from jax.experimental.pallas import tpu as pltpu
from jax.sharding import PartitionSpec as P

STEPS = 6
VMEM = 64 * 2**20 - 2**16
FLOOR = -2.0
MOST_PADS = 256
AHEAD = 2
FIRST, EARLY = 4, 2


class Move:
    def __init__(self, name, source, pairs, begins, stage, *after):
        self.name, self.source, self.pairs = name, source, pairs
        self.begins, self.stage, self.needs = begins, stage, (source, *after)


def grid_moves():
    def at(z, y, lane):
        return 4 * z + 2 * y + (y if lane == 0 else 1 - y)

    def rows(links):
        return [
            (at(z, y, lane), at(to, y, land)) for y in (0, 1) for (z, lane), (to, land) in links
        ]

    def across(planes):
        return [(at(z, y, lane), at(z, 1 - y, lane)) for z, lane in planes for y in (0, 1)]

    every = [(z, lane) for z in range(4) for lane in (0, 1)]
    swap = rows([((z, lane), (z, 1 - lane)) for z, lane in every])
    crossed = [(at(1, y, lane), at(1, 1 - y, 1 - lane)) for y in (0, 1) for lane in (0, 1)]
    first = [((0, 0), (2, 1)), ((2, 0), (3, 1)), ((3, 0), (1, 0)), ((1, 0), (0, 0)), ((0, 1), (1, 1))]
    second = [((3, 1), (1, 1)), ((1, 1), (0, 1)), ((2, 1), (3, 0)), ((1, 0), (2, 1))]
    return [
        Move("R1", "own", rows(first), 0, 1),
        Move("R2", "own", rows(second), 0, 1),
        Move("Y", "own", across([place for place in every if place[0] != 1]) + crossed, 0, 1),
        Move("A", "own", swap, 0, 0),
        Move("R3", "own", rows([((1, 1), (2, 0)), ((2, 0), (1, 1))]), 1, 2, "R1"),
        Move("V", "R1", [(at(2, y, 1), at(3, y, 1 - y)) for y in (0, 1)] + across([(1, 1)]), 1, 2),
        Move("F", "Y", swap, 2, 2),
        Move("W", "R1", rows([((1, 0), (1, 1)), ((1, 1), (1, 0))]), 2, 2),
    ]


GRID_PAIRS = (
    ((0, 2), (0, 4), (1, 4), (2, 4), (3, 4)),
    ((0, 1), (0, 5), (1, 3), (1, 5), (3, 5)),
    ((0, 3), (0, 6), (1, 6), (2, 3), (2, 6), (3, 6)),
    ((1, 2), (1, 7), (2, 7), (3, 7)),
    ((1, 12), (4, 5), (4, 6), (4, 7), (6, 12), (7, 12)),
    ((1, 13), (2, 8), (2, 12), (2, 13), (5, 8), (7, 13)),
    ((1, 11), (1, 14), (1, 15), (2, 14), (4, 14)),
    ((2, 5), (2, 15), (4, 15), (5, 6), (5, 7), (5, 15), (6, 7)),
    ((5, 9), (5, 10), (5, 11), (9, 10), (9, 11)),
    ((0, 10), (0, 11), (4, 8), (4, 9), (4, 10), (8, 9), (8, 11)),
    ((3, 8), (3, 9), (7, 8), (7, 9), (7, 10), (7, 11)),
    ((6, 8), (6, 9), (6, 10), (6, 11), (8, 10), (10, 11)),
    ((9, 12), (9, 13), (9, 14), (9, 15), (12, 13), (12, 14), (13, 14), (13, 15)),
    ((0, 12), (0, 13), (0, 14), (0, 15), (8, 12), (8, 13), (8, 14)),
    ((11, 12), (11, 13), (11, 14), (11, 15), (12, 15)),
    ((3, 13), (3, 14), (3, 15), (10, 12), (10, 13), (10, 14), (10, 15), (14, 15)),
)


def ring_moves(count):
    return [
        Move("N%d" % k, "own", [((i + k) % count, i) for i in range(count)], 0, k)
        for k in range(1, STEPS + 1)
    ]


def planned(count):
    if count == 16:
        moves, placed_pairs, sending = grid_moves(), GRID_PAIRS, (1, 2)
    else:
        moves, sending = ring_moves(count), (STEPS,)
        placed_pairs = [[(b, (b + k) % count) for k in range(1, STEPS + 1)] for b in range(count)]
    holds = {"own": {d: d for d in range(count)}}
    stage_of = {"own": 0}
    for move in moves:
        holds[move.name] = {to: holds[move.source][of] for of, to in move.pairs}
        stage_of[move.name] = move.stage
    stages = 1 + max(stage_of.values())
    work = [[[] for _ in range(count)] for _ in range(stages)]
    for device, pairs in enumerate(placed_pairs):
        slot_of = {}
        for slot in sorted(stage_of, key=stage_of.get):
            if device in holds[slot]:
                slot_of.setdefault(holds[slot][device], slot)
        for block, visitor in pairs:
            slot, other = slot_of[block], slot_of[visitor]
            stage = max(stage_of[slot], stage_of[other])
            work[stage][device].append((slot, other, block, visitor))
    scored_pairs = sorted(tuple(sorted(pair)) for pairs in placed_pairs for pair in pairs)
    needed = {tuple(sorted((b, (b + k) % count))) for b in range(count) for k in range(1, STEPS + 1)}
    assert scored_pairs == sorted(needed)
    return moves, work, sending


def colored(edges, count):
    ends = [of for of, _ in edges], [to for _, to in edges]
    most = max((side.count(device) for side in ends for device in range(count)), default=0)
    sends, takes = [{} for _ in range(count)], [{} for _ in range(count)]
    for of, to in sorted(edges, key=lambda edge: (min(edge) >= FIRST, -abs(edge[0] - edge[1]), edge)):
        both = next(c for c in range(2 * len(edges)) if c not in sends[of] and c not in takes[to])
        a = next(c for c in range(len(edges)) if c not in sends[of])
        b = next(c for c in range(len(edges)) if c not in takes[to])
        if both < most:
            a = b = both
        path, node, tables, colour = [], to, (takes, sends), a
        while a != b and colour in tables[0][node]:
            end = tables[0][node][colour]
            path.append(((end, node) if tables[0] is takes else (node, end), colour))
            node, tables, colour = end, tables[::-1], a + b - colour
        for (first, second), colour in path:
            del sends[first][colour], takes[second][colour]
        for (first, second), colour in path:
            sends[first][a + b - colour], takes[second][a + b - colour] = second, first
        sends[of][a], takes[to][a] = to, of
    return [
        [(of, to[c]) for of, to in enumerate(sends) if c in to]
        for c in range(max((c + 1 for to in sends for c in to), default=0))
    ]


def in_two(early, late, count):
    early, late = set(early) - set(late), set(late)

    def degrees(edges):
        return [
            [sum(edge[side] == device for edge in edges) for device in range(count)] for side in (0, 1)
        ]

    most = max(degrees(late)[0] + degrees(late)[1])
    while early:
        busy, taken = degrees(early), degrees(late)
        top = max(busy[0] + busy[1])
        free = [
            (min(of, to) >= FIRST, max(busy[0][of], busy[1][to]), busy[0][of] + busy[1][to], of, to)
            for of, to in sorted(early)
            if max(taken[0][of], taken[1][to]) < most and max(busy[0][of], busy[1][to]) == top
        ]
        if not free or top <= EARLY:
            break
        early.remove(max(free)[3:])
        late.add(max(free)[3:])
    return sorted(early), sorted(late)


def unit_kernel(pads, order_smem, order, embeddings, unit, value, result, tile, into, out, sem):
    rows = unit.shape[0]
    count = rows // into.shape[0]
    parts = [pl.ds(start, count) for start in range(0, rows, count)]
    loads = [
        pltpu.make_async_copy(embeddings.at[part], value.at[part], into.at[index])
        for index, part in enumerate(parts)
    ]
    stores = [
        pltpu.make_async_copy(result.at[part], unit.at[part], out.at[index])
        for index, part in enumerate(parts)
    ]
    first = order_smem[0]
    base = pl.multiple_of((first // 16) * 16, 16)
    filling = pltpu.make_async_copy(embeddings.at[pl.ds(base, 16)], tile, sem)
    filling.start()
    for load in loads:
        load.start()
    filling.wait()
    among = lax.broadcasted_iota(jnp.int32, (16, 1), 0) == first - base
    filler = jnp.sum(jnp.where(among, tile[...].astype(jnp.float32), 0.0), axis=0, keepdims=True)
    for index, part in enumerate(parts):
        found = valid_rows(pads, order, index * count, count)
        loads[index].wait()
        chunk = jnp.where(found, value[part, :].astype(jnp.float32), filler)
        scale = lax.rsqrt(jnp.sum(chunk * chunk, axis=1, keepdims=True) + 1e-06)
        result[part, :] = (chunk * scale).astype(jnp.bfloat16)
        stores[index].start()
    for store in stores:
        store.wait()


def valid_rows(pads, order, start, count):
    rows = order.shape[1]
    most = min(rows, MOST_PADS)
    valid_count = rows - pads[lax.axis_index("blk")]
    position = rows - most + lax.broadcasted_iota(jnp.int32, (1, most), 1)
    padding = jnp.where(position < valid_count, -1, order[:, rows - most :])
    row = start + lax.broadcasted_iota(jnp.int32, (count, 1), 0)
    return jnp.max(jnp.where(padding == row, 1.0, 0.0), axis=1, keepdims=True) < 1.0


def normalized(embeddings, order, pad_counts):
    rows, depth = embeddings.shape
    chunks = 4
    scalars = pl.BlockSpec(memory_space=pltpu.SMEM)
    return pl.pallas_call(
        unit_kernel,
        out_shape=jax.ShapeDtypeStruct((rows, depth), jnp.bfloat16),
        in_specs=[
            scalars,
            scalars,
            pl.BlockSpec(memory_space=pltpu.VMEM),
            pl.BlockSpec(memory_space=pl.ANY),
        ],
        out_specs=pl.BlockSpec(memory_space=pl.ANY),
        scratch_shapes=[
            pltpu.VMEM((rows, depth), jnp.bfloat16),
            pltpu.VMEM((rows, depth), jnp.bfloat16),
            pltpu.VMEM((16, depth), jnp.bfloat16),
            pltpu.SemaphoreType.DMA((chunks,)),
            pltpu.SemaphoreType.DMA((chunks,)),
            pltpu.SemaphoreType.DMA,
        ],
        compiler_params=pltpu.CompilerParams(vmem_limit_bytes=VMEM),
        cost_estimate=pl.CostEstimate(
            flops=4 * rows * depth, bytes_accessed=4 * rows * depth, transcendentals=rows
        ),
        name="normalized",
    )(pad_counts, order, order.reshape(1, rows), embeddings)


def product(left, right):
    return lax.dot_general(left, right, (((1,), (1,)), ((), ())), preferred_element_type=jnp.float32)


def own_kernel(pads, order, unit, best):
    rows = unit.shape[0]
    best[...] = jnp.full(best.shape, FLOOR, jnp.float32)
    valid = valid_rows(pads, order, 0, rows)
    row = lax.broadcasted_iota(jnp.int32, (rows, 1), 0)
    here = pl.ds(lax.axis_index("blk"), 1)
    for start in range(0, rows, 256):
        part = pl.ds(start, 256)
        scores = product(unit[...], unit[part, :])
        column = start + lax.broadcasted_iota(jnp.int32, (1, 256), 1)
        scores = jnp.where(valid & (row != column), scores, FLOOR)
        best[here, part] = jnp.max(scores, axis=0, keepdims=True)


def own_block(unit, order, pad_counts, nblocks):
    rows, depth = unit.shape
    whole = pl.BlockSpec(memory_space=pltpu.VMEM)
    return pl.pallas_call(
        own_kernel,
        out_shape=jax.ShapeDtypeStruct((nblocks, rows), jnp.float32),
        in_specs=[pl.BlockSpec(memory_space=pltpu.SMEM), whole, whole],
        out_specs=whole,
        compiler_params=pltpu.CompilerParams(vmem_limit_bytes=VMEM),
        cost_estimate=pl.CostEstimate(
            flops=2 * rows * rows * depth, bytes_accessed=2 * rows * depth, transcendentals=0
        ),
        name="own_block",
    )(pad_counts, order.reshape(1, rows), unit)


def pairs_kernel(nslots, nrows, ntaken, nloads, npairs, final, table, best, *refs):
    arrivals, slots, out = refs[:ntaken], refs[ntaken : ntaken + nslots], refs[ntaken + nslots]
    sent, (held, across, total, sems) = refs[ntaken + nslots + 1 : -4], refs[-4:]
    result, out = out, total if final else out
    rows = out.shape[1]
    here = lax.axis_index("blk")
    loads_at = here * (2 + nrows + ntaken + nloads + 5 * npairs) + 2 + nrows + ntaken
    pairs_at = loads_at + nloads
    rows_at = loads_at - nrows - ntaken
    loads, pairs = table[rows_at - 2], table[rows_at - 1]

    def fetch(load):
        @pl.when(load < loads)
        def _():
            wanted = table[loads_at + jnp.minimum(load, nloads - 1)]
            for index, slot in enumerate(slots):
                @pl.when(wanted == index)
                def _(slot=slot):
                    for start in range(0, rows, 256):
                        part = pl.ds(start, 256)
                        pltpu.make_async_copy(slot.at[part], held.at[load, part], sems.at[load]).start()

    for load in range(min(AHEAD, nloads)):
        fetch(load)
    out[...] = best[...]
    own = pl.ds(here, 1)
    for index, row in enumerate(arrivals):
        handed = table[rows_at + nrows + index] > 0
        out[own, :] = jnp.where(handed, jnp.maximum(out[own, :], row[...]), out[own, :])

    @pl.loop(0, pairs)
    def _(step):
        at = pairs_at + 5 * step
        before = jnp.where(step == 0, 0, table[jnp.maximum(at - 1, 0)])

        @pl.loop(before, table[at + 4])
        def _(load):
            pltpu.make_async_copy(slots[0], held.at[load], sems.at[load]).wait()
            fetch(load + AHEAD)

        left, right = table[at], table[at + 1]
        first, second = pl.ds(table[at + 2], 1), pl.ds(table[at + 3], 1)
        for start in range(0, rows, 256):
            part = pl.ds(start, 256)
            scores = product(held[left], held[right, part, :])
            down = jnp.max(scores, axis=0, keepdims=True)
            out[second, part] = jnp.maximum(out[second, part], down)
            along = jnp.maximum(scores[:, :128], scores[:, 128:])
            across[...] = along if start == 0 else jnp.maximum(across[...], along)
        found = jnp.max(across[...].T, axis=0, keepdims=True)
        out[first, :] = jnp.maximum(out[first, :], found)

    for index, row in enumerate(sent):
        row[...] = out[pl.ds(table[rows_at + index], 1), :]
    if final:
        result[...] = out[own, :]


def in_order_of_loads(pairs, rank):
    left, loaded, ordered = list(pairs), [], []
    while left:
        pair = min(
            left,
            key=lambda p: (sum(s not in loaded for s in p[:2]), max(rank[s] for s in p[:2]), p[2:]),
        )
        left.remove(pair)
        loaded += [slot for slot in pair[:2] if slot not in loaded]
        ordered.append((pair, len(loaded)))
    return loaded, ordered


def scored(best, found, permutes, slots, rank, work, sends, final):
    names = sorted({slot for pairs in work for pair in pairs for slot in pair[:2]})
    plans = [in_order_of_loads(pairs, rank) for pairs in work]
    nloads = max(len(loaded) for loaded, _ in plans)
    npairs = max(len(pairs) for pairs in work)
    table = []
    for device, (loaded, ordered) in enumerate(plans):
        table += [len(loaded), len(ordered)]
        table += [dict(permute).get(device, device) for permute in sends]
        table += [int(device in dict(permute).values()) for permute in permutes]
        table += [names.index(slot) for slot in loaded] + [0] * (nloads - len(loaded))
        for (slot, other, block, visitor), need in ordered:
            table += [loaded.index(slot), loaded.index(other), block, visitor, need]
        table += [0] * (5 * (npairs - len(ordered)))
    given = [slots[name] for name in names]
    rows, depth = given[0].shape
    whole = pl.BlockSpec(memory_space=pltpu.VMEM)
    return pl.pallas_call(
        functools.partial(pairs_kernel, len(given), len(sends), len(found), nloads, npairs, final),
        out_shape=[jax.ShapeDtypeStruct((1, rows) if final else best.shape, jnp.float32)]
        + [jax.ShapeDtypeStruct((1, rows), jnp.float32)] * len(sends),
        in_specs=[pl.BlockSpec(memory_space=pltpu.SMEM)]
        + [whole] * (1 + len(found))
        + [pl.BlockSpec(memory_space=pl.ANY)] * len(given),
        out_specs=[whole] * (1 + len(sends)),
        scratch_shapes=[
            pltpu.VMEM((nloads, rows, depth), jnp.bfloat16),
            pltpu.VMEM((rows, 128), jnp.float32),
            pltpu.VMEM(best.shape if final else (8, 128), jnp.float32),
            pltpu.SemaphoreType.DMA((nloads,)),
        ],
        compiler_params=pltpu.CompilerParams(vmem_limit_bytes=VMEM),
        cost_estimate=pl.CostEstimate(
            flops=2 * npairs * rows * rows * depth,
            bytes_accessed=2 * nloads * rows * depth,
            transcendentals=0,
        ),
        name="scored",
    )(jnp.asarray(np.array(table, np.int32)), best, *found, *given)


def placed_kernel(taken, pads, order, best, *refs):
    found, out = refs[:-1], refs[-1]
    rows = order.shape[1]
    here = lax.axis_index("blk")
    total = best[...]
    for index, row in enumerate(found):
        total = jnp.where(taken[here * len(found) + index] > 0, jnp.maximum(total, row[...]), total)
    column = jnp.broadcast_to(total, (128, rows)).T[:, :1]
    row = lax.broadcasted_iota(jnp.int32, (rows, 1), 0)
    in_order = jnp.max(jnp.where(order[...] == row, column, FLOOR), axis=0, keepdims=True)
    position = lax.broadcasted_iota(jnp.int32, (1, rows), 1)
    out[...] = jnp.where(position < rows - pads[here], in_order, 0.0)


def placed(best, found, permutes, order, pad_counts, nblocks):
    rows = order.shape[0]
    taken = np.zeros((nblocks, len(permutes)), np.int32)
    for index, permute in enumerate(permutes):
        taken[[to for _, to in permute], index] = 1
    whole, scalars = pl.BlockSpec(memory_space=pltpu.VMEM), pl.BlockSpec(memory_space=pltpu.SMEM)
    return pl.pallas_call(
        placed_kernel,
        out_shape=jax.ShapeDtypeStruct((1, rows), jnp.float32),
        in_specs=[scalars, scalars] + [whole] * (2 + len(found)),
        out_specs=whole,
        compiler_params=pltpu.CompilerParams(vmem_limit_bytes=VMEM),
        name="placed",
    )(jnp.asarray(taken.reshape(-1)), pad_counts, order.reshape(1, rows), best, *found).reshape(rows)


def local(embeddings, order, pad_counts):
    nblocks = lax.axis_size("blk")
    moves, work, sending = planned(nblocks)
    unit = normalized(embeddings, order, pad_counts)
    slots, best = {"own": unit}, None
    rank = dict({"own": -1}, **{move.name: move.stage for move in moves})
    edges = {}
    for stage, pairs in enumerate(work):
        due = edges.setdefault(min(last for last in sending if last >= stage), set())
        due |= {(of, to) for of in range(nblocks) for pair in pairs[of] for to in pair[2:] if to != of}
    if len(sending) == 2:
        edges = dict(zip(sending, in_two(*[edges[stage] for stage in sending], nblocks)))
    permutes, found = [], []
    for stage, pairs in enumerate(work):
        starting = [move for move in moves if move.begins == stage]
        for needs in sorted({move.needs for move in starting}):
            values = [slots[name] for name in needs]
            if best is not None:
                *values, best = lax.optimization_barrier((*values, best))
            for move in starting:
                if move.needs == needs:
                    value = values[needs.index(move.source)]
                    slots[move.name] = lax.ppermute(value, "blk", move.pairs)
        if stage == 0:
            best = own_block(unit, order, pad_counts, nblocks)
        sends = colored(sorted(edges[stage]), nblocks) if stage in sending else []
        if any(pairs):
            best, *rows = scored(best, found, permutes, slots, rank, pairs, sends, stage == len(work) - 1)
            found = [lax.ppermute(row, "blk", permute) for row, permute in zip(rows, sends)]
            permutes = sends
    return placed(best, found, permutes, order, pad_counts, nblocks)


def solution(mesh):
    in_specs = (P(("groups", "blk"), None), P(("groups", "blk")), P("groups"))
    out_specs = P(("groups", "blk"))
    return jax.shard_map(local, mesh=mesh, in_specs=in_specs, out_specs=out_specs, check_vma=False)
```

```python
import functools

import jax
import jax.numpy as jnp
import numpy as np
from jax import lax
from jax.experimental import pallas as pl
from jax.experimental.pallas import tpu as pltpu
from jax.sharding import PartitionSpec as P

STEPS = 6
VMEM = 64 * 2**20 - 2**16
FLOOR = -2.0
MOST_PADS = 256
AHEAD = 2
FIRST, EARLY = 4, 2


class Move:
    def __init__(self, name, source, pairs, begins, stage, *after):
        self.name, self.source, self.pairs = name, source, pairs
        self.begins, self.stage, self.needs = begins, stage, (source, *after)


def grid_moves():
    def at(z, y, lane):
        return 4 * z + 2 * y + (y if lane == 0 else 1 - y)

    def rows(links):
        return [
            (at(z, y, lane), at(to, y, land)) for y in (0, 1) for (z, lane), (to, land) in links
        ]

    def across(planes):
        return [(at(z, y, lane), at(z, 1 - y, lane)) for z, lane in planes for y in (0, 1)]

    every = [(z, lane) for z in range(4) for lane in (0, 1)]
    swap = rows([((z, lane), (z, 1 - lane)) for z, lane in every])
    crossed = [(at(1, y, lane), at(1, 1 - y, 1 - lane)) for y in (0, 1) for lane in (0, 1)]
    first = [((0, 0), (2, 1)), ((2, 0), (3, 1)), ((3, 0), (1, 0)), ((1, 0), (0, 0)), ((0, 1), (1, 1))]
    second = [((3, 1), (1, 1)), ((1, 1), (0, 1)), ((2, 1), (3, 0)), ((1, 0), (2, 1))]
    return [
        Move("R1", "own", rows(first), 0, 1),
        Move("R2", "own", rows(second), 0, 1),
        Move("Y", "own", across([place for place in every if place[0] != 1]) + crossed, 0, 1),
        Move("A", "own", swap, 0, 0),
        Move("R3", "own", rows([((1, 1), (2, 0)), ((2, 0), (1, 1))]), 1, 2, "R1"),
        Move("V", "R1", [(at(2, y, 1), at(3, y, 1 - y)) for y in (0, 1)] + across([(1, 1)]), 1, 2),
        Move("F", "Y", swap, 2, 2),
        Move("W", "R1", rows([((1, 0), (1, 1)), ((1, 1), (1, 0))]), 2, 2),
    ]


GRID_PAIRS = (
    ((0, 2), (0, 4), (1, 4), (2, 4), (3, 4)),
    ((0, 1), (0, 5), (1, 3), (1, 5), (3, 5)),
    ((0, 3), (0, 6), (1, 6), (2, 3), (2, 6), (3, 6)),
    ((1, 2), (1, 7), (2, 7), (3, 7)),
    ((1, 12), (4, 5), (4, 6), (4, 7), (6, 12), (7, 12)),
    ((1, 13), (2, 8), (2, 12), (2, 13), (5, 8), (7, 13)),
    ((1, 11), (1, 14), (1, 15), (2, 14), (4, 14)),
    ((2, 5), (2, 15), (4, 15), (5, 6), (5, 7), (5, 15), (6, 7)),
    ((5, 9), (5, 10), (5, 11), (9, 10), (9, 11)),
    ((0, 10), (0, 11), (4, 8), (4, 9), (4, 10), (8, 9), (8, 11)),
    ((3, 8), (3, 9), (7, 8), (7, 9), (7, 10), (7, 11)),
    ((6, 8), (6, 9), (6, 10), (6, 11), (8, 10), (10, 11)),
    ((9, 12), (9, 13), (9, 14), (9, 15), (12, 13), (12, 14), (13, 14), (13, 15)),
    ((0, 12), (0, 13), (0, 14), (0, 15), (8, 12), (8, 13), (8, 14)),
    ((11, 12), (11, 13), (11, 14), (11, 15), (12, 15)),
    ((3, 13), (3, 14), (3, 15), (10, 12), (10, 13), (10, 14), (10, 15), (14, 15)),
)


def ring_moves(count):
    return [
        Move("N%d" % k, "own", [((i + k) % count, i) for i in range(count)], 0, k)
        for k in range(1, STEPS + 1)
    ]


def planned(count):
    if count == 16:
        moves, placed_pairs, sending = grid_moves(), GRID_PAIRS, (1, 2)
    else:
        moves, sending = ring_moves(count), (STEPS,)
        placed_pairs = [[(b, (b + k) % count) for k in range(1, STEPS + 1)] for b in range(count)]
    holds = {"own": {d: d for d in range(count)}}
    stage_of = {"own": 0}
    for move in moves:
        holds[move.name] = {to: holds[move.source][of] for of, to in move.pairs}
        stage_of[move.name] = move.stage
    stages = 1 + max(stage_of.values())
    work = [[[] for _ in range(count)] for _ in range(stages)]
    for device, pairs in enumerate(placed_pairs):
        slot_of = {}
        for slot in sorted(stage_of, key=stage_of.get):
            if device in holds[slot]:
                slot_of.setdefault(holds[slot][device], slot)
        for block, visitor in pairs:
            slot, other = slot_of[block], slot_of[visitor]
            stage = max(stage_of[slot], stage_of[other])
            work[stage][device].append((slot, other, block, visitor))
    scored_pairs = sorted(tuple(sorted(pair)) for pairs in placed_pairs for pair in pairs)
    needed = {tuple(sorted((b, (b + k) % count))) for b in range(count) for k in range(1, STEPS + 1)}
    assert scored_pairs == sorted(needed)
    return moves, work, sending


def colored(edges, count):
    ends = [of for of, _ in edges], [to for _, to in edges]
    most = max((side.count(device) for side in ends for device in range(count)), default=0)
    sends, takes = [{} for _ in range(count)], [{} for _ in range(count)]
    for of, to in sorted(edges, key=lambda edge: (min(edge) >= FIRST, -abs(edge[0] - edge[1]), edge)):
        both = next(c for c in range(2 * len(edges)) if c not in sends[of] and c not in takes[to])
        a = next(c for c in range(len(edges)) if c not in sends[of])
        b = next(c for c in range(len(edges)) if c not in takes[to])
        if both < most:
            a = b = both
        path, node, tables, colour = [], to, (takes, sends), a
        while a != b and colour in tables[0][node]:
            end = tables[0][node][colour]
            path.append(((end, node) if tables[0] is takes else (node, end), colour))
            node, tables, colour = end, tables[::-1], a + b - colour
        for (first, second), colour in path:
            del sends[first][colour], takes[second][colour]
        for (first, second), colour in path:
            sends[first][a + b - colour], takes[second][a + b - colour] = second, first
        sends[of][a], takes[to][a] = to, of
    return [
        [(of, to[c]) for of, to in enumerate(sends) if c in to]
        for c in range(max((c + 1 for to in sends for c in to), default=0))
    ]


def in_two(early, late, count):
    early, late = set(early) - set(late), set(late)

    def degrees(edges):
        return [
            [sum(edge[side] == device for edge in edges) for device in range(count)] for side in (0, 1)
        ]

    most = max(degrees(late)[0] + degrees(late)[1])
    while early:
        busy, taken = degrees(early), degrees(late)
        top = max(busy[0] + busy[1])
        free = [
            (min(of, to) >= FIRST, max(busy[0][of], busy[1][to]), busy[0][of] + busy[1][to], of, to)
            for of, to in sorted(early)
            if max(taken[0][of], taken[1][to]) < most and max(busy[0][of], busy[1][to]) == top
        ]
        if not free or top <= EARLY:
            break
        early.remove(max(free)[3:])
        late.add(max(free)[3:])
    return sorted(early), sorted(late)


def unit_kernel(pads, order_smem, order, embeddings, unit, value, result, tile, into, out, sem):
    rows = unit.shape[0]
    count = rows // into.shape[0]
    parts = [pl.ds(start, count) for start in range(0, rows, count)]
    loads = [
        pltpu.make_async_copy(embeddings.at[part], value.at[part], into.at[index])
        for index, part in enumerate(parts)
    ]
    stores = [
        pltpu.make_async_copy(result.at[part], unit.at[part], out.at[index])
        for index, part in enumerate(parts)
    ]
    first = order_smem[0]
    base = pl.multiple_of((first // 16) * 16, 16)
    filling = pltpu.make_async_copy(embeddings.at[pl.ds(base, 16)], tile, sem)
    filling.start()
    for load in loads:
        load.start()
    filling.wait()
    among = lax.broadcasted_iota(jnp.int32, (16, 1), 0) == first - base
    filler = jnp.sum(jnp.where(among, tile[...].astype(jnp.float32), 0.0), axis=0, keepdims=True)
    for index, part in enumerate(parts):
        found = valid_rows(pads, order, index * count, count)
        loads[index].wait()
        chunk = jnp.where(found, value[part, :].astype(jnp.float32), filler)
        scale = lax.rsqrt(jnp.sum(chunk * chunk, axis=1, keepdims=True) + 1e-06)
        result[part, :] = (chunk * scale).astype(jnp.bfloat16)
        stores[index].start()
    for store in stores:
        store.wait()


def valid_rows(pads, order, start, count):
    rows = order.shape[1]
    most = min(rows, MOST_PADS)
    valid_count = rows - pads[lax.axis_index("blk")]
    position = rows - most + lax.broadcasted_iota(jnp.int32, (1, most), 1)
    padding = jnp.where(position < valid_count, -1, order[:, rows - most :])
    row = start + lax.broadcasted_iota(jnp.int32, (count, 1), 0)
    return jnp.max(jnp.where(padding == row, 1.0, 0.0), axis=1, keepdims=True) < 1.0


def normalized(embeddings, order, pad_counts):
    rows, depth = embeddings.shape
    chunks = 2
    scalars = pl.BlockSpec(memory_space=pltpu.SMEM)
    return pl.pallas_call(
        unit_kernel,
        out_shape=jax.ShapeDtypeStruct((rows, depth), jnp.bfloat16),
        in_specs=[
            scalars,
            scalars,
            pl.BlockSpec(memory_space=pltpu.VMEM),
            pl.BlockSpec(memory_space=pl.ANY),
        ],
        out_specs=pl.BlockSpec(memory_space=pl.ANY),
        scratch_shapes=[
            pltpu.VMEM((rows, depth), jnp.bfloat16),
            pltpu.VMEM((rows, depth), jnp.bfloat16),
            pltpu.VMEM((16, depth), jnp.bfloat16),
            pltpu.SemaphoreType.DMA((chunks,)),
            pltpu.SemaphoreType.DMA((chunks,)),
            pltpu.SemaphoreType.DMA,
        ],
        compiler_params=pltpu.CompilerParams(vmem_limit_bytes=VMEM),
        cost_estimate=pl.CostEstimate(
            flops=4 * rows * depth, bytes_accessed=4 * rows * depth, transcendentals=rows
        ),
        name="normalized",
    )(pad_counts, order, order.reshape(1, rows), embeddings)


def product(left, right):
    return lax.dot_general(left, right, (((1,), (1,)), ((), ())), preferred_element_type=jnp.float32)


def own_kernel(pads, order, unit, best):
    rows = unit.shape[0]
    best[...] = jnp.full(best.shape, FLOOR, jnp.float32)
    valid = valid_rows(pads, order, 0, rows)
    row = lax.broadcasted_iota(jnp.int32, (rows, 1), 0)
    here = pl.ds(lax.axis_index("blk"), 1)
    for start in range(0, rows, 256):
        part = pl.ds(start, 256)
        scores = product(unit[...], unit[part, :])
        column = start + lax.broadcasted_iota(jnp.int32, (1, 256), 1)
        scores = jnp.where(valid & (row != column), scores, FLOOR)
        best[here, part] = jnp.max(scores, axis=0, keepdims=True)


def own_block(unit, order, pad_counts, nblocks):
    rows, depth = unit.shape
    whole = pl.BlockSpec(memory_space=pltpu.VMEM)
    return pl.pallas_call(
        own_kernel,
        out_shape=jax.ShapeDtypeStruct((nblocks, rows), jnp.float32),
        in_specs=[pl.BlockSpec(memory_space=pltpu.SMEM), whole, whole],
        out_specs=whole,
        compiler_params=pltpu.CompilerParams(vmem_limit_bytes=VMEM),
        cost_estimate=pl.CostEstimate(
            flops=2 * rows * rows * depth, bytes_accessed=2 * rows * depth, transcendentals=0
        ),
        name="own_block",
    )(pad_counts, order.reshape(1, rows), unit)


def pairs_kernel(nslots, nrows, ntaken, nloads, npairs, final, table, best, *refs):
    arrivals, slots, out = refs[:ntaken], refs[ntaken : ntaken + nslots], refs[ntaken + nslots]
    sent, (held, across, total, sems) = refs[ntaken + nslots + 1 : -4], refs[-4:]
    result, out = out, total if final else out
    rows = out.shape[1]
    here = lax.axis_index("blk")
    loads_at = here * (2 + nrows + ntaken + nloads + 5 * npairs) + 2 + nrows + ntaken
    pairs_at = loads_at + nloads
    rows_at = loads_at - nrows - ntaken
    loads, pairs = table[rows_at - 2], table[rows_at - 1]

    def fetch(load):
        @pl.when(load < loads)
        def _():
            wanted = table[loads_at + jnp.minimum(load, nloads - 1)]
            for index, slot in enumerate(slots):
                @pl.when(wanted == index)
                def _(slot=slot):
                    for start in range(0, rows, 256):
                        part = pl.ds(start, 256)
                        pltpu.make_async_copy(slot.at[part], held.at[load, part], sems.at[load]).start()

    for load in range(min(AHEAD, nloads)):
        fetch(load)
    out[...] = best[...]
    own = pl.ds(here, 1)
    for index, row in enumerate(arrivals):
        handed = table[rows_at + nrows + index] > 0
        out[own, :] = jnp.where(handed, jnp.maximum(out[own, :], row[...]), out[own, :])

    @pl.loop(0, pairs)
    def _(step):
        at = pairs_at + 5 * step
        before = jnp.where(step == 0, 0, table[jnp.maximum(at - 1, 0)])

        @pl.loop(before, table[at + 4])
        def _(load):
            pltpu.make_async_copy(slots[0], held.at[load], sems.at[load]).wait()
            fetch(load + AHEAD)

        left, right = table[at], table[at + 1]
        first, second = pl.ds(table[at + 2], 1), pl.ds(table[at + 3], 1)
        for start in range(0, rows, 256):
            part = pl.ds(start, 256)
            scores = product(held[left], held[right, part, :])
            down = jnp.max(scores, axis=0, keepdims=True)
            out[second, part] = jnp.maximum(out[second, part], down)
            along = jnp.maximum(scores[:, :128], scores[:, 128:])
            across[...] = along if start == 0 else jnp.maximum(across[...], along)
        found = jnp.max(across[...].T, axis=0, keepdims=True)
        out[first, :] = jnp.maximum(out[first, :], found)

    for index, row in enumerate(sent):
        row[...] = out[pl.ds(table[rows_at + index], 1), :]
    if final:
        result[...] = out[own, :]


def in_order_of_loads(pairs, rank):
    left, loaded, ordered = list(pairs), [], []
    while left:
        pair = min(
            left,
            key=lambda p: (sum(s not in loaded for s in p[:2]), max(rank[s] for s in p[:2]), p[2:]),
        )
        left.remove(pair)
        loaded += [slot for slot in pair[:2] if slot not in loaded]
        ordered.append((pair, len(loaded)))
    return loaded, ordered


def scored(best, found, permutes, slots, rank, work, sends, final):
    names = sorted({slot for pairs in work for pair in pairs for slot in pair[:2]})
    plans = [in_order_of_loads(pairs, rank) for pairs in work]
    nloads = max(len(loaded) for loaded, _ in plans)
    npairs = max(len(pairs) for pairs in work)
    table = []
    for device, (loaded, ordered) in enumerate(plans):
        table += [len(loaded), len(ordered)]
        table += [dict(permute).get(device, device) for permute in sends]
        table += [int(device in dict(permute).values()) for permute in permutes]
        table += [names.index(slot) for slot in loaded] + [0] * (nloads - len(loaded))
        for (slot, other, block, visitor), need in ordered:
            table += [loaded.index(slot), loaded.index(other), block, visitor, need]
        table += [0] * (5 * (npairs - len(ordered)))
    given = [slots[name] for name in names]
    rows, depth = given[0].shape
    whole = pl.BlockSpec(memory_space=pltpu.VMEM)
    return pl.pallas_call(
        functools.partial(pairs_kernel, len(given), len(sends), len(found), nloads, npairs, final),
        out_shape=[jax.ShapeDtypeStruct((1, rows) if final else best.shape, jnp.float32)]
        + [jax.ShapeDtypeStruct((1, rows), jnp.float32)] * len(sends),
        in_specs=[pl.BlockSpec(memory_space=pltpu.SMEM)]
        + [whole] * (1 + len(found))
        + [pl.BlockSpec(memory_space=pl.ANY)] * len(given),
        out_specs=[whole] * (1 + len(sends)),
        scratch_shapes=[
            pltpu.VMEM((nloads, rows, depth), jnp.bfloat16),
            pltpu.VMEM((rows, 128), jnp.float32),
            pltpu.VMEM(best.shape if final else (8, 128), jnp.float32),
            pltpu.SemaphoreType.DMA((nloads,)),
        ],
        compiler_params=pltpu.CompilerParams(vmem_limit_bytes=VMEM),
        cost_estimate=pl.CostEstimate(
            flops=2 * npairs * rows * rows * depth,
            bytes_accessed=2 * nloads * rows * depth,
            transcendentals=0,
        ),
        name="scored",
    )(jnp.asarray(np.array(table, np.int32)), best, *found, *given)


def placed_kernel(taken, pads, order, best, *refs):
    found, out = refs[:-1], refs[-1]
    rows = order.shape[1]
    here = lax.axis_index("blk")
    total = best[...]
    for index, row in enumerate(found):
        total = jnp.where(taken[here * len(found) + index] > 0, jnp.maximum(total, row[...]), total)
    column = jnp.broadcast_to(total, (128, rows)).T[:, :1]
    row = lax.broadcasted_iota(jnp.int32, (rows, 1), 0)
    in_order = jnp.max(jnp.where(order[...] == row, column, FLOOR), axis=0, keepdims=True)
    position = lax.broadcasted_iota(jnp.int32, (1, rows), 1)
    out[...] = jnp.where(position < rows - pads[here], in_order, 0.0)


def placed(best, found, permutes, order, pad_counts, nblocks):
    rows = order.shape[0]
    taken = np.zeros((nblocks, len(permutes)), np.int32)
    for index, permute in enumerate(permutes):
        taken[[to for _, to in permute], index] = 1
    whole, scalars = pl.BlockSpec(memory_space=pltpu.VMEM), pl.BlockSpec(memory_space=pltpu.SMEM)
    return pl.pallas_call(
        placed_kernel,
        out_shape=jax.ShapeDtypeStruct((1, rows), jnp.float32),
        in_specs=[scalars, scalars] + [whole] * (2 + len(found)),
        out_specs=whole,
        compiler_params=pltpu.CompilerParams(vmem_limit_bytes=VMEM),
        name="placed",
    )(jnp.asarray(taken.reshape(-1)), pad_counts, order.reshape(1, rows), best, *found).reshape(rows)


def local(embeddings, order, pad_counts):
    nblocks = lax.axis_size("blk")
    moves, work, sending = planned(nblocks)
    unit = normalized(embeddings, order, pad_counts)
    slots, best = {"own": unit}, None
    rank = dict({"own": -1}, **{move.name: move.stage for move in moves})
    edges = {}
    for stage, pairs in enumerate(work):
        due = edges.setdefault(min(last for last in sending if last >= stage), set())
        due |= {(of, to) for of in range(nblocks) for pair in pairs[of] for to in pair[2:] if to != of}
    if len(sending) == 2:
        edges = dict(zip(sending, in_two(*[edges[stage] for stage in sending], nblocks)))
    permutes, found = [], []
    for stage, pairs in enumerate(work):
        starting = [move for move in moves if move.begins == stage]
        for needs in sorted({move.needs for move in starting}):
            values = [slots[name] for name in needs]
            if best is not None:
                *values, best = lax.optimization_barrier((*values, best))
            for move in starting:
                if move.needs == needs:
                    value = values[needs.index(move.source)]
                    slots[move.name] = lax.ppermute(value, "blk", move.pairs)
        if stage == 0:
            best = own_block(unit, order, pad_counts, nblocks)
        sends = colored(sorted(edges[stage]), nblocks) if stage in sending else []
        if any(pairs):
            best, *rows = scored(best, found, permutes, slots, rank, pairs, sends, stage == len(work) - 1)
            found = [lax.ppermute(row, "blk", permute) for row, permute in zip(rows, sends)]
            permutes = sends
    return placed(best, found, permutes, order, pad_counts, nblocks)


def solution(mesh):
    in_specs = (P(("groups", "blk"), None), P(("groups", "blk")), P("groups"))
    out_specs = P(("groups", "blk"))
    return jax.shard_map(local, mesh=mesh, in_specs=in_specs, out_specs=out_specs, check_vma=False)
```
